32 devices in a mesh: wide: 8 (over z, x), narrow: 4 (over y, core).
Axes of the slice: x: 2, y: 2, z: 4, core: 2. Of those that a mesh axis runs over, the one named last changes fastest.
Arguments:
- tokens: bfloat16 [32768, 768], P(('wide', 'narrow')), may hold values from -6 to 6
- qkv_weight: float32 [768, 2304], P('narrow', 'wide'), may hold values from -0.21875 to 0.21875
- out_weight: float32 [768, 768], P('wide', 'narrow'), may hold values from -1.25 to 1.25
- up_weight: float32 [768, 3072], P('narrow', 'wide'), may hold values from -0.21875 to 0.21875
- down_weight: float32 [3072, 768], P('wide', 'narrow'), may hold values from -0.109375 to 0.109375
- vectors: float32 [9216], P(('wide', 'narrow')), may hold values from -1.2 to 1.5, as said below
- bucket_counts: int32 [32, 3], P(('wide', 'narrow')), may hold values from 0 to 16, as said below
- cotangent: bfloat16 [32768, 768], P(('wide', 'narrow')), may hold values from -6 to 6
Outputs:
- block_out: bfloat16 [32768, 768], P(('wide', 'narrow'))
- input_grad: bfloat16 [32768, 768], P(('wide', 'narrow'))
- qkv_grad: float32 [768, 2304], P('narrow', 'wide')
- out_grad: float32 [768, 768], P('wide', 'narrow')
- up_grad: float32 [768, 3072], P('narrow', 'wide')
- down_grad: float32 [3072, 768], P('wide', 'narrow')
- vector_grad: float32 [9216], P(('wide', 'narrow'))
The draws below stay inside these ranges and needn't reach their ends.
Inputs may be any that keep to these rules, and one draw needn't show every extreme that they name: `bucket_counts`: row r gives how many images of 25, 49 and 64 patches device r holds, laid out in that order; together they fill its 1024 tokens exactly. No count exceeds 1024 // 64. `vectors`: gains lie in 0.5 to 1.5, all other entries in -1.2 to 1.2.
All inputs are finite; a program needn't handle non-finite values.
Results may differ from the reference program's by a relative error of at most 0.017.
Values may be sent and summed in bfloat16 or wider, within the bound.
No kernel may reach another device: no remote copies, remote signals or barrier semaphores. Data moves between devices by JAX's collectives and lax.ppermute only.
A program may use at most 256 MiB of HBM per device.

```python
import jax
import jax.numpy as jnp
import numpy as np
from jax import lax

D = 768
HEADS = 12
HEAD_DIM = 64
FF = 3072
TOK_DEV = 1024
P_ONE = 25
P_TWO = 49
P_THREE = 64
GROUPS = 32
TOKENS = 32768


def draw_vectors(key, part):
    key = jax.random.fold_in(key, 11)
    first, second = jax.random.split(key)
    place = jnp.arange(8 * D + FF, dtype=jnp.int32)
    is_gain = (place < D) | (place >= 5 * D) & (place < 6 * D)
    gains = jax.random.uniform(first, (8 * D + FF,), jnp.float32, 0.5, 1.5)
    shifts = jnp.clip(0.3 * jax.random.normal(second, (8 * D + FF,), jnp.float32), -1.2, 1.2)
    return jnp.where(is_gain, gains, shifts)


def draw_bucket_counts(key, part):
    key = jax.random.fold_in(key, 23)
    pick_key, place_key = jax.random.split(key)
    limit = TOK_DEV // P_THREE
    table = []
    forced = 0
    for first in range(min(TOK_DEV // P_ONE, limit) + 1):
        for second in range(min((TOK_DEV - first * P_ONE) // P_TWO, limit) + 1):
            remain = TOK_DEV - first * P_ONE - second * P_TWO
            if remain % P_THREE == 0 and remain // P_THREE <= limit:
                if first == 0 and second == 0:
                    forced = len(table)
                table.append([first, second, remain // P_THREE])
    options = jnp.asarray(np.array(table, dtype=np.int32))
    picks = jax.random.randint(pick_key, (GROUPS,), 0, len(table))
    chosen = jax.random.randint(place_key, (), 0, GROUPS)
    picks = jnp.where(jnp.arange(GROUPS, dtype=jnp.int32) == chosen, forced, picks)
    return options[picks]


def strengthened(drawn, own_key, source, target, blocks, factor):
    owner, partner = [(jnp.arange(drawn.shape[axis_at]) // (drawn.shape[axis_at] // blocks)).reshape([-1 if axis == axis_at else 1 for axis in range(drawn.ndim)]) for axis_at in (source, target)]
    chosen = jax.random.permutation(own_key, blocks)[partner]
    strong = (owner == chosen) | (owner == (partner + blocks // 2) % blocks)
    return jnp.where(strong, factor * drawn, drawn)


def steps_of(key, dims, cuts, smallest, high):
    level, own = 1.0, jax.random.fold_in(key, 6)
    for dim, shards_of in cuts:
        steps = jnp.exp(jax.random.uniform(jax.random.fold_in(own, dim), (shards_of,), jnp.float32, smallest / len(cuts), high / len(cuts)))
        level = level * jnp.repeat(steps, dims[dim] // shards_of).reshape([-1 if axis == dim else 1 for axis in range(len(dims))])
    return level


def bell_draw(key, dims, scale, reach, shards=(), held_as=jnp.bfloat16):
    values = jax.random.normal(key, dims, jnp.float32) * scale
    if len(shards) > 0:
        values = steps_of(key, dims, shards, -0.22, 0.18) * values
    return jnp.clip(values, min=-reach, max=reach).astype(held_as)


def noise_with(key, extent, width, reach, cuts, heavy, kind=jnp.bfloat16):
    entries = width * jax.random.normal(key, extent, jnp.float32)
    if cuts:
        entries = entries * steps_of(key, extent, cuts, -0.22, 0.18)
    return jnp.clip(strengthened(entries, jax.random.fold_in(key, 3), *heavy), -reach, reach).astype(kind)


def setup_inputs(seed: int = 0) -> dict:
    streams_of = jax.random.split(jax.random.key(seed), 9)
    return {
        "tokens": bell_draw(streams_of[0], (TOKENS, D), 1.0, 6.0, ((0, 32),)),
        "qkv_weight": bell_draw(streams_of[1], (D, 3 * D), D ** -0.5, 0.21875, ((0, 4), (1, 8)), jnp.float32),
        "out_weight": bell_draw(streams_of[2], (D, D), (D // 32) ** -0.5, 1.25, ((0, 8), (1, 4)), jnp.float32),
        "up_weight": bell_draw(streams_of[3], (D, FF), D ** -0.5, 0.21875, ((0, 4), (1, 8)), jnp.float32),
        "down_weight": bell_draw(streams_of[4], (FF, D), FF ** -0.5, 0.109375, ((0, 8), (1, 4)), jnp.float32),
        "vectors": draw_vectors(jax.random.fold_in(streams_of[8], 71), 0),
        "bucket_counts": draw_bucket_counts(jax.random.fold_in(streams_of[8], 71), 0),
        "cotangent": noise_with(streams_of[7], (TOKENS, D), 1.0, 6.0, ((0, 32),), (0, 1, 32, 2.75)),
    }


EPS = 1e-06
NEG = -1e+30
HIGH = lax.Precision.HIGHEST

@jax.custom_vjp
def low(v):
    return lax.optimization_barrier(v.astype(jnp.bfloat16)).astype(jnp.float32)

@jax.custom_vjp
def low_back(v):
    return v

def low_keep(v):
    return (low(v), None)

def low_pass(kept, grad):
    return (grad,)

def back_keep(v):
    return (v, None)

def back_low(kept, grad):
    return (low(grad),)
low.defvjp(low_keep, low_pass)
low_back.defvjp(back_keep, back_low)

def layer_norm(values, gain, shift):
    center = values - lax.optimization_barrier(jnp.mean(values, axis=-1, keepdims=True))
    spread = lax.optimization_barrier(jnp.mean(center * center, axis=-1, keepdims=True))
    return center * lax.rsqrt(spread + EPS) * gain + shift

def image_ids(counts, rows):
    place = jnp.arange(rows, dtype=jnp.int32)
    first = counts[0] * P_ONE
    second = first + counts[1] * P_TWO
    bucket = (place >= first).astype(jnp.int32) + (place >= second).astype(jnp.int32)
    start = jnp.where(bucket == 0, 0, jnp.where(bucket == 1, first, second)).astype(jnp.int32)
    length = jnp.where(bucket == 0, P_ONE, jnp.where(bucket == 1, P_TWO, P_THREE)).astype(jnp.int32)
    return bucket * rows + (place - start) // length

def gelu_exact(values):
    return jax.nn.gelu(values, approximate=False)

def attend(pieces):
    query, keys, values, segment = pieces
    raw = jnp.einsum('qhd,khd->hqk', query, keys, precision=HIGH) * HEAD_DIM ** (-0.5)
    raw = low_back(raw)
    masked = jnp.where(segment[:, None] == segment[None, :], raw, NEG)
    top = lax.optimization_barrier(jnp.max(masked, axis=-1, keepdims=True))
    expo = jnp.exp(masked - top)
    probs = low(expo / lax.optimization_barrier(jnp.sum(expo, axis=-1, keepdims=True)))
    return jnp.einsum('hqk,khd->qhd', probs, values, precision=HIGH).reshape(TOK_DEV, D)

def forward(inputs, qkv_weight, out_weight, up_weight, down_weight, vectors, segments):
    qkv_full = low(qkv_weight)
    out_full = low(out_weight)
    up_full = low(up_weight)
    down_full = low(down_weight)
    params = low(vectors)
    gain_one = params[0:D]
    shift_one = params[D:2 * D]
    bias_query = params[2 * D:3 * D]
    bias_value = params[3 * D:4 * D]
    bias_out = params[4 * D:5 * D]
    gain_two = params[5 * D:6 * D]
    shift_two = params[6 * D:7 * D]
    bias_down = params[7 * D:8 * D]
    bias_up = params[8 * D:]
    hidden_one = low(layer_norm(inputs, gain_one, shift_one))
    qkv_bias = jnp.concatenate([bias_query, jnp.zeros((D,), jnp.float32), bias_value])
    qkv_all = low_back(low(jnp.dot(hidden_one, qkv_full, precision=HIGH) + qkv_bias))
    shaped = qkv_all.reshape(GROUPS, TOK_DEV, 3, HEADS, HEAD_DIM)
    attended = lax.map(jax.checkpoint(attend), (shaped[:, :, 0], shaped[:, :, 1], shaped[:, :, 2], segments))
    attended = low_back(low(attended.reshape(TOKENS, D)))
    mid = inputs + low_back(jnp.dot(attended, out_full, precision=HIGH) + bias_out)
    hidden_two = low(layer_norm(mid, gain_two, shift_two))
    pre_act = low_back(jnp.dot(hidden_two, up_full, precision=HIGH) + bias_up)
    activated = low(gelu_exact(pre_act))
    return mid + low_back(jnp.dot(activated, down_full, precision=HIGH) + bias_down)

def reference(tokens, qkv_weight, out_weight, up_weight, down_weight, vectors, bucket_counts, cotangent):

    def device_ids(counts):
        return image_ids(counts, TOK_DEV)
    segments = jax.vmap(device_ids)(bucket_counts)

    def wrapped(inputs, first, second, third, fourth, fifth):
        return forward(inputs, first, second, third, fourth, fifth, segments)
    output, backward = jax.vjp(wrapped, tokens.astype(jnp.float32), qkv_weight, out_weight, up_weight, down_weight, vectors)
    grads = backward(cotangent.astype(jnp.float32))
    return (output.astype(jnp.bfloat16), grads[0].astype(jnp.bfloat16), grads[1], grads[2], grads[3], grads[4], grads[5])
```

```python
import jax
import jax.numpy as jnp
from jax import lax
from jax.experimental import pallas as pl
from jax.experimental.pallas import tpu as pltpu
from jax.sharding import PartitionSpec as P

HEADS = 12
HEAD_DIM = 64
QROWS = 512
P_ONE = 25
P_TWO = 49
P_THREE = 64


EPS = 1e-06
NEG = -1e30


def layer_norm(values, gain, shift):
    center = values - jnp.mean(values, axis=-1, keepdims=True)
    spread = jnp.mean(center * center, axis=-1, keepdims=True)
    return center * lax.rsqrt(spread + EPS) * gain + shift


def image_ids(counts, rows):
    place = jnp.arange(rows, dtype=jnp.int32)
    first = counts[0] * P_ONE
    second = first + counts[1] * P_TWO
    bucket = (place >= first).astype(jnp.int32) + (place >= second).astype(jnp.int32)
    start = jnp.where(bucket == 0, 0, jnp.where(bucket == 1, first, second))
    length = jnp.where(bucket == 0, P_ONE, jnp.where(bucket == 1, P_TWO, P_THREE)).astype(jnp.int32)
    return bucket * rows + (place - start) // length


def gelu_exact(values):
    return jax.nn.gelu(values, approximate=False)


def contract_rows(left, right):
    return lax.dot_general(
        left, right, (((0,), (0,)), ((), ())), preferred_element_type=jnp.float32
    )


def contract_cols(left, right):
    return lax.dot_general(
        left, right, (((1,), (1,)), ((), ())), preferred_element_type=jnp.float32
    )


def windows_of(values, margin, blocks, fill):
    rows = values.shape[0]
    block_rows = rows // blocks
    rest = values.shape[1:]
    padded = jnp.pad(
        values, ((margin, margin),) + tuple(((0, 0) for unused in rest)), constant_values=fill
    )
    before = padded[:rows].reshape((blocks, block_rows) + rest)[:, :margin]
    middle = values.reshape((blocks, block_rows) + rest)
    after = padded[2 * margin : 2 * margin + rows].reshape((blocks, block_rows) + rest)[
        :, block_rows - margin :
    ]
    return jnp.concatenate([before, middle, after], axis=1)


def fold_windows(grads, margin, block_rows):
    blocks = grads.shape[0]
    width = grads.shape[2]
    middle = grads[:, margin : margin + block_rows]
    before = jnp.pad(grads[1:, :margin], ((0, 1), (block_rows - margin, 0), (0, 0)))
    after = jnp.pad(grads[:-1, margin + block_rows :], ((1, 0), (0, block_rows - margin), (0, 0)))
    return (middle + before + after).reshape(blocks * block_rows, width)


BF = jnp.bfloat16
F32 = jnp.float32
AXES = ("wide", "narrow")


class Topo:
    def __init__(self, wide, narrow):
        self.wide, self.narrow = wide, narrow
        self.Y = narrow // 2
        self.X = self.Y
        self.Z = wide // self.X
        side, deep = self.X, self.Z
        self.zp = [self.perm(lambda z, x, y, c, k=k: ((z + k) % deep, x, y, c)) for k in range(deep)]
        self.ap = [
            self.perm(
                lambda z, x, y, c, k=k: (z, (x + k) % side, y, c) if c == 0 else (z, x, (y + k) % side, c)
            )
            for k in range(side)
        ]
        self.bp = [
            self.perm(
                lambda z, x, y, c, k=k: (z, x, (y + k) % side, c) if c == 0 else (z, (x + k) % side, y, c)
            )
            for k in range(side)
        ]
        self.cp = self.perm(lambda z, x, y, c: (z, x, y, 1 - c))

    def did(self, z, x, y, c):
        return ((z * self.X + x) * self.Y + y) * 2 + c

    def perm(self, target):
        return [
            (self.did(z, x, y, c), self.did(*target(z, x, y, c)))
            for z in range(self.Z)
            for x in range(self.X)
            for y in range(self.Y)
            for c in range(2)
        ]

    def here(self):
        wide, narrow = lax.axis_index("wide"), lax.axis_index("narrow")
        return wide // self.X, wide % self.X, narrow // 2, narrow % 2

    def origins(self):
        z0, x0, y0, c0 = self.here()
        rows = []
        for other in range(2):
            c = (c0 + other) % 2
            for kb in range(self.X):
                for ka in range(self.X):
                    x = (x0 + self.X - jnp.where(c == 0, ka, kb)) % self.X
                    y = (y0 + self.Y - jnp.where(c == 0, kb, ka)) % self.Y
                    for kz in range(self.Z):
                        z = (z0 + self.Z - kz) % self.Z
                        rows.append(jnp.stack([z * self.X + x, y, c]))
        return jnp.stack(rows).astype(jnp.int32)


def send(values, perm):
    return lax.ppermute(values, AXES, perm)


def pick_half(values, axis, index):
    half = values.shape[axis] // 2
    return lax.dynamic_slice_in_dim(values, index * half, half, axis)


def pair_up(shard, topo, core):
    mine = pick_half(shard, 0, core)
    other = send(pick_half(shard, 0, 1 - core), topo.cp)
    first = jnp.where(core == 0, mine, other)
    second = jnp.where(core == 0, other, mine)
    return jnp.concatenate([first, second], axis=1)


def unpair(piece, topo, core):
    mine = pick_half(piece, 1, core)
    other = send(pick_half(piece, 1, 1 - core), topo.cp)
    first = jnp.where(core == 0, mine, other)
    second = jnp.where(core == 0, other, mine)
    return jnp.concatenate([first, second], axis=0)


def gather(piece, topo):
    stack = jnp.stack([piece] + [send(piece, topo.zp[k]) for k in range(1, topo.Z)])
    line = [stack] + [send(stack, topo.ap[k]) for k in range(1, topo.X)]
    own = [p for k in range(topo.X) for p in (line if k == 0 else [send(q, topo.bp[k]) for q in line])]
    return own + [send(p, topo.cp) for p in own]


def total(first, *rest):
    result = first.astype(F32)
    for other in rest:
        result = result + other.astype(F32)
    return result


def scatter(pieces, topo):
    side, deep = topo.X, topo.Z
    half = side * side
    own = [total(pieces[i], send(pieces[half + i], topo.cp)).astype(BF) for i in range(half)]
    line = [
        total(own[a], *[send(own[k * side + a], topo.bp[side - k]) for k in range(1, side)]).astype(BF)
        for a in range(side)
    ]
    stack = total(line[0], *[send(line[k], topo.ap[side - k]) for k in range(1, side)]).astype(BF)
    return total(stack[0], *[send(stack[k], topo.zp[deep - k]) for k in range(1, deep)])


def dma_call(kernel, out_shape, operands, n):
    return pl.pallas_call(
        kernel,
        grid_spec=pltpu.PrefetchScalarGridSpec(
            num_scalar_prefetch=1,
            grid=(1,),
            in_specs=[pl.BlockSpec(memory_space=pl.ANY)] * (len(operands) - 1),
            out_specs=jax.tree.map(lambda _: pl.BlockSpec(memory_space=pl.ANY), out_shape),
            scratch_shapes=[pltpu.SemaphoreType.DMA((n,))],
        ),
        out_shape=out_shape,
    )(*operands)


def assemble(pieces, places, low, rows, topo):
    deep, lanes = topo.Z, pieces[0].shape[2]

    def kernel(at, *refs):
        out, sems = refs[-2], refs[-1]
        copies = []
        for i in range(len(pieces)):
            for k in range(deep):
                j = i * deep + k
                row = pl.multiple_of((at[j, 0] * 2 + at[j, 2]) * rows, 16)
                lane = pl.multiple_of(at[j, 1] * lanes, 128)
                copy = pltpu.make_async_copy(
                    refs[i].at[k, pl.ds(low, rows), :],
                    out.at[pl.ds(row, rows), pl.ds(lane, lanes)],
                    sems.at[j],
                )
                copy.start()
                copies.append(copy)
        for copy in copies:
            copy.wait()

    shape = jax.ShapeDtypeStruct((topo.wide * 2 * rows, topo.Y * lanes), pieces[0].dtype)
    return dma_call(kernel, shape, (places, *pieces), len(pieces) * deep)


def disassemble(whole, places, topo):
    deep, rows, lanes = topo.Z, whole.shape[0] // (2 * topo.wide), whole.shape[1] // topo.Y
    count = 2 * topo.X * topo.X

    def kernel(at, src, *refs):
        outs, sems = refs[:-1], refs[-1]
        copies = []
        for i in range(count):
            for k in range(deep):
                j = i * deep + k
                row = pl.multiple_of((at[j, 0] * 2 + at[j, 2]) * rows, 16)
                lane = pl.multiple_of(at[j, 1] * lanes, 128)
                copy = pltpu.make_async_copy(
                    src.at[pl.ds(row, rows), pl.ds(lane, lanes)], outs[i].at[k], sems.at[j]
                )
                copy.start()
                copies.append(copy)
        for copy in copies:
            copy.wait()

    shapes = [jax.ShapeDtypeStruct((deep, rows, lanes), whole.dtype)] * count
    return dma_call(kernel, shapes, (places, whole), count * deep)


def tail_rows(values, rows, lanes):
    return jnp.pad(values[None], ((0, 15), (0, lanes - values.shape[0])))


def vector_slots(places, topo):
    slot = places[:, 0] * topo.narrow + places[:, 1] * 2 + places[:, 2]
    return (slot[:, None] == jnp.arange(topo.wide * topo.narrow)[None]).astype(BF)


def fits(topo, width, hidden):
    lanes = 2 * width // topo.narrow
    return lanes % 128 == 0 and (width // topo.wide) % 32 == 0 and (hidden // topo.wide) % 32 == 0


def gather_weights(qkv_weight, out_weight, up_weight, down_weight, vectors, topo, places):
    shards = [
        qkv_weight.astype(BF).T,
        out_weight.astype(BF),
        up_weight.astype(BF).T,
        down_weight.astype(BF),
    ]
    if places is None:
        wholes = [
            lax.all_gather(lax.all_gather(s, "narrow", axis=1, tiled=True), "wide", axis=0, tiled=True)
            for s in shards
        ]
        return (*wholes, lax.all_gather(vectors.astype(BF), AXES, axis=0, tiled=True))
    core = topo.here()[3]
    first = pair_up(shards[0], topo, core)
    rest = pair_up(
        jnp.concatenate(
            [pick_half(s, 0, h) for h in range(2) for s in shards[1:]], axis=0
        ),
        topo,
        core,
    )
    rows = [s.shape[0] // 2 for s in shards]
    lanes = first.shape[1]
    one = gather(jnp.concatenate([first, tail_rows(vectors.astype(BF), 16, lanes)], axis=0), topo)
    two = gather(rest[: rows[1] + rows[2]], topo)
    three = gather(rest[rows[1] + rows[2] :], topo)
    packed = jnp.concatenate([p[:, rows[0], : vectors.shape[0]] for p in one], axis=0)
    ordered = lax.dot_general(
        vector_slots(places, topo), packed, (((0,), (0,)), ((), ())), preferred_element_type=F32
    )
    return (
        assemble(one, places, 0, rows[0], topo),
        assemble(two, places, 0, rows[1], topo),
        assemble(two, places, rows[1], rows[2], topo),
        assemble(three, places, 0, rows[3], topo),
        ordered.reshape(-1).astype(BF),
    )


def reduce_grad(whole, topo, places, extra=None):
    if places is None:
        part = lax.psum_scatter(whole.astype(BF), "wide", scatter_dimension=0, tiled=True)
        return lax.psum_scatter(part, "narrow", scatter_dimension=1, tiled=True).astype(F32)
    pieces = disassemble(whole.astype(BF), places, topo)
    if extra is not None:
        pieces = [jnp.concatenate([p, e], axis=1) for p, e in zip(pieces, extra)]
    return scatter(pieces, topo)

def per_device(
    tokens, qkv_weight, out_weight, up_weight, down_weight, vectors, bucket_counts, cotangent
):
    rows, width = tokens.shape
    topo = Topo(lax.axis_size("wide"), lax.axis_size("narrow"))
    places = topo.origins() if fits(topo, width, up_weight.shape[1] * topo.wide) else None
    core = topo.here()[3]
    wholes = gather_weights(qkv_weight, out_weight, up_weight, down_weight, vectors, topo, places)
    qkv_full, out_full, up_full, down_full, packed = wholes
    params = packed.astype(jnp.float32)
    gain_one = params[0:width]
    shift_one = params[width : 2 * width]
    bias_query = params[2 * width : 3 * width]
    bias_value = params[3 * width : 4 * width]
    bias_out = params[4 * width : 5 * width]
    gain_two = params[5 * width : 6 * width]
    shift_two = params[6 * width : 7 * width]
    bias_down = params[7 * width : 8 * width]
    bias_up = params[8 * width :]
    inputs = tokens.astype(jnp.float32)
    hidden_one = layer_norm(inputs, gain_one, shift_one).astype(jnp.bfloat16)
    qkv_bias = jnp.concatenate([bias_query, jnp.zeros((width,), jnp.float32), bias_value])
    qkv_all = (contract_cols(hidden_one, qkv_full) + qkv_bias).astype(
        jnp.bfloat16
    )
    margin = P_THREE
    blocks = rows // QROWS
    span = QROWS + 2 * margin
    scale = HEAD_DIM ** (-0.5)
    query_blk = qkv_all[:, :width].reshape(blocks, QROWS, HEADS, HEAD_DIM)
    keys_win = windows_of(qkv_all[:, width : 2 * width], margin, blocks, 0).reshape(
        blocks, span, HEADS, HEAD_DIM
    )
    values_win = windows_of(qkv_all[:, 2 * width :], margin, blocks, 0).reshape(
        blocks, span, HEADS, HEAD_DIM
    )
    segment = image_ids(bucket_counts[0], rows)
    seg_rows = segment.reshape(blocks, QROWS)
    seg_cols = windows_of(segment, margin, blocks, -1)
    same = seg_rows[:, None, :, None] == seg_cols[:, None, None, :]
    raw = (
        jnp.einsum("bqhd,bkhd->bhqk", query_blk, keys_win, preferred_element_type=jnp.float32)
        * scale
    )
    masked = jnp.where(same, raw, NEG)
    top = jnp.max(masked, axis=3, keepdims=True)
    expo = jnp.exp(masked - top)
    total = jnp.sum(expo, axis=3, keepdims=True)
    probs_low = (expo / total).astype(jnp.bfloat16)
    log_total = top + jnp.log(total)
    attended = jnp.einsum(
        "bhqk,bkhd->bqhd", probs_low, values_win, preferred_element_type=jnp.float32
    )
    attn_low = attended.reshape(rows, width).astype(jnp.bfloat16)
    mid = inputs + jnp.dot(attn_low, out_full, preferred_element_type=jnp.float32) + bias_out
    hidden_two = layer_norm(mid, gain_two, shift_two).astype(jnp.bfloat16)
    pre_act = contract_cols(hidden_two, up_full) + bias_up
    activated = gelu_exact(pre_act).astype(jnp.bfloat16)
    output = mid + jnp.dot(activated, down_full, preferred_element_type=jnp.float32) + bias_down
    block_out = output.astype(jnp.bfloat16)
    grad_top = cotangent.astype(jnp.float32)
    d_down = contract_rows(activated, cotangent)
    d_bias_down = jnp.sum(grad_top, axis=0)
    grad_act = contract_cols(cotangent, down_full)
    unused_act, gelu_back = jax.vjp(gelu_exact, pre_act)
    grad_pre = gelu_back(grad_act)[0].astype(jnp.bfloat16)
    d_up = contract_rows(grad_pre, hidden_two)
    d_bias_up = jnp.sum(grad_pre.astype(jnp.float32), axis=0)
    grad_hidden_two = jnp.dot(grad_pre, up_full, preferred_element_type=F32)
    unused_two, norm_back_two = jax.vjp(layer_norm, mid, gain_two, shift_two)
    grad_mid_part, d_gain_two, d_shift_two = norm_back_two(grad_hidden_two)
    grad_mid = grad_top + grad_mid_part
    grad_mid_low = grad_mid.astype(jnp.bfloat16)
    d_out = contract_rows(attn_low, grad_mid_low)
    d_bias_out = jnp.sum(grad_mid_low.astype(jnp.float32), axis=0)
    grad_attn = contract_cols(grad_mid_low, out_full).astype(jnp.bfloat16)
    raw_again = (
        jnp.einsum("bqhd,bkhd->bhqk", query_blk, keys_win, preferred_element_type=jnp.float32)
        * scale
    )
    probs = jnp.exp(jnp.where(same, raw_again, NEG) - log_total)
    grad_blk = grad_attn.reshape(blocks, QROWS, HEADS, HEAD_DIM)
    grad_probs = jnp.einsum(
        "bqhd,bkhd->bhqk", grad_blk, values_win, preferred_element_type=jnp.float32
    )
    grad_scores = (
        probs * (grad_probs - jnp.sum(probs * grad_probs, axis=3, keepdims=True))
    ).astype(jnp.bfloat16)
    grad_query = (
        jnp.einsum("bhqk,bkhd->bqhd", grad_scores, keys_win, preferred_element_type=jnp.float32)
        * scale
    )
    grad_keys_win = (
        jnp.einsum("bhqk,bqhd->bkhd", grad_scores, query_blk, preferred_element_type=jnp.float32)
        * scale
    )
    grad_values_win = jnp.einsum(
        "bhqk,bqhd->bkhd", probs.astype(jnp.bfloat16), grad_blk, preferred_element_type=jnp.float32
    )
    grad_keys = fold_windows(grad_keys_win.reshape(blocks, span, width), margin, QROWS)
    grad_values = fold_windows(grad_values_win.reshape(blocks, span, width), margin, QROWS)
    grad_qkv = jnp.concatenate(
        [grad_query.reshape(rows, width), grad_keys, grad_values], axis=1
    ).astype(jnp.bfloat16)
    d_qkv = contract_rows(grad_qkv, hidden_one)
    column_sums = jnp.sum(grad_qkv.astype(jnp.float32), axis=0)
    grad_hidden_one = jnp.dot(grad_qkv, qkv_full, preferred_element_type=F32)
    unused_one, norm_back_one = jax.vjp(layer_norm, inputs, gain_one, shift_one)
    grad_in_part, d_gain_one, d_shift_one = norm_back_one(grad_hidden_one)
    input_grad = (grad_mid + grad_in_part).astype(jnp.bfloat16)
    d_vector = jnp.concatenate(
        [
            d_gain_one,
            d_shift_one,
            column_sums[:width],
            column_sums[2 * width :],
            d_bias_out,
            d_gain_two,
            d_shift_two,
            d_bias_down,
            d_bias_up,
        ]
    )
    if places is None:
        grads = [reduce_grad(g, topo, None) for g in (d_qkv, d_out, d_up, d_down)]
        vector_grad = lax.psum_scatter(d_vector.astype(BF), AXES, scatter_dimension=0, tiled=True).astype(F32)
    else:
        lanes = topo.Y * 0 + 2 * width // topo.narrow
        rel = jnp.dot(
            vector_slots(places, topo),
            d_vector.astype(BF).reshape(topo.wide * topo.narrow, -1),
            preferred_element_type=F32,
        ).astype(BF)
        rel = jnp.pad(rel[:, None, :], ((0, 0), (0, 15), (0, lanes - rel.shape[1])))
        extra = [rel[i : i + topo.Z] for i in range(0, rel.shape[0], topo.Z)]
        down_sum = reduce_grad(d_down, topo, places)
        up_sum = reduce_grad(d_up, topo, places)
        out_sum = reduce_grad(d_out, topo, places)
        qkv_sum = reduce_grad(d_qkv, topo, places, extra)
        vector_grad = qkv_sum[-16, : vectors.shape[0]]
        grads = [unpair(g, topo, core) for g in (qkv_sum[:-16], out_sum, up_sum, down_sum)]
    return (block_out, input_grad, grads[0].T, grads[1], grads[2].T, grads[3], vector_grad)


def solution(mesh):
    return jax.shard_map(
        per_device,
        mesh=mesh,
        in_specs=(
            P(("wide", "narrow"), None),
            P("narrow", "wide"),
            P("wide", "narrow"),
            P("narrow", "wide"),
            P("wide", "narrow"),
            P(("wide", "narrow")),
            P(("wide", "narrow"), None),
            P(("wide", "narrow"), None),
        ),
        out_specs=(
            P(("wide", "narrow"), None),
            P(("wide", "narrow"), None),
            P("narrow", "wide"),
            P("wide", "narrow"),
            P("narrow", "wide"),
            P("wide", "narrow"),
            P(("wide", "narrow")),
        ),
        check_vma=False,
    )
```

```python
import jax
import jax.numpy as jnp
from jax import lax
from jax.experimental import pallas as pl
from jax.experimental.pallas import tpu as pltpu
from jax.sharding import PartitionSpec as P

HEADS = 12
HEAD_DIM = 64
QROWS = 512
P_ONE = 25
P_TWO = 49
P_THREE = 64


EPS = 1e-06
NEG = -1e30


def layer_norm(values, gain, shift):
    center = values - jnp.mean(values, axis=-1, keepdims=True)
    spread = jnp.mean(center * center, axis=-1, keepdims=True)
    return center * lax.rsqrt(spread + EPS) * gain + shift


def image_ids(counts, rows):
    place = jnp.arange(rows, dtype=jnp.int32)
    first = counts[0] * P_ONE
    second = first + counts[1] * P_TWO
    bucket = (place >= first).astype(jnp.int32) + (place >= second).astype(jnp.int32)
    start = jnp.where(bucket == 0, 0, jnp.where(bucket == 1, first, second))
    length = jnp.where(bucket == 0, P_ONE, jnp.where(bucket == 1, P_TWO, P_THREE)).astype(jnp.int32)
    return bucket * rows + (place - start) // length


def gelu_exact(values):
    return jax.nn.gelu(values, approximate=False)


def contract_rows(left, right):
    return lax.dot_general(
        left, right, (((0,), (0,)), ((), ())), preferred_element_type=jnp.float32
    )


def contract_cols(left, right):
    return lax.dot_general(
        left, right, (((1,), (1,)), ((), ())), preferred_element_type=jnp.float32
    )


def windows_of(values, margin, blocks, fill):
    rows = values.shape[0]
    block_rows = rows // blocks
    rest = values.shape[1:]
    padded = jnp.pad(
        values, ((margin, margin),) + tuple(((0, 0) for unused in rest)), constant_values=fill
    )
    before = padded[:rows].reshape((blocks, block_rows) + rest)[:, :margin]
    middle = values.reshape((blocks, block_rows) + rest)
    after = padded[2 * margin : 2 * margin + rows].reshape((blocks, block_rows) + rest)[
        :, block_rows - margin :
    ]
    return jnp.concatenate([before, middle, after], axis=1)


def fold_windows(grads, margin, block_rows):
    blocks = grads.shape[0]
    width = grads.shape[2]
    middle = grads[:, margin : margin + block_rows]
    before = jnp.pad(grads[1:, :margin], ((0, 1), (block_rows - margin, 0), (0, 0)))
    after = jnp.pad(grads[:-1, margin + block_rows :], ((1, 0), (0, block_rows - margin), (0, 0)))
    return (middle + before + after).reshape(blocks * block_rows, width)


BF = jnp.bfloat16
F32 = jnp.float32
AXES = ("wide", "narrow")


class Topo:
    def __init__(self, wide, narrow):
        self.wide, self.narrow = wide, narrow
        self.Y = narrow // 2
        self.X = self.Y
        self.Z = wide // self.X
        side, deep = self.X, self.Z
        self.zp = [self.perm(lambda z, x, y, c, k=k: ((z + k) % deep, x, y, c)) for k in range(deep)]
        self.ap = [
            self.perm(
                lambda z, x, y, c, k=k: (z, (x + k) % side, y, c) if c == 0 else (z, x, (y + k) % side, c)
            )
            for k in range(side)
        ]
        self.bp = [
            self.perm(
                lambda z, x, y, c, k=k: (z, x, (y + k) % side, c) if c == 0 else (z, (x + k) % side, y, c)
            )
            for k in range(side)
        ]
        self.cp = self.perm(lambda z, x, y, c: (z, x, y, 1 - c))

    def did(self, z, x, y, c):
        return ((z * self.X + x) * self.Y + y) * 2 + c

    def perm(self, target):
        return [
            (self.did(z, x, y, c), self.did(*target(z, x, y, c)))
            for z in range(self.Z)
            for x in range(self.X)
            for y in range(self.Y)
            for c in range(2)
        ]

    def here(self):
        wide, narrow = lax.axis_index("wide"), lax.axis_index("narrow")
        return wide // self.X, wide % self.X, narrow // 2, narrow % 2

    def origins(self):
        z0, x0, y0, c0 = self.here()
        rows = []
        for other in range(2):
            c = (c0 + other) % 2
            for kb in range(self.X):
                for ka in range(self.X):
                    x = (x0 + self.X - jnp.where(c == 0, ka, kb)) % self.X
                    y = (y0 + self.Y - jnp.where(c == 0, kb, ka)) % self.Y
                    for kz in range(self.Z):
                        z = (z0 + self.Z - kz) % self.Z
                        rows.append(jnp.stack([z * self.X + x, y, c]))
        return jnp.stack(rows).astype(jnp.int32)


def send(values, perm):
    return lax.ppermute(values, AXES, perm)


def pick_half(values, axis, index):
    half = values.shape[axis] // 2
    return lax.dynamic_slice_in_dim(values, index * half, half, axis)


def pair_up(shard, topo, core):
    mine = pick_half(shard, 0, core)
    other = send(pick_half(shard, 0, 1 - core), topo.cp)
    first = jnp.where(core == 0, mine, other)
    second = jnp.where(core == 0, other, mine)
    return jnp.concatenate([first, second], axis=1)


def unpair(piece, topo, core):
    mine = pick_half(piece, 1, core)
    other = send(pick_half(piece, 1, 1 - core), topo.cp)
    first = jnp.where(core == 0, mine, other)
    second = jnp.where(core == 0, other, mine)
    return jnp.concatenate([first, second], axis=0)


def gather(piece, topo):
    stack = jnp.stack([piece] + [send(piece, topo.zp[k]) for k in range(1, topo.Z)])
    line = [stack] + [send(stack, topo.ap[k]) for k in range(1, topo.X)]
    own = [p for k in range(topo.X) for p in (line if k == 0 else [send(q, topo.bp[k]) for q in line])]
    return own + [send(p, topo.cp) for p in own]


def total(first, *rest):
    result = first.astype(F32)
    for other in rest:
        result = result + other.astype(F32)
    return result


def scatter(pieces, topo):
    side, deep = topo.X, topo.Z
    half = side * side
    own = [total(pieces[i], send(pieces[half + i], topo.cp)).astype(BF) for i in range(half)]
    line = [
        total(own[a], *[send(own[k * side + a], topo.bp[side - k]) for k in range(1, side)]).astype(BF)
        for a in range(side)
    ]
    stack = total(line[0], *[send(line[k], topo.ap[side - k]) for k in range(1, side)]).astype(BF)
    return total(stack[0], *[send(stack[k], topo.zp[deep - k]) for k in range(1, deep)])


def dma_call(kernel, out_shape, operands, n, in_spec, out_spec):
    return pl.pallas_call(
        kernel,
        grid_spec=pltpu.PrefetchScalarGridSpec(
            num_scalar_prefetch=1,
            grid=(1,),
            in_specs=[in_spec] * (len(operands) - 1),
            out_specs=jax.tree.map(lambda _: out_spec, out_shape),
            scratch_shapes=[pltpu.SemaphoreType.DMA((n,))],
        ),
        out_shape=out_shape,
        compiler_params=pltpu.CompilerParams(vmem_limit_bytes=32 * 1024 * 1024),
    )(*operands)


ANYWHERE = pl.BlockSpec(memory_space=pl.ANY)


def whole_block(shape):
    return pl.BlockSpec(shape, lambda i, at: (0,) * len(shape))


def assemble(pieces, places, low, rows, topo):
    deep, lanes = topo.Z, pieces[0].shape[2]

    def kernel(at, *refs):
        out, sems = refs[-2], refs[-1]
        copies = []
        for i in range(len(pieces)):
            for k in range(deep):
                j = i * deep + k
                row = pl.multiple_of((at[j, 0] * 2 + at[j, 2]) * rows, 16)
                lane = pl.multiple_of(at[j, 1] * lanes, 128)
                copy = pltpu.make_async_copy(
                    refs[i].at[k, pl.ds(low, rows), :],
                    out.at[pl.ds(row, rows), pl.ds(lane, lanes)],
                    sems.at[j],
                )
                copy.start()
                copies.append(copy)
        for copy in copies:
            copy.wait()

    shape = jax.ShapeDtypeStruct((topo.wide * 2 * rows, topo.Y * lanes), pieces[0].dtype)
    return dma_call(kernel, shape, (places, *pieces), len(pieces) * deep, ANYWHERE, whole_block(shape.shape))


def disassemble(whole, places, topo):
    deep, rows, lanes = topo.Z, whole.shape[0] // (2 * topo.wide), whole.shape[1] // topo.Y
    count = 2 * topo.X * topo.X

    def kernel(at, src, *refs):
        outs, sems = refs[:-1], refs[-1]
        copies = []
        for i in range(count):
            for k in range(deep):
                j = i * deep + k
                row = pl.multiple_of((at[j, 0] * 2 + at[j, 2]) * rows, 16)
                lane = pl.multiple_of(at[j, 1] * lanes, 128)
                copy = pltpu.make_async_copy(
                    src.at[pl.ds(row, rows), pl.ds(lane, lanes)], outs[i].at[k], sems.at[j]
                )
                copy.start()
                copies.append(copy)
        for copy in copies:
            copy.wait()

    shapes = [jax.ShapeDtypeStruct((deep, rows, lanes), whole.dtype)] * count
    return dma_call(kernel, shapes, (places, whole), count * deep, whole_block(whole.shape), ANYWHERE)


def tail_rows(values, rows, lanes):
    return jnp.pad(values[None], ((0, 15), (0, lanes - values.shape[0])))


def vector_slots(places, topo):
    slot = places[:, 0] * topo.narrow + places[:, 1] * 2 + places[:, 2]
    return (slot[:, None] == jnp.arange(topo.wide * topo.narrow)[None]).astype(BF)


def fits(topo, width, hidden):
    lanes = 2 * width // topo.narrow
    return lanes % 128 == 0 and (width // topo.wide) % 32 == 0 and (hidden // topo.wide) % 32 == 0


def gather_weights(qkv_weight, out_weight, up_weight, down_weight, vectors, topo, places):
    shards = [
        qkv_weight.astype(BF).T,
        out_weight.astype(BF),
        up_weight.astype(BF).T,
        down_weight.astype(BF),
    ]
    if places is None:
        wholes = [
            lax.all_gather(lax.all_gather(s, "narrow", axis=1, tiled=True), "wide", axis=0, tiled=True)
            for s in shards
        ]
        return (*wholes, lax.all_gather(vectors.astype(BF), AXES, axis=0, tiled=True))
    core = topo.here()[3]
    first = pair_up(shards[0], topo, core)
    rest = pair_up(
        jnp.concatenate(
            [pick_half(s, 0, h) for h in range(2) for s in shards[1:]], axis=0
        ),
        topo,
        core,
    )
    rows = [s.shape[0] // 2 for s in shards]
    lanes = first.shape[1]
    one = gather(jnp.concatenate([first, tail_rows(vectors.astype(BF), 16, lanes)], axis=0), topo)
    two = gather(rest[: rows[1] + rows[2]], topo)
    three = gather(rest[rows[1] + rows[2] :], topo)
    packed = jnp.concatenate([p[:, rows[0], : vectors.shape[0]] for p in one], axis=0)
    ordered = lax.dot_general(
        vector_slots(places, topo), packed, (((0,), (0,)), ((), ())), preferred_element_type=F32
    )
    return (
        assemble(one, places, 0, rows[0], topo),
        assemble(two, places, 0, rows[1], topo),
        assemble(two, places, rows[1], rows[2], topo),
        assemble(three, places, 0, rows[3], topo),
        ordered.reshape(-1).astype(BF),
    )


def reduce_grad(whole, topo, places, extra=None):
    if places is None:
        part = lax.psum_scatter(whole.astype(BF), "wide", scatter_dimension=0, tiled=True)
        return lax.psum_scatter(part, "narrow", scatter_dimension=1, tiled=True).astype(F32)
    pieces = disassemble(whole.astype(BF), places, topo)
    if extra is not None:
        pieces = [jnp.concatenate([p, e], axis=1) for p, e in zip(pieces, extra)]
    return scatter(pieces, topo)

def per_device(
    tokens, qkv_weight, out_weight, up_weight, down_weight, vectors, bucket_counts, cotangent
):
    rows, width = tokens.shape
    topo = Topo(lax.axis_size("wide"), lax.axis_size("narrow"))
    places = topo.origins() if fits(topo, width, up_weight.shape[1] * topo.wide) else None
    core = topo.here()[3]
    wholes = gather_weights(qkv_weight, out_weight, up_weight, down_weight, vectors, topo, places)
    qkv_full, out_full, up_full, down_full, packed = wholes
    params = packed.astype(jnp.float32)
    gain_one = params[0:width]
    shift_one = params[width : 2 * width]
    bias_query = params[2 * width : 3 * width]
    bias_value = params[3 * width : 4 * width]
    bias_out = params[4 * width : 5 * width]
    gain_two = params[5 * width : 6 * width]
    shift_two = params[6 * width : 7 * width]
    bias_down = params[7 * width : 8 * width]
    bias_up = params[8 * width :]
    inputs = tokens.astype(jnp.float32)
    hidden_one = layer_norm(inputs, gain_one, shift_one).astype(jnp.bfloat16)
    qkv_bias = jnp.concatenate([bias_query, jnp.zeros((width,), jnp.float32), bias_value])
    qkv_all = (contract_cols(hidden_one, qkv_full) + qkv_bias).astype(
        jnp.bfloat16
    )
    margin = P_THREE
    blocks = rows // QROWS
    span = QROWS + 2 * margin
    scale = HEAD_DIM ** (-0.5)
    query_blk = qkv_all[:, :width].reshape(blocks, QROWS, HEADS, HEAD_DIM)
    keys_win = windows_of(qkv_all[:, width : 2 * width], margin, blocks, 0).reshape(
        blocks, span, HEADS, HEAD_DIM
    )
    values_win = windows_of(qkv_all[:, 2 * width :], margin, blocks, 0).reshape(
        blocks, span, HEADS, HEAD_DIM
    )
    segment = image_ids(bucket_counts[0], rows)
    seg_rows = segment.reshape(blocks, QROWS)
    seg_cols = windows_of(segment, margin, blocks, -1)
    same = seg_rows[:, None, :, None] == seg_cols[:, None, None, :]
    raw = (
        jnp.einsum("bqhd,bkhd->bhqk", query_blk, keys_win, preferred_element_type=jnp.float32)
        * scale
    )
    masked = jnp.where(same, raw, NEG)
    top = jnp.max(masked, axis=3, keepdims=True)
    expo = jnp.exp(masked - top)
    total = jnp.sum(expo, axis=3, keepdims=True)
    probs_low = (expo / total).astype(jnp.bfloat16)
    log_total = top + jnp.log(total)
    attended = jnp.einsum(
        "bhqk,bkhd->bqhd", probs_low, values_win, preferred_element_type=jnp.float32
    )
    attn_low = attended.reshape(rows, width).astype(jnp.bfloat16)
    mid = inputs + jnp.dot(attn_low, out_full, preferred_element_type=jnp.float32) + bias_out
    hidden_two = layer_norm(mid, gain_two, shift_two).astype(jnp.bfloat16)
    pre_act = contract_cols(hidden_two, up_full) + bias_up
    activated = gelu_exact(pre_act).astype(jnp.bfloat16)
    output = mid + jnp.dot(activated, down_full, preferred_element_type=jnp.float32) + bias_down
    block_out = output.astype(jnp.bfloat16)
    grad_top = cotangent.astype(jnp.float32)
    d_down = contract_rows(activated, cotangent)
    d_bias_down = jnp.sum(grad_top, axis=0)
    grad_act = contract_cols(cotangent, down_full)
    unused_act, gelu_back = jax.vjp(gelu_exact, pre_act)
    grad_pre = gelu_back(grad_act)[0].astype(jnp.bfloat16)
    d_up = contract_rows(grad_pre, hidden_two)
    d_bias_up = jnp.sum(grad_pre.astype(jnp.float32), axis=0)
    grad_hidden_two = jnp.dot(grad_pre, up_full, preferred_element_type=F32)
    unused_two, norm_back_two = jax.vjp(layer_norm, mid, gain_two, shift_two)
    grad_mid_part, d_gain_two, d_shift_two = norm_back_two(grad_hidden_two)
    grad_mid = grad_top + grad_mid_part
    grad_mid_low = grad_mid.astype(jnp.bfloat16)
    d_out = contract_rows(attn_low, grad_mid_low)
    d_bias_out = jnp.sum(grad_mid_low.astype(jnp.float32), axis=0)
    grad_attn = contract_cols(grad_mid_low, out_full).astype(jnp.bfloat16)
    raw_again = (
        jnp.einsum("bqhd,bkhd->bhqk", query_blk, keys_win, preferred_element_type=jnp.float32)
        * scale
    )
    probs = jnp.exp(jnp.where(same, raw_again, NEG) - log_total)
    grad_blk = grad_attn.reshape(blocks, QROWS, HEADS, HEAD_DIM)
    grad_probs = jnp.einsum(
        "bqhd,bkhd->bhqk", grad_blk, values_win, preferred_element_type=jnp.float32
    )
    grad_scores = (
        probs * (grad_probs - jnp.sum(probs * grad_probs, axis=3, keepdims=True))
    ).astype(jnp.bfloat16)
    grad_query = (
        jnp.einsum("bhqk,bkhd->bqhd", grad_scores, keys_win, preferred_element_type=jnp.float32)
        * scale
    )
    grad_keys_win = (
        jnp.einsum("bhqk,bqhd->bkhd", grad_scores, query_blk, preferred_element_type=jnp.float32)
        * scale
    )
    grad_values_win = jnp.einsum(
        "bhqk,bqhd->bkhd", probs.astype(jnp.bfloat16), grad_blk, preferred_element_type=jnp.float32
    )
    grad_keys = fold_windows(grad_keys_win.reshape(blocks, span, width), margin, QROWS)
    grad_values = fold_windows(grad_values_win.reshape(blocks, span, width), margin, QROWS)
    grad_qkv = jnp.concatenate(
        [grad_query.reshape(rows, width), grad_keys, grad_values], axis=1
    ).astype(jnp.bfloat16)
    d_qkv = contract_rows(grad_qkv, hidden_one)
    column_sums = jnp.sum(grad_qkv.astype(jnp.float32), axis=0)
    grad_hidden_one = jnp.dot(grad_qkv, qkv_full, preferred_element_type=F32)
    unused_one, norm_back_one = jax.vjp(layer_norm, inputs, gain_one, shift_one)
    grad_in_part, d_gain_one, d_shift_one = norm_back_one(grad_hidden_one)
    input_grad = (grad_mid + grad_in_part).astype(jnp.bfloat16)
    d_vector = jnp.concatenate(
        [
            d_gain_one,
            d_shift_one,
            column_sums[:width],
            column_sums[2 * width :],
            d_bias_out,
            d_gain_two,
            d_shift_two,
            d_bias_down,
            d_bias_up,
        ]
    )
    if places is None:
        grads = [reduce_grad(g, topo, None) for g in (d_qkv, d_out, d_up, d_down)]
        vector_grad = lax.psum_scatter(d_vector.astype(BF), AXES, scatter_dimension=0, tiled=True).astype(F32)
    else:
        lanes = topo.Y * 0 + 2 * width // topo.narrow
        rel = jnp.dot(
            vector_slots(places, topo),
            d_vector.astype(BF).reshape(topo.wide * topo.narrow, -1),
            preferred_element_type=F32,
        ).astype(BF)
        rel = jnp.pad(rel[:, None, :], ((0, 0), (0, 15), (0, lanes - rel.shape[1])))
        extra = [rel[i : i + topo.Z] for i in range(0, rel.shape[0], topo.Z)]
        down_sum = reduce_grad(d_down, topo, places)
        up_sum = reduce_grad(d_up, topo, places)
        out_sum = reduce_grad(d_out, topo, places)
        qkv_sum = reduce_grad(d_qkv, topo, places, extra)
        vector_grad = qkv_sum[-16, : vectors.shape[0]]
        grads = [unpair(g, topo, core) for g in (qkv_sum[:-16], out_sum, up_sum, down_sum)]
    return (block_out, input_grad, grads[0].T, grads[1], grads[2].T, grads[3], vector_grad)


def solution(mesh):
    return jax.shard_map(
        per_device,
        mesh=mesh,
        in_specs=(
            P(("wide", "narrow"), None),
            P("narrow", "wide"),
            P("wide", "narrow"),
            P("narrow", "wide"),
            P("wide", "narrow"),
            P(("wide", "narrow")),
            P(("wide", "narrow"), None),
            P(("wide", "narrow"), None),
        ),
        out_specs=(
            P(("wide", "narrow"), None),
            P(("wide", "narrow"), None),
            P("narrow", "wide"),
            P("wide", "narrow"),
            P("narrow", "wide"),
            P("wide", "narrow"),
            P(("wide", "narrow")),
        ),
        check_vma=False,
    )
```

```python
import jax
import jax.numpy as jnp
from jax import lax
from jax.experimental import pallas as pl
from jax.experimental.pallas import tpu as pltpu
from jax.sharding import PartitionSpec as P

HEADS = 12
HEAD_DIM = 64
QROWS = 512
P_ONE = 25
P_TWO = 49
P_THREE = 64


EPS = 1e-06
NEG = -1e30


def layer_norm(values, gain, shift):
    center = values - jnp.mean(values, axis=-1, keepdims=True)
    spread = jnp.mean(center * center, axis=-1, keepdims=True)
    return center * lax.rsqrt(spread + EPS) * gain + shift


def image_ids(counts, rows):
    place = jnp.arange(rows, dtype=jnp.int32)
    first = counts[0] * P_ONE
    second = first + counts[1] * P_TWO
    bucket = (place >= first).astype(jnp.int32) + (place >= second).astype(jnp.int32)
    start = jnp.where(bucket == 0, 0, jnp.where(bucket == 1, first, second))
    length = jnp.where(bucket == 0, P_ONE, jnp.where(bucket == 1, P_TWO, P_THREE)).astype(jnp.int32)
    return bucket * rows + (place - start) // length


def gelu_exact(values):
    return jax.nn.gelu(values, approximate=False)


def contract_rows(left, right):
    return lax.dot_general(
        left, right, (((0,), (0,)), ((), ())), preferred_element_type=jnp.float32
    )


def contract_cols(left, right):
    return lax.dot_general(
        left, right, (((1,), (1,)), ((), ())), preferred_element_type=jnp.float32
    )


def windows_of(values, margin, blocks, fill):
    rows = values.shape[0]
    block_rows = rows // blocks
    rest = values.shape[1:]
    padded = jnp.pad(
        values, ((margin, margin),) + tuple(((0, 0) for unused in rest)), constant_values=fill
    )
    before = padded[:rows].reshape((blocks, block_rows) + rest)[:, :margin]
    middle = values.reshape((blocks, block_rows) + rest)
    after = padded[2 * margin : 2 * margin + rows].reshape((blocks, block_rows) + rest)[
        :, block_rows - margin :
    ]
    return jnp.concatenate([before, middle, after], axis=1)


def fold_windows(grads, margin, block_rows):
    blocks = grads.shape[0]
    width = grads.shape[2]
    middle = grads[:, margin : margin + block_rows]
    before = jnp.pad(grads[1:, :margin], ((0, 1), (block_rows - margin, 0), (0, 0)))
    after = jnp.pad(grads[:-1, margin + block_rows :], ((1, 0), (0, block_rows - margin), (0, 0)))
    return (middle + before + after).reshape(blocks * block_rows, width)


BF = jnp.bfloat16
F32 = jnp.float32
AXES = ("wide", "narrow")


class Topo:
    def __init__(self, wide, narrow):
        self.wide, self.narrow = wide, narrow
        self.Y = narrow // 2
        self.X = self.Y
        self.Z = wide // self.X
        side, deep = self.X, self.Z
        self.zp = [self.perm(lambda z, x, y, c, k=k: ((z + k) % deep, x, y, c)) for k in range(deep)]
        self.ap = [
            self.perm(
                lambda z, x, y, c, k=k: (z, (x + k) % side, y, c) if c == 0 else (z, x, (y + k) % side, c)
            )
            for k in range(side)
        ]
        self.bp = [
            self.perm(
                lambda z, x, y, c, k=k: (z, x, (y + k) % side, c) if c == 0 else (z, (x + k) % side, y, c)
            )
            for k in range(side)
        ]
        self.cp = self.perm(lambda z, x, y, c: (z, x, y, 1 - c))

    def did(self, z, x, y, c):
        return ((z * self.X + x) * self.Y + y) * 2 + c

    def perm(self, target):
        return [
            (self.did(z, x, y, c), self.did(*target(z, x, y, c)))
            for z in range(self.Z)
            for x in range(self.X)
            for y in range(self.Y)
            for c in range(2)
        ]

    def here(self):
        wide, narrow = lax.axis_index("wide"), lax.axis_index("narrow")
        return wide // self.X, wide % self.X, narrow // 2, narrow % 2

    def origins(self):
        z0, x0, y0, c0 = self.here()
        rows = []
        for other in range(2):
            c = (c0 + other) % 2
            for kb in range(self.X):
                for ka in range(self.X):
                    x = (x0 + self.X - jnp.where(c == 0, ka, kb)) % self.X
                    y = (y0 + self.Y - jnp.where(c == 0, kb, ka)) % self.Y
                    for kz in range(self.Z):
                        z = (z0 + self.Z - kz) % self.Z
                        rows.append(jnp.stack([z * self.X + x, y, c]))
        return jnp.stack(rows).astype(jnp.int32)


def send(values, perm):
    return lax.ppermute(values, AXES, perm)


def pick_half(values, axis, index):
    half = values.shape[axis] // 2
    return lax.dynamic_slice_in_dim(values, index * half, half, axis)


def pair_up(shard, topo, core):
    mine = pick_half(shard, 0, core)
    other = send(pick_half(shard, 0, 1 - core), topo.cp)
    first = jnp.where(core == 0, mine, other)
    second = jnp.where(core == 0, other, mine)
    return jnp.concatenate([first, second], axis=1)


def unpair(piece, topo, core):
    mine = pick_half(piece, 1, core)
    other = send(pick_half(piece, 1, 1 - core), topo.cp)
    first = jnp.where(core == 0, mine, other)
    second = jnp.where(core == 0, other, mine)
    return jnp.concatenate([first, second], axis=0)


def gather(piece, topo):
    stack = jnp.stack([piece] + [send(piece, topo.zp[k]) for k in range(1, topo.Z)])
    line = [stack] + [send(stack, topo.ap[k]) for k in range(1, topo.X)]
    own = [p for k in range(topo.X) for p in (line if k == 0 else [send(q, topo.bp[k]) for q in line])]
    return own + [send(p, topo.cp) for p in own]


def nn(a, b):
    return lax.dot_general(a, b, (((1,), (0,)), ((), ())), preferred_element_type=F32)


def nt(a, b):
    return lax.dot_general(a, b, (((1,), (1,)), ((), ())), preferred_element_type=F32)


def tn(a, b):
    return lax.dot_general(a, b, (((0,), (0,)), ((), ())), preferred_element_type=F32)


def normed(values):
    center = values - jnp.mean(values, axis=-1, keepdims=True)
    spread = jnp.mean(center * center, axis=-1, keepdims=True)
    inverse = lax.rsqrt(spread + EPS)
    return center * inverse, inverse


def norm_back(grad, hat, inverse, gain):
    scaled = grad * gain
    first = jnp.mean(scaled, axis=-1, keepdims=True)
    second = jnp.mean(scaled * hat, axis=-1, keepdims=True)
    return inverse * (scaled - first - hat * second)


ROOT_HALF = 0.7071067811865476
ROOT_TAU = 0.3989422804014327
MIB = 1024 * 1024


def cdf_pdf(u):
    bell = jnp.exp(-0.5 * (u * u))
    t = 1.0 / (1.0 + (0.3275911 * ROOT_HALF) * jnp.abs(u))
    poly = 1.061405429 * 0.5
    for coef in (-1.453152027, 1.421413741, -0.284496736, 0.254829592):
        poly = poly * t + coef * 0.5
    upper = poly * t * bell
    return jnp.where(u < 0, upper, 1.0 - upper), ROOT_TAU * bell


def call(kernel, grid, in_specs, out_specs, out_shape, scratch, vmem, flops, bytes_accessed, operands, prefetch=0, aliases=None, after=()):
    first, count = len(operands), len(after)

    def body(*refs):
        kernel(*refs[:first], *refs[first + count :])

    return pl.pallas_call(
        body,
        grid_spec=pltpu.PrefetchScalarGridSpec(
            num_scalar_prefetch=prefetch,
            grid=grid,
            in_specs=in_specs + [ANYWHERE] * count,
            out_specs=out_specs,
            scratch_shapes=scratch,
        ),
        out_shape=out_shape,
        input_output_aliases=aliases or {},
        compiler_params=pltpu.CompilerParams(vmem_limit_bytes=vmem * MIB),
        cost_estimate=pl.CostEstimate(flops=flops, bytes_accessed=bytes_accessed, transcendentals=0),
    )(*operands, *after)


ANYWHERE = pl.BlockSpec(memory_space=pl.ANY)


def full(shape):
    return pl.BlockSpec(shape, lambda *unused: (0,) * len(shape))


def rows_of(shape):
    return pl.BlockSpec(shape, lambda i, *unused: (i,) + (0,) * (len(shape) - 1))


def lanes_of(shape):
    return pl.BlockSpec(shape, lambda i, *unused: (0, i))


def piece_place(at, j, rows, lanes):
    row = pl.multiple_of((at[j, 0] * 2 + at[j, 2]) * rows, 16)
    lane = pl.multiple_of(at[j, 1] * lanes, 128)
    return pl.ds(row, rows), pl.ds(lane, lanes)


def load_pieces(at, pieces, low, rows, whole, sem):
    copies = []
    deep, lanes = pieces[0].shape[0], pieces[0].shape[2]
    for i, piece in enumerate(pieces):
        for k in range(deep):
            place = piece_place(at, i * deep + k, rows, lanes)
            copy = pltpu.make_async_copy(piece.at[k, pl.ds(low, rows), :], whole.at[place], sem.at[i * deep + k])
            copy.start()
            copies.append(copy)
    return copies


def store_pieces(at, whole, rows, own, far, low, sem):
    copies = []
    count, deep, lanes = own.shape[0], own.shape[1], own.shape[3]
    for i in range(2 * count):
        for k in range(deep):
            place = piece_place(at, i * deep + k, rows, lanes)
            target = own.at[i, k] if i < count else far.at[i - count, k]
            copy = pltpu.make_async_copy(whole.at[place], target.at[pl.ds(low, rows), :], sem.at[i * deep + k])
            copy.start()
            copies.append(copy)
    return copies


def wait_all(copies):
    for copy in copies:
        copy.wait()


def unpack_vectors(pieces, places, low, share, width, wide, narrow):
    n, deep, lanes = len(pieces), pieces[0].shape[0], pieces[0].shape[2]
    hidden = wide * narrow * share - 8 * width
    group = hidden // (2 * wide)
    unit = group // 2
    lines = 8 + hidden // width

    def kernel(at, *refs):
        parts, (vecs, bias, up_a, up_b, slots, flat, sem) = refs[:n], refs[n:]
        copies = []
        for i, piece in enumerate(parts):
            for k in range(deep):
                j = i * deep + k
                slot = at[j, 0] * narrow + at[j, 1] * 2 + at[j, 2]
                copy = pltpu.make_async_copy(piece.at[k, pl.ds(low, 16), :], slots.at[slot], sem.at[j])
                copy.start()
                copies.append(copy)
        wait_all(copies)
        for j in range(wide * narrow):
            values = slots[j].astype(F32)[0:1, :]
            done = 0
            while done < share:
                line, lane = divmod(j * share + done, width)
                take = min(share - done, width - lane)
                flat[line : line + 1, lane : lane + take] = values[:, done : done + take]
                done += take
        vecs[...] = flat[0:8, :]
        columns = lambda line: jnp.broadcast_to(flat[line : line + 1, :], (128, width)).T[:, 0:1]
        bias[0:width, :] = columns(2)
        bias[width : 2 * width, :] = jnp.zeros((width, 1), F32)
        bias[2 * width :, :] = columns(3)
        up = jnp.concatenate([columns(line) for line in range(8, lines)], axis=0)
        for k in range(2 * wide):
            up_a[k * unit : (k + 1) * unit, :] = up[k * group : k * group + unit, :]
            up_b[k * unit : (k + 1) * unit, :] = up[k * group + unit : (k + 1) * group, :]

    column = jax.ShapeDtypeStruct((hidden // 2, 1), F32)
    return call(
        kernel,
        (1,),
        [ANYWHERE] * n,
        [full((8, width)), full((3 * width, 1)), full(column.shape), full(column.shape)],
        [jax.ShapeDtypeStruct((8, width), F32), jax.ShapeDtypeStruct((3 * width, 1), F32), column, column],
        [
            pltpu.VMEM((wide * narrow, 16, lanes), BF),
            pltpu.VMEM((16, width), F32),
            pltpu.SemaphoreType.DMA((n * deep,)),
        ],
        16,
        1000,
        1000,
        (places, *pieces),
        prefetch=1,
    )


def project_qkv(tokens, vecs, bias, pieces, places, shape):
    rows, width = tokens.shape
    half, wide = shape
    n, block, steps = len(pieces), 256, 3 * width // 256

    def kernel(at, tok, vec, bias_ref, *refs):
        parts, (hid_out, out, weight, hid, sem) = refs[:n], refs[n:]
        step = pl.program_id(0)

        @pl.when(step == 0)
        def first():
            copies = load_pieces(at, parts, 0, half, weight, sem)
            hat, unused = normed(tok[...].astype(F32))
            hid[...] = (hat * vec[0:1, :] + vec[1:2, :]).astype(BF)
            hid_out[...] = hid[...]
            wait_all(copies)

        start = pl.multiple_of(step * block, block)
        out[...] = (nt(weight[pl.ds(start, block), :], hid[...]) + bias_ref[...]).astype(BF)

    return call(
        kernel,
        (steps,),
        [full((rows, width)), full(vecs.shape), rows_of((block, 1))] + [ANYWHERE] * n,
        [full((rows, width)), rows_of((block, rows))],
        [jax.ShapeDtypeStruct((rows, width), BF), jax.ShapeDtypeStruct((3 * width, rows), BF)],
        [
            pltpu.VMEM((3 * width, width), BF),
            pltpu.VMEM((rows, width), BF),
            pltpu.SemaphoreType.DMA((n * pieces[0].shape[0],)),
        ],
        32,
        6 * rows * width * width,
        12 * MIB,
        (places, tokens, vecs, bias, *pieces),
        prefetch=1,
    )


QB = 128
KB = 256
PARTS = 2


def window_bias(seg_row, seg_col):
    return jnp.where(seg_col == seg_row, 0.0, NEG).astype(F32)


def shift_in(dst, src):
    count, rows = src.shape
    half = KB // 4
    zero = jnp.zeros((count, half), src.dtype)
    dst[...] = jnp.concatenate([zero, src, zero], axis=1)


def head_parts(width, rows, part):
    half = width // PARTS
    return [
        pl.BlockSpec((half, QB), lambda i, *unused: (part, i)),
        pl.BlockSpec((half, rows), lambda i, *unused: (PARTS + part, 0)),
        pl.BlockSpec((half, rows), lambda i, *unused: (2 * PARTS + part, 0)),
    ]


def attend(qkv_t, seg_row, seg_col, width, part, after=()):
    rows = qkv_t.shape[1]
    half = width // PARTS
    heads = half // HEAD_DIM

    def kernel(q_ref, k_ref, v_ref, seg_r, seg_c, o_ref, lse_ref, keys, values):
        step = pl.program_id(0)

        @pl.when(step == 0)
        def first():
            shift_in(keys, k_ref[...])
            shift_in(values, v_ref[...])

        start = pl.multiple_of(step * QB, QB)
        window = pl.ds(start, KB)
        bias = window_bias(seg_r[0:1, :], seg_c[window, :])
        ats = [slice(h * HEAD_DIM, (h + 1) * HEAD_DIM) for h in range(heads)]
        scores = [tn(keys[at, window], q_ref[at, :] * BF(HEAD_DIM**-0.5)) + bias for at in ats]
        tops = [jnp.max(s, axis=0, keepdims=True) for s in scores]
        expos = [jnp.exp(s - t) for s, t in zip(scores, tops)]
        sums = [jnp.sum(e, axis=0, keepdims=True) for e in expos]
        probs = [(e * (1.0 / s)).astype(BF) for e, s in zip(expos, sums)]
        for at, p in zip(ats, probs):
            o_ref[at, :] = nn(values[at, window], p).astype(BF)
        for h, (t, s) in enumerate(zip(tops, sums)):
            lse_ref[h : h + 1, :] = t + jnp.log(s)

    return call(
        kernel,
        (rows // QB,),
        head_parts(width, rows, part) + [lanes_of((8, QB)), full(seg_col.shape)],
        [lanes_of((half, QB)), lanes_of((16, QB))],
        [jax.ShapeDtypeStruct((half, rows), BF), jax.ShapeDtypeStruct((16, rows), F32)],
        [pltpu.VMEM((half, rows + QB), BF), pltpu.VMEM((half, rows + QB), BF)],
        40,
        4 * rows * KB * half * 4,
        8 * MIB,
        (qkv_t, qkv_t, qkv_t, seg_row, seg_col),
        after=after,
    )


def project_out(o_parts, tokens, vecs, pieces, places, rows_piece, after=()):
    rows, width = tokens.shape
    n, block = len(pieces), 256

    def kernel(at, o_a, o_b, tok, vec, *refs):
        parts, (mid_out, hid_out, weight, sem) = refs[:n], refs[n:]

        @pl.when(pl.program_id(0) == 0)
        def first():
            wait_all(load_pieces(at, parts, 0, rows_piece, weight, sem))

        both = jnp.concatenate([o_a[...], o_b[...]], axis=0)
        mid = tok[...].astype(F32) + tn(both, weight[...]) + vec[4:5, :]
        mid_out[...] = mid
        hat, unused = normed(mid)
        hid_out[...] = (hat * vec[5:6, :] + vec[6:7, :]).astype(BF)

    return call(
        kernel,
        (rows // block,),
        [lanes_of((width // PARTS, block))] * PARTS + [rows_of((block, width)), full(vecs.shape)] + [ANYWHERE] * n,
        [rows_of((block, width)), rows_of((block, width))],
        [jax.ShapeDtypeStruct((rows, width), F32), jax.ShapeDtypeStruct((rows, width), BF)],
        [pltpu.VMEM((width, width), BF), pltpu.SemaphoreType.DMA((n * pieces[0].shape[0],))],
        32,
        2 * rows * width * width,
        12 * MIB,
        (places, *o_parts, tokens, vecs, *pieces),
        prefetch=1,
        after=after,
    )


def mlp_half(hidden, cot, bias, pieces, places, low, unit_rows, group_rows, wide, after=()):
    rows, width = hidden.shape
    n, deep, lanes = len(pieces), pieces[0].shape[0], pieces[0].shape[2]
    units = 2 * wide * unit_rows
    block = min(384, units)

    def kernel(at, hid, cot_ref, bias_ref, *refs):
        parts = refs[:n]
        act_out, grad_out, sum_out, own, far, up, down, d_up, d_down, sem_a, sem_b = refs[n:]
        step = pl.program_id(0)

        @pl.when(step == 0)
        def first():
            one = load_pieces(at, parts, low, unit_rows, up, sem_a)
            two = load_pieces(at, parts, low + unit_rows, unit_rows, down, sem_b)
            wait_all(one)
            wait_all(two)

        here = pl.ds(pl.multiple_of(step * block, block), block)
        pre = nt(up[here, :], hid[...]) + bias_ref[...]
        grad_act = nt(down[here, :], cot_ref[...])
        cdf, pdf = cdf_pdf(pre)
        act = (pre * cdf).astype(BF)
        grad = (grad_act * (cdf + pre * pdf)).astype(BF)
        act_out[...] = act
        grad_out[...] = grad
        sum_out[...] = jnp.sum(grad.astype(F32), axis=1, keepdims=True)
        d_down[here, :] = nn(act, cot_ref[...]).astype(BF)
        d_up[here, :] = nn(grad, hid[...]).astype(BF)

        @pl.when(step == pl.num_programs(0) - 1)
        def last():
            one = store_pieces(at, d_up, unit_rows, own, far, 0, sem_a)
            two = store_pieces(at, d_down, unit_rows, own, far, unit_rows, sem_b)
            wait_all(one)
            wait_all(two)

    piece_shape = jax.ShapeDtypeStruct((n // 2, deep, group_rows, lanes), BF)
    return call(
        kernel,
        (units // block,),
        [full((rows, width)), full((rows, width)), rows_of((block, 1))] + [ANYWHERE] * n,
        [rows_of((block, rows)), rows_of((block, rows)), rows_of((block, 1)), ANYWHERE, ANYWHERE],
        [
            jax.ShapeDtypeStruct((units, rows), BF),
            jax.ShapeDtypeStruct((units, rows), BF),
            jax.ShapeDtypeStruct((units, 1), F32),
            piece_shape,
            piece_shape,
        ],
        [pltpu.VMEM((units, width), BF)] * 4
        + [pltpu.SemaphoreType.DMA((n * deep,))] * 2,
        48,
        8 * rows * units * width,
        16 * MIB,
        (places, hidden, cot, bias, *pieces),
        prefetch=1,
        after=after,
    )


def second_norm_back(grads, mid, cot, vecs, groups, places, unit_rows, wide, after=()):
    rows, width = mid.shape
    block = 256
    n, deep = len(groups[0][0]), groups[0][0][0].shape[0]
    units = 2 * wide * unit_rows

    def kernel(at, ga, gb, mid_ref, cot_ref, vec, *refs):
        parts = refs[: 2 * n]
        out, low_out, sums, up_a, up_b, sem = refs[2 * n :]
        step = pl.program_id(0)

        @pl.when(step == 0)
        def first():
            one = load_pieces(at, parts[:n], groups[0][1], unit_rows, up_a, sem.at[0])
            two = load_pieces(at, parts[n:], groups[1][1], unit_rows, up_b, sem.at[1])
            wait_all(one)
            wait_all(two)
            sums[...] = jnp.zeros_like(sums)

        grad = tn(ga[...], up_a[...]) + tn(gb[...], up_b[...])
        hat, inverse = normed(mid_ref[...])
        top = cot_ref[...].astype(F32)
        total_grad = top + norm_back(grad, hat, inverse, vec[5:6, :])
        out[...] = total_grad
        lower = total_grad.astype(BF)
        low_out[...] = lower
        sums[0:1, :] += jnp.sum(grad * hat, axis=0, keepdims=True)
        sums[1:2, :] += jnp.sum(grad, axis=0, keepdims=True)
        sums[2:3, :] += jnp.sum(lower.astype(F32), axis=0, keepdims=True)
        sums[3:4, :] += jnp.sum(top, axis=0, keepdims=True)

    return call(
        kernel,
        (rows // block,),
        [lanes_of((units, block)), lanes_of((units, block)), rows_of((block, width)), rows_of((block, width)), full(vecs.shape)]
        + [ANYWHERE] * (2 * n),
        [rows_of((block, width)), rows_of((block, width)), full((8, width))],
        [
            jax.ShapeDtypeStruct((rows, width), F32),
            jax.ShapeDtypeStruct((rows, width), BF),
            jax.ShapeDtypeStruct((8, width), F32),
        ],
        [pltpu.VMEM((units, width), BF)] * 2 + [pltpu.SemaphoreType.DMA((2, n * deep))],
        48,
        4 * rows * units * width,
        20 * MIB,
        (places, *grads, mid, cot, vecs, *groups[0][0], *groups[1][0]),
        prefetch=1,
        after=after,
    )


def out_back(o_parts, grad_low, pieces, places, rows_piece, own, far, low, after=()):
    rows, width = grad_low.shape
    half = width // PARTS
    n, deep = len(pieces), pieces[0].shape[0]

    def kernel(at, o_a, o_b, grad, own_in, far_in, *refs):
        parts, (do_ref, own_ref, far_ref, weight, d_weight, sem) = refs[:n], refs[n:]
        copies = load_pieces(at, parts, 0, rows_piece, weight, sem)
        d_weight[:half, :] = nn(o_a[...], grad[...]).astype(BF)
        d_weight[half:, :] = nn(o_b[...], grad[...]).astype(BF)
        wait_all(copies)
        copies = store_pieces(at, d_weight, rows_piece, own_ref, far_ref, low, sem)
        do_ref[...] = nt(weight[...], grad[...]).astype(BF)
        wait_all(copies)

    return call(
        kernel,
        (1,),
        [full((half, rows))] * PARTS + [full((rows, width)), ANYWHERE, ANYWHERE] + [ANYWHERE] * n,
        [full((width, rows)), ANYWHERE, ANYWHERE],
        [
            jax.ShapeDtypeStruct((width, rows), BF),
            jax.ShapeDtypeStruct(own.shape, BF),
            jax.ShapeDtypeStruct(far.shape, BF),
        ],
        [pltpu.VMEM((width, width), BF)] * 2 + [pltpu.SemaphoreType.DMA((n * deep,))],
        32,
        4 * rows * width * width,
        8 * MIB,
        (places, *o_parts, grad_low, own, far, *pieces),
        prefetch=1,
        aliases={4: 1, 5: 2},
        after=after,
    )


def attend_back(qkv_t, do_t, lse, seg_row, seg_col, width, part, after=()):
    rows = qkv_t.shape[1]
    half = width // PARTS
    heads = half // HEAD_DIM
    scale = HEAD_DIM**-0.5

    def kernel(q_ref, k_ref, v_ref, do_ref, lse_ref, seg_r, seg_c, out, sums, keys, values, d_keys, d_values):
        step = pl.program_id(0)

        @pl.when(step == 0)
        def first():
            shift_in(keys, k_ref[...])
            shift_in(values, v_ref[...])
            d_keys[...] = jnp.zeros_like(d_keys)
            d_values[...] = jnp.zeros_like(d_values)

        start = pl.multiple_of(step * QB, QB)
        window = pl.ds(start, KB)
        bias = window_bias(seg_r[0:1, :], seg_c[window, :])
        ats = [slice(h * HEAD_DIM, (h + 1) * HEAD_DIM) for h in range(heads)]
        queries = [q_ref[at, :] * BF(scale) for at in ats]
        raw = [tn(keys[at, window], q) for at, q in zip(ats, queries)]
        grad_probs = [tn(values[at, window], do_ref[at, :]) for at in ats]
        probs = [jnp.exp(r + (bias - lse_ref[h : h + 1, :])) for h, r in enumerate(raw)]
        weighted = [p * g for p, g in zip(probs, grad_probs)]
        deltas = [jnp.sum(w, axis=0, keepdims=True) for w in weighted]
        scores = [(w - p * d).astype(BF) for w, p, d in zip(weighted, probs, deltas)]
        for at, s in zip(ats, scores):
            out[at, pl.ds(start, QB)] = (nn(keys[at, window], s) * scale).astype(BF)
        for at, q, s in zip(ats, queries, scores):
            d_keys[at, window] += nt(q, s)
        for at, p in zip(ats, probs):
            d_values[at, window] += nt(do_ref[at, :], p.astype(BF))

        @pl.when(step == pl.num_programs(0) - 1)
        def last():
            edge = KB // 4
            out[half : 2 * half, :] = d_keys[...][:, edge : edge + rows].astype(BF)
            out[2 * half : 3 * half, :] = d_values[...][:, edge : edge + rows].astype(BF)
            sums[...] = jnp.sum(out[...].astype(F32), axis=1, keepdims=True)

    return call(
        kernel,
        (rows // QB,),
        head_parts(width, rows, part)
        + [
            pl.BlockSpec((half, QB), lambda i, *unused: (part, i)),
            lanes_of((16, QB)),
            lanes_of((8, QB)),
            full(seg_col.shape),
        ],
        [full((3 * half, rows)), full((3 * half, 1))],
        [jax.ShapeDtypeStruct((3 * half, rows), BF), jax.ShapeDtypeStruct((3 * half, 1), F32)],
        [pltpu.VMEM((half, rows + QB), BF)] * 2 + [pltpu.VMEM((half, rows + QB), F32)] * 2,
        48,
        10 * rows * KB * half * 4,
        16 * MIB,
        (qkv_t, qkv_t, qkv_t, do_t, lse, seg_row, seg_col),
        after=after,
    )


def qkv_back(grad_parts, hidden, places, rows_piece, topo, after=()):
    rows, width = hidden.shape
    half = width // PARTS
    count = 3 * width
    sites, lanes = topo.X * topo.X, width // topo.Y

    def kernel(at, grad_a, grad_b, hid, own, far, whole, sem):
        step = pl.program_id(0)
        for part, grad in enumerate((grad_a, grad_b)):
            here = pl.ds(pl.multiple_of(step * width + part * half, half), half)
            whole[here, :] = nn(grad[...], hid[...]).astype(BF)

        @pl.when(step == pl.num_programs(0) - 1)
        def last():
            wait_all(store_pieces(at, whole, rows_piece, own, far, 0, sem))

    piece_shape = jax.ShapeDtypeStruct((sites, topo.Z, rows_piece, lanes), BF)
    return call(
        kernel,
        (3,),
        [rows_of((half, rows))] * PARTS + [full((rows, width))],
        [ANYWHERE, ANYWHERE],
        [piece_shape, piece_shape],
        [pltpu.VMEM((count, width), BF), pltpu.SemaphoreType.DMA((2 * sites * topo.Z,))],
        32,
        2 * rows * count * width,
        12 * MIB,
        (places, *grad_parts, hidden),
        prefetch=1,
        after=after,
    )


def first_norm_back(grad_parts, tokens, grad_mid, vecs, pieces, places, rows_piece, after=()):
    rows, width = tokens.shape
    count, half = 3 * width, width // PARTS
    block = 256
    n = len(pieces)

    def kernel(at, grad_a, grad_b, tok, mid, vec, *refs):
        parts, (out, sums, weight, sem) = refs[:n], refs[n:]

        @pl.when(pl.program_id(0) == 0)
        def first():
            wait_all(load_pieces(at, parts, 0, rows_piece, weight, sem))
            sums[...] = jnp.zeros_like(sums)

        both = jnp.concatenate([g[k * half : (k + 1) * half, :] for k in range(3) for g in (grad_a, grad_b)], axis=0)
        grad = tn(both, weight[...])
        hat, inverse = normed(tok[...].astype(F32))
        out[...] = (mid[...] + norm_back(grad, hat, inverse, vec[0:1, :])).astype(BF)
        sums[0:1, :] += jnp.sum(grad * hat, axis=0, keepdims=True)
        sums[1:2, :] += jnp.sum(grad, axis=0, keepdims=True)

    return call(
        kernel,
        (rows // block,),
        [lanes_of((count // PARTS, block))] * PARTS
        + [rows_of((block, width)), rows_of((block, width)), full(vecs.shape)]
        + [ANYWHERE] * n,
        [rows_of((block, width)), full((8, width))],
        [jax.ShapeDtypeStruct((rows, width), BF), jax.ShapeDtypeStruct((8, width), F32)],
        [pltpu.VMEM((count, width), BF), pltpu.SemaphoreType.DMA((n * pieces[0].shape[0],))],
        40,
        2 * rows * count * width,
        16 * MIB,
        (places, *grad_parts, tokens, grad_mid, vecs, *pieces),
        prefetch=1,
        after=after,
    )


def finish_out(acts, mid, vecs, groups, places, unit_rows, wide, after=()):
    rows, width = mid.shape
    block = 256
    n, deep = len(groups[0][0]), groups[0][0][0].shape[0]
    units = 2 * wide * unit_rows

    def kernel(at, act_a, act_b, mid_ref, vec, *refs):
        parts = refs[: 2 * n]
        out, down_a, down_b, sem = refs[2 * n :]

        @pl.when(pl.program_id(0) == 0)
        def first():
            one = load_pieces(at, parts[:n], groups[0][1], unit_rows, down_a, sem.at[0])
            two = load_pieces(at, parts[n:], groups[1][1], unit_rows, down_b, sem.at[1])
            wait_all(one)
            wait_all(two)

        result = tn(act_a[...], down_a[...]) + tn(act_b[...], down_b[...])
        out[...] = (mid_ref[...] + result + vec[7:8, :]).astype(BF)

    return call(
        kernel,
        (rows // block,),
        [lanes_of((units, block)), lanes_of((units, block)), rows_of((block, width)), full(vecs.shape)]
        + [ANYWHERE] * (2 * n),
        rows_of((block, width)),
        jax.ShapeDtypeStruct((rows, width), BF),
        [pltpu.VMEM((units, width), BF)] * 2 + [pltpu.SemaphoreType.DMA((2, n * deep))],
        48,
        4 * rows * units * width,
        16 * MIB,
        (places, *acts, mid, vecs, *groups[0][0], *groups[1][0]),
        prefetch=1,
        after=after,
    )


def total(first, *rest):
    result = first.astype(F32)
    for other in rest:
        result = result + other.astype(F32)
    return result


class Chain:
    def __init__(self, own, far, topo):
        self.topo, self.held = topo, own
        self.coming = [send(far, topo.cp)]

    def arrived(self):
        return tuple(self.coming)

    def fold(self):
        return total(self.held, *self.coming)

    def across(self):
        topo, side = self.topo, self.topo.X
        own = self.fold().astype(BF).reshape(side, side, *self.held.shape[1:])
        self.held = own[0]
        self.coming = [send(own[k], topo.bp[side - k]) for k in range(1, side)]

    def along(self):
        topo, side = self.topo, self.topo.X
        line = self.fold().astype(BF)
        self.held = line[0]
        self.coming = [send(line[k], topo.ap[side - k]) for k in range(1, side)]

    def down(self):
        topo, deep = self.topo, self.topo.Z
        stack = self.fold().astype(BF)
        self.held = stack[0]
        self.coming = [send(stack[k], topo.zp[deep - k]) for k in range(1, deep)]

    def result(self):
        return self.fold()


def scatter(own, far, topo):
    chain = Chain(own, far, topo)
    chain.across()
    chain.along()
    chain.down()
    return chain.result()


def tail_rows(values, rows, lanes):
    return jnp.pad(values[None], ((0, rows - 1), (0, lanes - values.shape[0])))


def vector_slots(places, topo):
    slot = places[:, 0] * topo.narrow + places[:, 1] * 2 + places[:, 2]
    return (slot[:, None] == jnp.arange(topo.wide * topo.narrow)[None]).astype(BF)


def fits(topo, rows, width, hidden):
    lanes = 2 * width // topo.narrow
    return (
        lanes % 128 == 0
        and rows % 256 == 0
        and (width // topo.wide) % 32 == 0
        and (hidden // topo.wide) % 64 == 0
        and 2 * P_THREE == QB
    )


def fast_device(
    tokens, qkv_weight, out_weight, up_weight, down_weight, vectors, bucket_counts, cotangent, topo
):
    rows, width = tokens.shape
    wide = topo.wide
    places = topo.origins()
    core = topo.here()[3]
    shards = [qkv_weight.astype(BF).T, out_weight.astype(BF), up_weight.astype(BF).T, down_weight.astype(BF)]
    r_qkv, r_out, r_unit = shards[0].shape[0] // 2, shards[1].shape[0] // 2, shards[2].shape[0] // 4
    first = pair_up(shards[0], topo, core)
    rest = pair_up(
        jnp.concatenate([pick_half(s, 0, h) for h in range(2) for s in shards[1:]], axis=0), topo, core
    )
    lanes = first.shape[1]
    low_vec = vectors.astype(BF)
    out_end, up_end = r_out, r_out + 2 * r_unit
    one = gather(jnp.concatenate([first, tail_rows(low_vec, 16, lanes)], axis=0), topo)
    two = gather(
        jnp.concatenate([rest[: out_end + r_unit], rest[up_end : up_end + r_unit]], axis=0), topo
    )
    three = gather(
        jnp.concatenate([rest[out_end + r_unit : up_end], rest[up_end + r_unit :]], axis=0), topo
    )
    slots = vector_slots(places, topo)
    vecs, bias_qkv, *bias_up = unpack_vectors(one, places, r_qkv, vectors.shape[0], width, wide, topo.narrow)
    segment = image_ids(bucket_counts[0], rows)
    seg_row = jnp.broadcast_to(segment[None], (8, rows))
    seg_col = jnp.pad(segment, (QB // 2, QB // 2), constant_values=-1)[:, None]

    hidden_one, qkv_t = project_qkv(tokens, vecs, bias_qkv, one, places, (r_qkv, wide))
    attn = [attend(qkv_t, seg_row, seg_col, width, part) for part in range(PARTS)]
    attn_t, lse = [a[0] for a in attn], [a[1] for a in attn]
    mid, hidden_two = project_out(attn_t, tokens, vecs, two, places, r_out)
    act_a, grad_a, sum_a, own_a, far_a = mlp_half(
        hidden_two, cotangent, bias_up[0], two, places, r_out, r_unit, 2 * r_unit, wide
    )
    chain_a = Chain(own_a, far_a, topo)
    act_b, grad_b, sum_b, own_b, far_b = mlp_half(
        hidden_two, cotangent, bias_up[1], three, places, 0, r_unit, 2 * r_unit + r_out, wide
    )
    grad_mid, grad_mid_low, sums_two = second_norm_back(
        (grad_a, grad_b), mid, cotangent, vecs, ((two, r_out), (three, 0)), places, r_unit, wide,
        after=chain_a.arrived(),
    )
    chain_a.across()
    do_t, own_b, far_b = out_back(attn_t, grad_mid_low, two, places, r_out, own_b, far_b, 2 * r_unit)
    chain_b = Chain(own_b, far_b, topo)
    grads_0, sums_0 = attend_back(
        qkv_t, do_t, lse[0], seg_row, seg_col, width, 0, after=chain_a.arrived()
    )
    chain_a.along()
    grads_1, sums_1 = attend_back(
        qkv_t, do_t, lse[1], seg_row, seg_col, width, 1, after=chain_a.arrived() + chain_b.arrived()
    )
    chain_a.down()
    chain_b.across()
    grad_t = (grads_0, grads_1)
    own_q, far_q = qkv_back(
        grad_t, hidden_one, places, r_qkv, topo, after=chain_b.arrived()
    )
    chain_q = Chain(own_q, far_q, topo)
    chain_b.along()
    input_grad, sums_one = first_norm_back(
        grad_t, tokens, grad_mid, vecs, one, places, r_qkv, after=chain_a.arrived() + chain_q.arrived()
    )
    chain_q.across()
    block_out = finish_out(
        (act_a, act_b), mid, vecs, ((two, r_out + r_unit), (three, r_unit)), places, r_unit, wide,
        after=chain_b.arrived(),
    )
    chain_b.down()
    chain_q.along()
    chain_q.down()
    half = width // PARTS
    sums_qkv = [[s[k * half : (k + 1) * half, 0] for s in (sums_0, sums_1)] for k in (0, 2)]
    sums_up = jnp.stack([s.reshape(2 * wide, r_unit) for s in (sum_a, sum_b)], axis=1).reshape(-1)
    d_vector = jnp.concatenate(
        [
            sums_one[0],
            sums_one[1],
            *sums_qkv[0],
            *sums_qkv[1],
            sums_two[2],
            sums_two[0],
            sums_two[1],
            sums_two[3],
            sums_up,
        ]
    )
    part_a, part_b, part_q = chain_a.result(), chain_b.result(), chain_q.result()
    rel = jnp.dot(slots, d_vector.astype(BF).reshape(slots.shape[1], -1), preferred_element_type=F32).astype(BF)
    rel = jnp.pad(rel, ((0, 0), (0, lanes - rel.shape[1]))).reshape(2, topo.X * topo.X, topo.Z, 1, lanes)
    vector_grad = scatter(rel[0], rel[1], topo)[0, : vectors.shape[0]]
    down = jnp.concatenate([part_a[r_unit:], part_b[r_unit : 2 * r_unit]], axis=0)
    up = jnp.concatenate([part_a[:r_unit], part_b[:r_unit]], axis=0)
    out = part_b[2 * r_unit :]
    grads = [unpair(g, topo, core) for g in (part_q, out, up, down)]
    return (block_out, input_grad, grads[0].T, grads[1], grads[2].T, grads[3], vector_grad)


def per_device(
    tokens, qkv_weight, out_weight, up_weight, down_weight, vectors, bucket_counts, cotangent
):
    topo = Topo(lax.axis_size("wide"), lax.axis_size("narrow"))
    operands = (tokens, qkv_weight, out_weight, up_weight, down_weight, vectors, bucket_counts, cotangent)
    if fits(topo, *tokens.shape, up_weight.shape[1] * topo.wide):
        return fast_device(*operands, topo)
    return plain_device(*operands)


def plain_device(
    tokens, qkv_weight, out_weight, up_weight, down_weight, vectors, bucket_counts, cotangent
):
    rows, width = tokens.shape
    halves = (
        lax.all_gather(qkv_weight.astype(jnp.bfloat16), "narrow", axis=0, tiled=True),
        lax.all_gather(out_weight.astype(jnp.bfloat16), "narrow", axis=1, tiled=True),
        lax.all_gather(up_weight.astype(jnp.bfloat16), "narrow", axis=0, tiled=True),
        lax.all_gather(down_weight.astype(jnp.bfloat16), "narrow", axis=1, tiled=True),
        lax.all_gather(vectors.astype(jnp.bfloat16), "narrow", axis=0, tiled=True),
    )
    wholes = (
        lax.all_gather(halves[0], "wide", axis=1, tiled=True),
        lax.all_gather(halves[1], "wide", axis=0, tiled=True),
        lax.all_gather(halves[2], "wide", axis=1, tiled=True),
        lax.all_gather(halves[3], "wide", axis=0, tiled=True),
        lax.all_gather(halves[4], "wide", axis=0, tiled=True),
    )
    qkv_full, out_full, up_full, down_full, packed = wholes
    params = packed.astype(jnp.float32)
    gain_one = params[0:width]
    shift_one = params[width : 2 * width]
    bias_query = params[2 * width : 3 * width]
    bias_value = params[3 * width : 4 * width]
    bias_out = params[4 * width : 5 * width]
    gain_two = params[5 * width : 6 * width]
    shift_two = params[6 * width : 7 * width]
    bias_down = params[7 * width : 8 * width]
    bias_up = params[8 * width :]
    inputs = tokens.astype(jnp.float32)
    hidden_one = layer_norm(inputs, gain_one, shift_one).astype(jnp.bfloat16)
    qkv_bias = jnp.concatenate([bias_query, jnp.zeros((width,), jnp.float32), bias_value])
    qkv_all = (jnp.dot(hidden_one, qkv_full, preferred_element_type=jnp.float32) + qkv_bias).astype(
        jnp.bfloat16
    )
    margin = P_THREE
    blocks = rows // QROWS
    span = QROWS + 2 * margin
    scale = HEAD_DIM ** (-0.5)
    query_blk = qkv_all[:, :width].reshape(blocks, QROWS, HEADS, HEAD_DIM)
    keys_win = windows_of(qkv_all[:, width : 2 * width], margin, blocks, 0).reshape(
        blocks, span, HEADS, HEAD_DIM
    )
    values_win = windows_of(qkv_all[:, 2 * width :], margin, blocks, 0).reshape(
        blocks, span, HEADS, HEAD_DIM
    )
    segment = image_ids(bucket_counts[0], rows)
    seg_rows = segment.reshape(blocks, QROWS)
    seg_cols = windows_of(segment, margin, blocks, -1)
    same = seg_rows[:, None, :, None] == seg_cols[:, None, None, :]
    raw = (
        jnp.einsum("bqhd,bkhd->bhqk", query_blk, keys_win, preferred_element_type=jnp.float32)
        * scale
    )
    masked = jnp.where(same, raw, NEG)
    top = jnp.max(masked, axis=3, keepdims=True)
    expo = jnp.exp(masked - top)
    total = jnp.sum(expo, axis=3, keepdims=True)
    probs_low = (expo / total).astype(jnp.bfloat16)
    log_total = top + jnp.log(total)
    attended = jnp.einsum(
        "bhqk,bkhd->bqhd", probs_low, values_win, preferred_element_type=jnp.float32
    )
    attn_low = attended.reshape(rows, width).astype(jnp.bfloat16)
    mid = inputs + jnp.dot(attn_low, out_full, preferred_element_type=jnp.float32) + bias_out
    hidden_two = layer_norm(mid, gain_two, shift_two).astype(jnp.bfloat16)
    pre_act = jnp.dot(hidden_two, up_full, preferred_element_type=jnp.float32) + bias_up
    activated = gelu_exact(pre_act).astype(jnp.bfloat16)
    output = mid + jnp.dot(activated, down_full, preferred_element_type=jnp.float32) + bias_down
    block_out = output.astype(jnp.bfloat16)
    grad_top = cotangent.astype(jnp.float32)
    d_down = contract_rows(activated, cotangent)
    d_bias_down = jnp.sum(grad_top, axis=0)
    grad_act = contract_cols(cotangent, down_full)
    unused_act, gelu_back = jax.vjp(gelu_exact, pre_act)
    grad_pre = gelu_back(grad_act)[0].astype(jnp.bfloat16)
    d_up = contract_rows(hidden_two, grad_pre)
    d_bias_up = jnp.sum(grad_pre.astype(jnp.float32), axis=0)
    grad_hidden_two = contract_cols(grad_pre, up_full)
    unused_two, norm_back_two = jax.vjp(layer_norm, mid, gain_two, shift_two)
    grad_mid_part, d_gain_two, d_shift_two = norm_back_two(grad_hidden_two)
    grad_mid = grad_top + grad_mid_part
    grad_mid_low = grad_mid.astype(jnp.bfloat16)
    d_out = contract_rows(attn_low, grad_mid_low)
    d_bias_out = jnp.sum(grad_mid_low.astype(jnp.float32), axis=0)
    grad_attn = contract_cols(grad_mid_low, out_full).astype(jnp.bfloat16)
    raw_again = (
        jnp.einsum("bqhd,bkhd->bhqk", query_blk, keys_win, preferred_element_type=jnp.float32)
        * scale
    )
    probs = jnp.exp(jnp.where(same, raw_again, NEG) - log_total)
    grad_blk = grad_attn.reshape(blocks, QROWS, HEADS, HEAD_DIM)
    grad_probs = jnp.einsum(
        "bqhd,bkhd->bhqk", grad_blk, values_win, preferred_element_type=jnp.float32
    )
    grad_scores = (
        probs * (grad_probs - jnp.sum(probs * grad_probs, axis=3, keepdims=True))
    ).astype(jnp.bfloat16)
    grad_query = (
        jnp.einsum("bhqk,bkhd->bqhd", grad_scores, keys_win, preferred_element_type=jnp.float32)
        * scale
    )
    grad_keys_win = (
        jnp.einsum("bhqk,bqhd->bkhd", grad_scores, query_blk, preferred_element_type=jnp.float32)
        * scale
    )
    grad_values_win = jnp.einsum(
        "bhqk,bqhd->bkhd", probs.astype(jnp.bfloat16), grad_blk, preferred_element_type=jnp.float32
    )
    grad_keys = fold_windows(grad_keys_win.reshape(blocks, span, width), margin, QROWS)
    grad_values = fold_windows(grad_values_win.reshape(blocks, span, width), margin, QROWS)
    grad_qkv = jnp.concatenate(
        [grad_query.reshape(rows, width), grad_keys, grad_values], axis=1
    ).astype(jnp.bfloat16)
    d_qkv = contract_rows(hidden_one, grad_qkv)
    column_sums = jnp.sum(grad_qkv.astype(jnp.float32), axis=0)
    grad_hidden_one = contract_cols(grad_qkv, qkv_full)
    unused_one, norm_back_one = jax.vjp(layer_norm, inputs, gain_one, shift_one)
    grad_in_part, d_gain_one, d_shift_one = norm_back_one(grad_hidden_one)
    input_grad = (grad_mid + grad_in_part).astype(jnp.bfloat16)
    d_vector = jnp.concatenate(
        [
            d_gain_one,
            d_shift_one,
            column_sums[:width],
            column_sums[2 * width :],
            d_bias_out,
            d_gain_two,
            d_shift_two,
            d_bias_down,
            d_bias_up,
        ]
    )
    partial_sums = (
        lax.psum_scatter(
            d_qkv.astype(jnp.bfloat16), "wide", scatter_dimension=1, tiled=True
        ).astype(jnp.float32),
        lax.psum_scatter(
            d_out.astype(jnp.bfloat16), "wide", scatter_dimension=0, tiled=True
        ).astype(jnp.float32),
        lax.psum_scatter(d_up.astype(jnp.bfloat16), "wide", scatter_dimension=1, tiled=True).astype(
            jnp.float32
        ),
        lax.psum_scatter(
            d_down.astype(jnp.bfloat16), "wide", scatter_dimension=0, tiled=True
        ).astype(jnp.float32),
        lax.psum_scatter(
            d_vector.astype(jnp.bfloat16), "wide", scatter_dimension=0, tiled=True
        ).astype(jnp.float32),
    )
    final = (
        lax.psum_scatter(
            partial_sums[0].astype(jnp.bfloat16), "narrow", scatter_dimension=0, tiled=True
        ).astype(jnp.float32),
        lax.psum_scatter(
            partial_sums[1].astype(jnp.bfloat16), "narrow", scatter_dimension=1, tiled=True
        ).astype(jnp.float32),
        lax.psum_scatter(
            partial_sums[2].astype(jnp.bfloat16), "narrow", scatter_dimension=0, tiled=True
        ).astype(jnp.float32),
        lax.psum_scatter(
            partial_sums[3].astype(jnp.bfloat16), "narrow", scatter_dimension=1, tiled=True
        ).astype(jnp.float32),
        lax.psum_scatter(
            partial_sums[4].astype(jnp.bfloat16), "narrow", scatter_dimension=0, tiled=True
        ).astype(jnp.float32),
    )
    return (block_out, input_grad, final[0], final[1], final[2], final[3], final[4])


def solution(mesh):
    return jax.shard_map(
        per_device,
        mesh=mesh,
        in_specs=(
            P(("wide", "narrow"), None),
            P("narrow", "wide"),
            P("wide", "narrow"),
            P("narrow", "wide"),
            P("wide", "narrow"),
            P(("wide", "narrow")),
            P(("wide", "narrow"), None),
            P(("wide", "narrow"), None),
        ),
        out_specs=(
            P(("wide", "narrow"), None),
            P(("wide", "narrow"), None),
            P("narrow", "wide"),
            P("wide", "narrow"),
            P("narrow", "wide"),
            P("wide", "narrow"),
            P(("wide", "narrow")),
        ),
        check_vma=False,
    )
```

```python
import jax
import jax.numpy as jnp
from jax import lax
from jax.experimental import pallas as pl
from jax.experimental.pallas import tpu as pltpu
from jax.sharding import PartitionSpec as P

HEADS = 12
HEAD_DIM = 64
QROWS = 512
P_ONE = 25
P_TWO = 49
P_THREE = 64


EPS = 1e-06
NEG = -1e30


def layer_norm(values, gain, shift):
    center = values - jnp.mean(values, axis=-1, keepdims=True)
    spread = jnp.mean(center * center, axis=-1, keepdims=True)
    return center * lax.rsqrt(spread + EPS) * gain + shift


def image_ids(counts, rows):
    place = jnp.arange(rows, dtype=jnp.int32)
    first = counts[0] * P_ONE
    second = first + counts[1] * P_TWO
    bucket = (place >= first).astype(jnp.int32) + (place >= second).astype(jnp.int32)
    start = jnp.where(bucket == 0, 0, jnp.where(bucket == 1, first, second))
    length = jnp.where(bucket == 0, P_ONE, jnp.where(bucket == 1, P_TWO, P_THREE)).astype(jnp.int32)
    return bucket * rows + (place - start) // length


def gelu_exact(values):
    return jax.nn.gelu(values, approximate=False)


def contract_rows(left, right):
    return lax.dot_general(
        left, right, (((0,), (0,)), ((), ())), preferred_element_type=jnp.float32
    )


def contract_cols(left, right):
    return lax.dot_general(
        left, right, (((1,), (1,)), ((), ())), preferred_element_type=jnp.float32
    )


def windows_of(values, margin, blocks, fill):
    rows = values.shape[0]
    block_rows = rows // blocks
    rest = values.shape[1:]
    padded = jnp.pad(
        values, ((margin, margin),) + tuple(((0, 0) for unused in rest)), constant_values=fill
    )
    before = padded[:rows].reshape((blocks, block_rows) + rest)[:, :margin]
    middle = values.reshape((blocks, block_rows) + rest)
    after = padded[2 * margin : 2 * margin + rows].reshape((blocks, block_rows) + rest)[
        :, block_rows - margin :
    ]
    return jnp.concatenate([before, middle, after], axis=1)


def fold_windows(grads, margin, block_rows):
    blocks = grads.shape[0]
    width = grads.shape[2]
    middle = grads[:, margin : margin + block_rows]
    before = jnp.pad(grads[1:, :margin], ((0, 1), (block_rows - margin, 0), (0, 0)))
    after = jnp.pad(grads[:-1, margin + block_rows :], ((1, 0), (0, block_rows - margin), (0, 0)))
    return (middle + before + after).reshape(blocks * block_rows, width)


BF = jnp.bfloat16
F32 = jnp.float32
AXES = ("wide", "narrow")


class Topo:
    def __init__(self, wide, narrow):
        self.wide, self.narrow = wide, narrow
        self.Y = narrow // 2
        self.X = self.Y
        self.Z = wide // self.X
        side, deep = self.X, self.Z
        self.zp = [self.perm(lambda z, x, y, c, k=k: ((z + k) % deep, x, y, c)) for k in range(deep)]
        self.ap = [
            self.perm(
                lambda z, x, y, c, k=k: (z, (x + k) % side, y, c) if c == 0 else (z, x, (y + k) % side, c)
            )
            for k in range(side)
        ]
        self.bp = [
            self.perm(
                lambda z, x, y, c, k=k: (z, x, (y + k) % side, c) if c == 0 else (z, (x + k) % side, y, c)
            )
            for k in range(side)
        ]
        self.cp = self.perm(lambda z, x, y, c: (z, x, y, 1 - c))

    def did(self, z, x, y, c):
        return ((z * self.X + x) * self.Y + y) * 2 + c

    def perm(self, target):
        return [
            (self.did(z, x, y, c), self.did(*target(z, x, y, c)))
            for z in range(self.Z)
            for x in range(self.X)
            for y in range(self.Y)
            for c in range(2)
        ]

    def here(self):
        wide, narrow = lax.axis_index("wide"), lax.axis_index("narrow")
        return wide // self.X, wide % self.X, narrow // 2, narrow % 2

    def origins(self):
        z0, x0, y0, c0 = self.here()
        side, deep = self.X, self.Z
        index = jnp.arange(2 * side * side * deep, dtype=jnp.int32)
        kz, ka, kb = index % deep, index // deep % side, index // (deep * side) % side
        c = (c0 + index // (deep * side * side)) % 2
        x = (x0 + side - jnp.where(c == 0, ka, kb)) % side
        y = (y0 + side - jnp.where(c == 0, kb, ka)) % side
        z = (z0 + deep - kz) % deep
        return jnp.stack([z * side + x, y, c], axis=1).astype(jnp.int32)


def send(values, perm):
    return lax.ppermute(values, AXES, perm)


def pick_half(values, axis, index):
    half = values.shape[axis] // 2
    return lax.dynamic_slice_in_dim(values, index * half, half, axis)


def pair_up(shard, topo, core):
    mine = pick_half(shard, 0, core)
    other = send(pick_half(shard, 0, 1 - core), topo.cp)
    first = jnp.where(core == 0, mine, other)
    second = jnp.where(core == 0, other, mine)
    return jnp.concatenate([first, second], axis=1)


def unpair(piece, topo, core):
    mine = pick_half(piece, 1, core)
    other = send(pick_half(piece, 1, 1 - core), topo.cp)
    first = jnp.where(core == 0, mine, other)
    second = jnp.where(core == 0, other, mine)
    return jnp.concatenate([first, second], axis=0)


def gather(piece, topo):
    stack = jnp.stack([piece] + [send(piece, topo.zp[k]) for k in range(1, topo.Z)])
    line = [stack] + [send(stack, topo.ap[k]) for k in range(1, topo.X)]
    own = [p for k in range(topo.X) for p in (line if k == 0 else [send(q, topo.bp[k]) for q in line])]
    return own + [send(p, topo.cp) for p in own]


def nn(a, b):
    return lax.dot_general(a, b, (((1,), (0,)), ((), ())), preferred_element_type=F32)


def nt(a, b):
    return lax.dot_general(a, b, (((1,), (1,)), ((), ())), preferred_element_type=F32)


def tn(a, b):
    return lax.dot_general(a, b, (((0,), (0,)), ((), ())), preferred_element_type=F32)


def normed(values):
    center = values - jnp.mean(values, axis=-1, keepdims=True)
    spread = jnp.mean(center * center, axis=-1, keepdims=True)
    inverse = lax.rsqrt(spread + EPS)
    return center * inverse, inverse


def norm_back(grad, hat, inverse, gain):
    scaled = grad * gain
    first = jnp.mean(scaled, axis=-1, keepdims=True)
    second = jnp.mean(scaled * hat, axis=-1, keepdims=True)
    return inverse * (scaled - first - hat * second)


ROOT_HALF = 0.7071067811865476
ROOT_TAU = 0.3989422804014327
MIB = 1024 * 1024
SCALE = 1.0
BACK = 3


def cdf_pdf(u):
    bell = jnp.exp(-0.5 * (u * u))
    t = 1.0 / (1.0 + (0.3275911 * ROOT_HALF) * jnp.abs(u))
    poly = 1.061405429 * 0.5
    for coef in (-1.453152027, 1.421413741, -0.284496736, 0.254829592):
        poly = poly * t + coef * 0.5
    upper = poly * t * bell
    return jnp.where(u < 0, upper, 1.0 - upper), ROOT_TAU * bell


def call(kernel, grid, in_specs, out_specs, out_shape, scratch, vmem, us, operands, prefetch=0, aliases=None, after=()):
    first, count = len(operands), len(after)

    def body(*refs):
        kernel(*refs[:first], *refs[first + count :])

    return pl.pallas_call(
        body,
        grid_spec=pltpu.PrefetchScalarGridSpec(
            num_scalar_prefetch=prefetch,
            grid=grid,
            in_specs=in_specs + [ANYWHERE] * count,
            out_specs=out_specs,
            scratch_shapes=scratch,
        ),
        out_shape=out_shape,
        input_output_aliases=aliases or {},
        compiler_params=pltpu.CompilerParams(vmem_limit_bytes=vmem * MIB),
        cost_estimate=pl.CostEstimate(flops=int(us * SCALE * 1.0e9), bytes_accessed=int(us * SCALE * 3.0e6), transcendentals=0),
    )(*operands, *after)


ANYWHERE = pl.BlockSpec(memory_space=pltpu.HBM)


def full(shape):
    return pl.BlockSpec(shape, lambda *unused: (0,) * len(shape))


def rows_of(shape):
    return pl.BlockSpec(shape, lambda i, *unused: (i,) + (0,) * (len(shape) - 1))


def lanes_of(shape):
    return pl.BlockSpec(shape, lambda i, *unused: (0, i))


def piece_place(at, j, rows, lanes):
    row = pl.multiple_of((at[j, 0] * 2 + at[j, 2]) * rows, 16)
    lane = pl.multiple_of(at[j, 1] * lanes, 128)
    return pl.ds(row, rows), pl.ds(lane, lanes)


def load_pieces(at, pieces, low, rows, whole, sem):
    copies = []
    deep, lanes = pieces[0].shape[0], pieces[0].shape[2]
    for i, piece in enumerate(pieces):
        for k in range(deep):
            place = piece_place(at, i * deep + k, rows, lanes)
            copy = pltpu.make_async_copy(piece.at[k, pl.ds(low, rows), :], whole.at[place], sem.at[i * deep + k])
            copy.start()
            copies.append(copy)
    return copies


def store_pieces(at, whole, rows, own, far, low, sem):
    copies = []
    count, deep, lanes = own.shape[0], own.shape[1], own.shape[3]
    for i in range(2 * count):
        for k in range(deep):
            place = piece_place(at, i * deep + k, rows, lanes)
            target = own.at[i, k] if i < count else far.at[i - count, k]
            copy = pltpu.make_async_copy(whole.at[place], target.at[pl.ds(low, rows), :], sem.at[i * deep + k])
            copy.start()
            copies.append(copy)
    return copies


def wait_all(copies):
    for copy in copies:
        copy.wait()


def unpack_vectors(pieces, places, low, share, width, wide, narrow):
    n, deep, lanes = len(pieces), pieces[0].shape[0], pieces[0].shape[2]
    hidden = wide * narrow * share - 8 * width
    group = hidden // (2 * wide)
    unit = group // 2
    lines = 8 + hidden // width

    def kernel(at, *refs):
        parts, (vecs, bias, up_a, up_b, slots, flat, sem) = refs[:n], refs[n:]
        copies = []
        for i, piece in enumerate(parts):
            for k in range(deep):
                j = i * deep + k
                slot = at[j, 0] * narrow + at[j, 1] * 2 + at[j, 2]
                copy = pltpu.make_async_copy(piece.at[k, pl.ds(low, 16), :], slots.at[slot], sem.at[j])
                copy.start()
                copies.append(copy)
        wait_all(copies)
        for j in range(wide * narrow):
            values = slots[j].astype(F32)[0:1, :]
            done = 0
            while done < share:
                line, lane = divmod(j * share + done, width)
                take = min(share - done, width - lane)
                flat[line : line + 1, lane : lane + take] = values[:, done : done + take]
                done += take
        vecs[...] = flat[0:8, :]
        columns = lambda line: jnp.broadcast_to(flat[line : line + 1, :], (128, width)).T[:, 0:1]
        bias[0:width, :] = columns(2)
        bias[width : 2 * width, :] = jnp.zeros((width, 1), F32)
        bias[2 * width :, :] = columns(3)
        up = jnp.concatenate([columns(line) for line in range(8, lines)], axis=0)
        for k in range(2 * wide):
            up_a[k * unit : (k + 1) * unit, :] = up[k * group : k * group + unit, :]
            up_b[k * unit : (k + 1) * unit, :] = up[k * group + unit : (k + 1) * group, :]

    column = jax.ShapeDtypeStruct((hidden // 2, 1), F32)
    return call(
        kernel,
        (1,),
        [ANYWHERE] * n,
        [full((8, width)), full((3 * width, 1)), full(column.shape), full(column.shape)],
        [jax.ShapeDtypeStruct((8, width), F32), jax.ShapeDtypeStruct((3 * width, 1), F32), column, column],
        [
            pltpu.VMEM((wide * narrow, 16, lanes), BF),
            pltpu.VMEM((16, width), F32),
            pltpu.SemaphoreType.DMA((n * deep,)),
        ],
        16,
        3,
        (places, *pieces),
        prefetch=1,
    )


def project_qkv(tokens, vecs, bias, pieces, places, shape, after=()):
    rows, width = tokens.shape
    half, wide = shape
    n, block, steps = len(pieces), 256, 3 * width // 256

    def kernel(at, tok, vec, bias_ref, *refs):
        parts, (hid_out, out, weight, hid, sem) = refs[:n], refs[n:]
        step = pl.program_id(0)

        @pl.when(step == 0)
        def first():
            copies = load_pieces(at, parts, 0, half, weight, sem)
            hat, unused = normed(tok[...].astype(F32))
            hid[...] = (hat * vec[0:1, :] + vec[1:2, :]).astype(BF)
            hid_out[...] = hid[...]
            wait_all(copies)

        start = pl.multiple_of(step * block, block)
        out[...] = (nt(weight[pl.ds(start, block), :], hid[...]) + bias_ref[...]).astype(BF)

    return call(
        kernel,
        (steps,),
        [full((rows, width)), full(vecs.shape), rows_of((block, 1))] + [ANYWHERE] * n,
        [full((rows, width)), rows_of((block, rows))],
        [jax.ShapeDtypeStruct((rows, width), BF), jax.ShapeDtypeStruct((3 * width, rows), BF)],
        [
            pltpu.VMEM((3 * width, width), BF),
            pltpu.VMEM((rows, width), BF),
            pltpu.SemaphoreType.DMA((n * pieces[0].shape[0],)),
        ],
        32,
        9,
        (places, tokens, vecs, bias, *pieces),
        prefetch=1,
        after=after,
    )


QB = 128
KB = 256
PARTS = 2


def window_bias(seg_row, seg_col):
    return jnp.where(seg_col == seg_row, 0.0, NEG).astype(F32)


def shift_in(dst, src):
    count, rows = src.shape
    half = KB // 4
    zero = jnp.zeros((count, half), src.dtype)
    dst[...] = jnp.concatenate([zero, src, zero], axis=1)


def head_parts(width, rows, part):
    half = width // PARTS
    return [
        pl.BlockSpec((half, QB), lambda i, *unused: (part, i)),
        pl.BlockSpec((half, rows), lambda i, *unused: (PARTS + part, 0)),
        pl.BlockSpec((half, rows), lambda i, *unused: (2 * PARTS + part, 0)),
    ]


def attend(qkv_t, seg_row, seg_col, width, part, after=()):
    rows = qkv_t.shape[1]
    half = width // PARTS
    heads = half // HEAD_DIM

    def kernel(q_ref, k_ref, v_ref, seg_r, seg_c, o_ref, lse_ref, keys, values):
        step = pl.program_id(0)

        @pl.when(step == 0)
        def first():
            shift_in(keys, k_ref[...])
            shift_in(values, v_ref[...])

        start = pl.multiple_of(step * QB, QB)
        window = pl.ds(start, KB)
        bias = window_bias(seg_r[0:1, :], seg_c[window, :])
        ats = [slice(h * HEAD_DIM, (h + 1) * HEAD_DIM) for h in range(heads)]
        scores = [tn(keys[at, window], q_ref[at, :] * BF(HEAD_DIM**-0.5)) + bias for at in ats]
        tops = [jnp.max(s, axis=0, keepdims=True) for s in scores]
        expos = [jnp.exp(s - t) for s, t in zip(scores, tops)]
        sums = [jnp.sum(e, axis=0, keepdims=True) for e in expos]
        probs = [(e * (1.0 / s)).astype(BF) for e, s in zip(expos, sums)]
        for at, p in zip(ats, probs):
            o_ref[at, :] = nn(values[at, window], p).astype(BF)
        for h, (t, s) in enumerate(zip(tops, sums)):
            lse_ref[h : h + 1, :] = t + jnp.log(s)

    return call(
        kernel,
        (rows // QB,),
        head_parts(width, rows, part) + [lanes_of((8, QB)), full(seg_col.shape)],
        [lanes_of((half, QB)), lanes_of((16, QB))],
        [jax.ShapeDtypeStruct((half, rows), BF), jax.ShapeDtypeStruct((16, rows), F32)],
        [pltpu.VMEM((half, rows + QB), BF), pltpu.VMEM((half, rows + QB), BF)],
        40,
        6,
        (qkv_t, qkv_t, qkv_t, seg_row, seg_col),
        after=after,
    )


def project_out(o_parts, tokens, vecs, pieces, places, low, rows_piece, after=()):
    rows, width = tokens.shape
    n, block = len(pieces), 256

    def kernel(at, o_a, o_b, tok, vec, *refs):
        parts, (mid_out, hid_out, weight, sem) = refs[:n], refs[n:]

        @pl.when(pl.program_id(0) == 0)
        def first():
            wait_all(load_pieces(at, parts, low, rows_piece, weight, sem))

        both = jnp.concatenate([o_a[...], o_b[...]], axis=0)
        mid = tok[...].astype(F32) + tn(both, weight[...]) + vec[4:5, :]
        mid_out[...] = mid
        hat, unused = normed(mid)
        hid_out[...] = (hat * vec[5:6, :] + vec[6:7, :]).astype(BF)

    return call(
        kernel,
        (rows // block,),
        [lanes_of((width // PARTS, block))] * PARTS + [rows_of((block, width)), full(vecs.shape)] + [ANYWHERE] * n,
        [rows_of((block, width)), rows_of((block, width))],
        [jax.ShapeDtypeStruct((rows, width), F32), jax.ShapeDtypeStruct((rows, width), BF)],
        [pltpu.VMEM((width, width), BF), pltpu.SemaphoreType.DMA((n * pieces[0].shape[0],))],
        32,
        5,
        (places, *o_parts, tokens, vecs, *pieces),
        prefetch=1,
        after=after,
    )


def mlp_half(hidden, cot, bias, pieces, places, low, unit_rows, group_rows, wide, after=()):
    rows, width = hidden.shape
    n, deep, lanes = len(pieces), pieces[0].shape[0], pieces[0].shape[2]
    units = 2 * wide * unit_rows
    block = min(384, units)

    def kernel(at, hid, cot_ref, bias_ref, *refs):
        parts = refs[:n]
        act_out, grad_out, sum_out, own, far, up, down, d_up, d_down, sem_a, sem_b = refs[n:]
        step = pl.program_id(0)

        @pl.when(step == 0)
        def first():
            one = load_pieces(at, parts, low, unit_rows, up, sem_a)
            two = load_pieces(at, parts, low + unit_rows, unit_rows, down, sem_b)
            wait_all(one)
            wait_all(two)

        here = pl.ds(pl.multiple_of(step * block, block), block)
        pre = nt(up[here, :], hid[...]) + bias_ref[...]
        grad_act = nt(down[here, :], cot_ref[...])
        cdf, pdf = cdf_pdf(pre)
        act = (pre * cdf).astype(BF)
        grad = (grad_act * (cdf + pre * pdf)).astype(BF)
        act_out[...] = act
        grad_out[...] = grad
        sum_out[...] = nt(jnp.ones((8, rows), BF), grad)
        d_down[here, :] = nn(act, cot_ref[...]).astype(BF)
        d_up[here, :] = nn(grad, hid[...]).astype(BF)

        @pl.when(step == pl.num_programs(0) - 1)
        def last():
            one = store_pieces(at, d_up, unit_rows, own, far, 0, sem_a)
            two = store_pieces(at, d_down, unit_rows, own, far, unit_rows, sem_b)
            wait_all(one)
            wait_all(two)

    piece_shape = jax.ShapeDtypeStruct((n // 2, deep, group_rows, lanes), BF)
    return call(
        kernel,
        (units // block,),
        [full((rows, width)), full((rows, width)), rows_of((block, 1))] + [ANYWHERE] * n,
        [rows_of((block, rows)), rows_of((block, rows)), lanes_of((8, block)), ANYWHERE, ANYWHERE],
        [
            jax.ShapeDtypeStruct((units, rows), BF),
            jax.ShapeDtypeStruct((units, rows), BF),
            jax.ShapeDtypeStruct((8, units), F32),
            piece_shape,
            piece_shape,
        ],
        [pltpu.VMEM((units, width), BF)] * 4
        + [pltpu.SemaphoreType.DMA((n * deep,))] * 2,
        48,
        22,
        (places, hidden, cot, bias, *pieces),
        prefetch=1,
        after=after,
    )


def second_norm_back(grads, mid, cot, vecs, groups, places, unit_rows, wide, after=()):
    rows, width = mid.shape
    block = 256
    n, deep = len(groups[0][0]), groups[0][0][0].shape[0]
    units = 2 * wide * unit_rows

    def kernel(at, ga, gb, mid_ref, cot_ref, vec, *refs):
        parts = refs[: 2 * n]
        out, low_out, sums, up_a, up_b, sem = refs[2 * n :]
        step = pl.program_id(0)

        @pl.when(step == 0)
        def first():
            one = load_pieces(at, parts[:n], groups[0][1], unit_rows, up_a, sem.at[0])
            two = load_pieces(at, parts[n:], groups[1][1], unit_rows, up_b, sem.at[1])
            wait_all(one)
            wait_all(two)
            sums[...] = jnp.zeros_like(sums)

        grad = tn(ga[...], up_a[...]) + tn(gb[...], up_b[...])
        hat, inverse = normed(mid_ref[...])
        top = cot_ref[...].astype(F32)
        total_grad = top + norm_back(grad, hat, inverse, vec[5:6, :])
        out[...] = total_grad
        lower = total_grad.astype(BF)
        low_out[...] = lower
        sums[0:1, :] += jnp.sum(grad * hat, axis=0, keepdims=True)
        sums[1:2, :] += jnp.sum(grad, axis=0, keepdims=True)
        sums[2:3, :] += jnp.sum(lower.astype(F32), axis=0, keepdims=True)
        sums[3:4, :] += jnp.sum(top, axis=0, keepdims=True)

    return call(
        kernel,
        (rows // block,),
        [lanes_of((units, block)), lanes_of((units, block)), rows_of((block, width)), rows_of((block, width)), full(vecs.shape)]
        + [ANYWHERE] * (2 * n),
        [rows_of((block, width)), rows_of((block, width)), full((8, width))],
        [
            jax.ShapeDtypeStruct((rows, width), F32),
            jax.ShapeDtypeStruct((rows, width), BF),
            jax.ShapeDtypeStruct((8, width), F32),
        ],
        [pltpu.VMEM((units, width), BF)] * 2 + [pltpu.SemaphoreType.DMA((2, n * deep))],
        48,
        14 * BACK,
        (places, *grads, mid, cot, vecs, *groups[0][0], *groups[1][0]),
        prefetch=1,
        after=after,
    )


def out_back(o_parts, grad_low, pieces, places, low_in, rows_piece, own, far, low, after=()):
    rows, width = grad_low.shape
    half = width // PARTS
    n, deep = len(pieces), pieces[0].shape[0]

    def kernel(at, o_a, o_b, grad, own_in, far_in, *refs):
        parts, (do_ref, own_ref, far_ref, weight, d_weight, sem) = refs[:n], refs[n:]
        copies = load_pieces(at, parts, low_in, rows_piece, weight, sem)
        d_weight[:half, :] = nn(o_a[...], grad[...]).astype(BF)
        d_weight[half:, :] = nn(o_b[...], grad[...]).astype(BF)
        wait_all(copies)
        copies = store_pieces(at, d_weight, rows_piece, own_ref, far_ref, low, sem)
        do_ref[...] = nt(weight[...], grad[...]).astype(BF)
        wait_all(copies)

    return call(
        kernel,
        (1,),
        [full((half, rows))] * PARTS + [full((rows, width)), ANYWHERE, ANYWHERE] + [ANYWHERE] * n,
        [full((width, rows)), ANYWHERE, ANYWHERE],
        [
            jax.ShapeDtypeStruct((width, rows), BF),
            jax.ShapeDtypeStruct(own.shape, BF),
            jax.ShapeDtypeStruct(far.shape, BF),
        ],
        [pltpu.VMEM((width, width), BF)] * 2 + [pltpu.SemaphoreType.DMA((n * deep,))],
        32,
        5 * BACK,
        (places, *o_parts, grad_low, own, far, *pieces),
        prefetch=1,
        aliases={4: 1, 5: 2},
        after=after,
    )


def attend_back(qkv_t, do_t, lse, seg_row, seg_col, width, part, after=()):
    rows = qkv_t.shape[1]
    half = width // PARTS
    heads = half // HEAD_DIM
    scale = HEAD_DIM**-0.5

    def kernel(q_ref, k_ref, v_ref, do_ref, lse_ref, seg_r, seg_c, out, sums, keys, values, d_keys, d_values):
        step = pl.program_id(0)

        @pl.when(step == 0)
        def first():
            shift_in(keys, k_ref[...])
            shift_in(values, v_ref[...])
            d_keys[...] = jnp.zeros_like(d_keys)
            d_values[...] = jnp.zeros_like(d_values)

        start = pl.multiple_of(step * QB, QB)
        window = pl.ds(start, KB)
        bias = window_bias(seg_r[0:1, :], seg_c[window, :])
        ats = [slice(h * HEAD_DIM, (h + 1) * HEAD_DIM) for h in range(heads)]
        queries = [q_ref[at, :] * BF(scale) for at in ats]
        raw = [tn(keys[at, window], q) for at, q in zip(ats, queries)]
        grad_probs = [tn(values[at, window], do_ref[at, :]) for at in ats]
        probs = [jnp.exp(r + (bias - lse_ref[h : h + 1, :])) for h, r in enumerate(raw)]
        weighted = [p * g for p, g in zip(probs, grad_probs)]
        deltas = [jnp.sum(w, axis=0, keepdims=True) for w in weighted]
        scores = [(w - p * d).astype(BF) for w, p, d in zip(weighted, probs, deltas)]
        for at, s in zip(ats, scores):
            out[at, pl.ds(start, QB)] = (nn(keys[at, window], s) * scale).astype(BF)
        for at, q, s in zip(ats, queries, scores):
            d_keys[at, window] += nt(q, s)
        for at, p in zip(ats, probs):
            d_values[at, window] += nt(do_ref[at, :], p.astype(BF))

        @pl.when(step == pl.num_programs(0) - 1)
        def last():
            edge = KB // 4
            out[half : 2 * half, :] = d_keys[...][:, edge : edge + rows].astype(BF)
            out[2 * half : 3 * half, :] = d_values[...][:, edge : edge + rows].astype(BF)
            sums[...] = nt(jnp.ones((8, rows), BF), out[...])

    return call(
        kernel,
        (rows // QB,),
        head_parts(width, rows, part)
        + [
            pl.BlockSpec((half, QB), lambda i, *unused: (part, i)),
            lanes_of((16, QB)),
            lanes_of((8, QB)),
            full(seg_col.shape),
        ],
        [full((3 * half, rows)), full((8, 3 * half))],
        [jax.ShapeDtypeStruct((3 * half, rows), BF), jax.ShapeDtypeStruct((8, 3 * half), F32)],
        [pltpu.VMEM((half, rows + QB), BF)] * 2 + [pltpu.VMEM((half, rows + QB), F32)] * 2,
        48,
        12 * BACK,
        (qkv_t, qkv_t, qkv_t, do_t, lse, seg_row, seg_col),
        after=after,
    )


def qkv_back(grad_parts, hidden, places, rows_piece, topo, after=()):
    rows, width = hidden.shape
    half = width // PARTS
    count = 3 * width
    sites, lanes = topo.X * topo.X, width // topo.Y

    def kernel(at, grad_a, grad_b, hid, own, far, whole, sem):
        step = pl.program_id(0)
        for part, grad in enumerate((grad_a, grad_b)):
            here = pl.ds(pl.multiple_of(step * width + part * half, half), half)
            whole[here, :] = nn(grad[...], hid[...]).astype(BF)

        @pl.when(step == pl.num_programs(0) - 1)
        def last():
            wait_all(store_pieces(at, whole, rows_piece, own, far, 0, sem))

    piece_shape = jax.ShapeDtypeStruct((sites, topo.Z, rows_piece, lanes), BF)
    return call(
        kernel,
        (3,),
        [rows_of((half, rows))] * PARTS + [full((rows, width))],
        [ANYWHERE, ANYWHERE],
        [piece_shape, piece_shape],
        [pltpu.VMEM((count, width), BF), pltpu.SemaphoreType.DMA((2 * sites * topo.Z,))],
        32,
        7 * BACK,
        (places, *grad_parts, hidden),
        prefetch=1,
        after=after,
    )


def first_norm_back(grad_parts, tokens, grad_mid, vecs, pieces, places, rows_piece, after=()):
    rows, width = tokens.shape
    count, half = 3 * width, width // PARTS
    block = 256
    n = len(pieces)

    def kernel(at, grad_a, grad_b, tok, mid, vec, *refs):
        parts, (out, sums, weight, sem) = refs[:n], refs[n:]

        @pl.when(pl.program_id(0) == 0)
        def first():
            wait_all(load_pieces(at, parts, 0, rows_piece, weight, sem))
            sums[...] = jnp.zeros_like(sums)

        both = jnp.concatenate([g[k * half : (k + 1) * half, :] for k in range(3) for g in (grad_a, grad_b)], axis=0)
        grad = tn(both, weight[...])
        hat, inverse = normed(tok[...].astype(F32))
        out[...] = (mid[...] + norm_back(grad, hat, inverse, vec[0:1, :])).astype(BF)
        sums[0:1, :] += jnp.sum(grad * hat, axis=0, keepdims=True)
        sums[1:2, :] += jnp.sum(grad, axis=0, keepdims=True)

    return call(
        kernel,
        (rows // block,),
        [lanes_of((count // PARTS, block))] * PARTS
        + [rows_of((block, width)), rows_of((block, width)), full(vecs.shape)]
        + [ANYWHERE] * n,
        [rows_of((block, width)), full((8, width))],
        [jax.ShapeDtypeStruct((rows, width), BF), jax.ShapeDtypeStruct((8, width), F32)],
        [pltpu.VMEM((count, width), BF), pltpu.SemaphoreType.DMA((n * pieces[0].shape[0],))],
        40,
        11 * BACK,
        (places, *grad_parts, tokens, grad_mid, vecs, *pieces),
        prefetch=1,
        after=after,
    )


def finish_out(acts, mid, vecs, groups, places, unit_rows, wide, after=()):
    rows, width = mid.shape
    block = 256
    n, deep = len(groups[0][0]), groups[0][0][0].shape[0]
    units = 2 * wide * unit_rows

    def kernel(at, act_a, act_b, mid_ref, vec, *refs):
        parts = refs[: 2 * n]
        out, down_a, down_b, sem = refs[2 * n :]

        @pl.when(pl.program_id(0) == 0)
        def first():
            one = load_pieces(at, parts[:n], groups[0][1], unit_rows, down_a, sem.at[0])
            two = load_pieces(at, parts[n:], groups[1][1], unit_rows, down_b, sem.at[1])
            wait_all(one)
            wait_all(two)

        result = tn(act_a[...], down_a[...]) + tn(act_b[...], down_b[...])
        out[...] = (mid_ref[...] + result + vec[7:8, :]).astype(BF)

    return call(
        kernel,
        (rows // block,),
        [lanes_of((units, block)), lanes_of((units, block)), rows_of((block, width)), full(vecs.shape)]
        + [ANYWHERE] * (2 * n),
        rows_of((block, width)),
        jax.ShapeDtypeStruct((rows, width), BF),
        [pltpu.VMEM((units, width), BF)] * 2 + [pltpu.SemaphoreType.DMA((2, n * deep))],
        48,
        11 * BACK,
        (places, *acts, mid, vecs, *groups[0][0], *groups[1][0]),
        prefetch=1,
        after=after,
    )


def pack_vectors(sums_one, sums_two, sums_qkv, sums_up, places, topo, share, after=()):
    width = sums_one.shape[1]
    half = width // PARTS
    hidden = PARTS * sums_up[0].shape[1]
    group = hidden // (2 * topo.wide)
    unit = group // 2
    sites, deep, lanes = topo.X * topo.X, topo.Z, width // topo.Y
    lines = 8 + hidden // width

    def kernel(at, one, two, qkv_a, qkv_b, up_a, up_b, own, far, flat, ups, slots):
        flat[0:2, :] = one[0:2, :]
        for part, ref in enumerate((qkv_a, qkv_b)):
            lane = slice(part * half, (part + 1) * half)
            flat[2:3, lane] = ref[0:1, 0:half]
            flat[3:4, lane] = ref[0:1, 2 * half : 3 * half]
        flat[4:5, :] = two[2:3, :]
        flat[5:7, :] = two[0:2, :]
        flat[7:8, :] = two[3:4, :]
        for k in range(2 * topo.wide):
            for part, ref in enumerate((up_a, up_b)):
                ups[0:1, k * group + part * unit : k * group + (part + 1) * unit] = ref[0:1, k * unit : (k + 1) * unit]
        for line in range(8, lines):
            flat[line : line + 1, :] = ups[0:1, (line - 8) * width : (line - 7) * width]
        slots[...] = jnp.zeros_like(slots)
        for j in range(topo.wide * topo.narrow):
            done = 0
            while done < share:
                line, lane = divmod(j * share + done, width)
                take = min(share - done, width - lane)
                slots[j, 0:1, done : done + take] = flat[line : line + 1, lane : lane + take]
                done += take
        for j in range(2 * sites * deep):
            i, k = divmod(j, deep)
            slot = at[j, 0] * topo.narrow + at[j, 1] * 2 + at[j, 2]
            target = own.at[i, k] if i < sites else far.at[i - sites, k]
            target[...] = jnp.broadcast_to(slots[slot, 0:1, :], (16, lanes)).astype(BF)

    shape = (sites, deep, 16, lanes)
    return call(
        kernel,
        (1,),
        [full(a.shape) for a in (sums_one, sums_two, *sums_qkv, *sums_up)],
        [full(shape)] * 2,
        [jax.ShapeDtypeStruct(shape, BF)] * 2,
        [
            pltpu.VMEM((16, width), F32),
            pltpu.VMEM((8, hidden), F32),
            pltpu.VMEM((topo.wide * topo.narrow, 8, lanes), F32),
        ],
        16,
        3 * BACK,
        (places, sums_one, sums_two, *sums_qkv, *sums_up),
        prefetch=1,
        after=after,
    )


def total(first, *rest):
    result = first.astype(F32)
    for other in rest:
        result = result + other.astype(F32)
    return result


def tied(values, others):
    return lax.optimization_barrier((values, tuple(others)))[0] if others else values


class Spread:
    def __init__(self, piece, topo):
        self.topo, self.piece = topo, piece
        self.coming = tuple(send(piece, topo.zp[k]) for k in range(1, topo.Z))

    def along(self, others=()):
        stack = tied(jnp.stack((self.piece, *self.coming)), others)
        self.coming = tuple(send(stack, self.topo.ap[k]) for k in range(1, self.topo.X))
        self.line = (stack, *self.coming)

    def across(self, others=()):
        self.near = tuple(send(p, self.topo.cp) for p in self.line)
        line = tied(self.line, others)
        self.coming = tuple(send(q, self.topo.bp[k]) for k in range(1, self.topo.X) for q in line)

    def core(self, others=()):
        coming = tied(self.coming, others)
        self.pieces = [*self.line, *coming, *self.near, *[send(p, self.topo.cp) for p in coming]]


class Chain:
    def __init__(self, own, far, topo):
        self.topo, self.held = topo, own
        self.coming = [send(far, topo.cp)]

    def arrived(self):
        return tuple(self.coming)

    def fold(self, part=None):
        terms = (self.held, *self.coming)
        return total(*(terms if part is None else [t[part] for t in terms]))

    def stage(self, count, perms, others):
        self.held, self.coming = tied((self.held, self.coming), others)
        self.held, *sent = [self.fold(k).astype(BF) for k in range(count)]
        self.sent = tuple(sent)
        self.coming = [send(values, perms[count - 1 - k]) for k, values in enumerate(sent)]

    def across(self, others=()):
        side = self.topo.X
        split = lambda values: values.reshape(side, side, *values.shape[1:])
        self.held, self.coming = split(self.held), [split(c) for c in self.coming]
        self.stage(side, self.topo.bp, others)

    def along(self, others=()):
        self.stage(self.topo.X, self.topo.ap, others)

    def down(self, others=()):
        self.stage(self.topo.Z, self.topo.zp, others)

    def result(self, others=()):
        self.held, self.coming = tied((self.held, self.coming), others)
        return self.fold()


def tail_rows(values, rows, lanes):
    return jnp.pad(values[None], ((0, rows - 1), (0, lanes - values.shape[0])))


def fits(topo, rows, width, hidden):
    lanes = 2 * width // topo.narrow
    return (
        lanes % 128 == 0
        and rows % 256 == 0
        and (width // topo.wide) % 32 == 0
        and (hidden // topo.wide) % 64 == 0
        and 2 * P_THREE == QB
    )


def fast_device(
    tokens, qkv_weight, out_weight, up_weight, down_weight, vectors, bucket_counts, cotangent, topo
):
    rows, width = tokens.shape
    wide = topo.wide
    places = topo.origins()
    core = topo.here()[3]
    shards = [qkv_weight.astype(BF).T, out_weight.astype(BF), up_weight.astype(BF).T, down_weight.astype(BF)]
    r_qkv, r_out, r_unit = shards[0].shape[0] // 2, shards[1].shape[0] // 2, shards[2].shape[0] // 4
    lanes = 2 * out_weight.shape[1]
    halves = [jnp.concatenate([pick_half(s, 0, h) for h in range(2) for s in pair], axis=0) for pair in (shards[:2], shards[2:])]
    first = pair_up(halves[0], topo, core)
    vec_low, out_low = r_qkv, r_qkv + 16
    one = Spread(
        jnp.concatenate([first[:r_qkv], tail_rows(vectors.astype(BF), 16, lanes), first[r_qkv:]], axis=0), topo
    )
    rest = pair_up(tied(halves[1], one.coming), topo, core)
    piece_two = jnp.concatenate([rest[:r_unit], rest[2 * r_unit : 3 * r_unit]], axis=0)
    piece_three = jnp.concatenate([rest[r_unit : 2 * r_unit], rest[3 * r_unit :]], axis=0)
    one.along()
    two = Spread(tied(piece_two, one.line[:1]), topo)
    one.across()
    one.core()
    one = one.pieces
    vecs, bias_qkv, *bias_up = unpack_vectors(one, places, vec_low, vectors.shape[0], width, wide, topo.narrow)
    segment = image_ids(bucket_counts[0], rows)
    seg_row = jnp.broadcast_to(segment[None], (8, rows))
    seg_col = jnp.pad(segment, (QB // 2, QB // 2), constant_values=-1)[:, None]

    hidden_one, qkv_t = project_qkv(tokens, vecs, bias_qkv, one, places, (r_qkv, wide))
    two.along((hidden_one,))
    three = Spread(tied(piece_three, (hidden_one,)), topo)
    attn_a, lse_a = attend(qkv_t, seg_row, seg_col, width, 0, after=two.line[:1])
    two.across((lse_a,))
    attn_b, lse_b = attend(qkv_t, seg_row, seg_col, width, 1)
    attn_t, lse = (attn_a, attn_b), (lse_a, lse_b)
    three.along((lse_b,))
    mid, hidden_two = project_out(attn_t, tokens, vecs, one, places, out_low, r_out, after=three.line[:1])
    two.core((hidden_two,))
    three.across((hidden_two,))
    two = two.pieces
    three_along = three.line
    act_a, grad_a, sum_a, own_a, far_a = mlp_half(
        hidden_two, cotangent, bias_up[0], two, places, 0, r_unit, 2 * r_unit, wide, after=three_along
    )
    three.core((sum_a,))
    three = three.pieces
    chain_a = Chain(own_a, far_a, topo)
    act_b, grad_b, sum_b, own_b, far_b = mlp_half(
        hidden_two, cotangent, bias_up[1], three, places, 0, r_unit, 2 * r_unit + r_out, wide
    )
    chain_a.across((sum_b,))
    grad_mid, grad_mid_low, sums_two = second_norm_back(
        (grad_a, grad_b), mid, cotangent, vecs, ((two, 0), (three, 0)), places, r_unit, wide,
        after=chain_a.sent,
    )
    do_t, own_b, far_b = out_back(attn_t, grad_mid_low, one, places, out_low, r_out, own_b, far_b, 2 * r_unit)
    chain_b = Chain(own_b, far_b, topo)
    chain_a.along((do_t,))
    grads_0, sums_0 = attend_back(qkv_t, do_t, lse[0], seg_row, seg_col, width, 0, after=chain_a.sent)
    chain_a.down((sums_0,))
    chain_b.across((sums_0,))
    grads_1, sums_1 = attend_back(
        qkv_t, do_t, lse[1], seg_row, seg_col, width, 1, after=chain_a.sent + chain_b.sent
    )
    grad_t = (grads_0, grads_1)
    own_q, far_q = qkv_back(grad_t, hidden_one, places, r_qkv, topo)
    chain_q = Chain(own_q, far_q, topo)
    chain_b.along((far_q,))
    chain_q.across()
    input_grad, sums_one = first_norm_back(
        grad_t, tokens, grad_mid, vecs, one, places, r_qkv, after=chain_q.sent + chain_b.sent
    )
    chain_q.along((sums_one,))
    chain_b.down((sums_one,))
    own_v, far_v = pack_vectors(
        sums_one, sums_two, (sums_0, sums_1), (sum_a, sum_b), places, topo, vectors.shape[0], after=chain_q.sent
    )
    chain_v = Chain(own_v, far_v, topo)
    chain_v.across()
    chain_q.down()
    block_out = finish_out(
        (act_a, act_b), mid, vecs, ((two, r_unit), (three, r_unit)), places, r_unit, wide,
        after=chain_q.sent + chain_v.sent,
    )
    chain_v.along((block_out,))
    chain_v.down()
    part_a, part_b, part_q = chain_a.result((sums_one,)), chain_b.result((block_out,)), chain_q.result()
    vector_grad = chain_v.result()[0, : vectors.shape[0]]
    down = jnp.concatenate([part_a[r_unit:], part_b[r_unit : 2 * r_unit]], axis=0)
    up = jnp.concatenate([part_a[:r_unit], part_b[:r_unit]], axis=0)
    out = part_b[2 * r_unit :]
    grads = [unpair(g, topo, core) for g in (part_q, out, up, down)]
    return (block_out, input_grad, grads[0].T, grads[1], grads[2].T, grads[3], vector_grad)


def per_device(
    tokens, qkv_weight, out_weight, up_weight, down_weight, vectors, bucket_counts, cotangent
):
    topo = Topo(lax.axis_size("wide"), lax.axis_size("narrow"))
    operands = (tokens, qkv_weight, out_weight, up_weight, down_weight, vectors, bucket_counts, cotangent)
    if fits(topo, *tokens.shape, up_weight.shape[1] * topo.wide):
        return fast_device(*operands, topo)
    return plain_device(*operands)


def plain_device(
    tokens, qkv_weight, out_weight, up_weight, down_weight, vectors, bucket_counts, cotangent
):
    rows, width = tokens.shape
    halves = (
        lax.all_gather(qkv_weight.astype(jnp.bfloat16), "narrow", axis=0, tiled=True),
        lax.all_gather(out_weight.astype(jnp.bfloat16), "narrow", axis=1, tiled=True),
        lax.all_gather(up_weight.astype(jnp.bfloat16), "narrow", axis=0, tiled=True),
        lax.all_gather(down_weight.astype(jnp.bfloat16), "narrow", axis=1, tiled=True),
        lax.all_gather(vectors.astype(jnp.bfloat16), "narrow", axis=0, tiled=True),
    )
    wholes = (
        lax.all_gather(halves[0], "wide", axis=1, tiled=True),
        lax.all_gather(halves[1], "wide", axis=0, tiled=True),
        lax.all_gather(halves[2], "wide", axis=1, tiled=True),
        lax.all_gather(halves[3], "wide", axis=0, tiled=True),
        lax.all_gather(halves[4], "wide", axis=0, tiled=True),
    )
    qkv_full, out_full, up_full, down_full, packed = wholes
    params = packed.astype(jnp.float32)
    gain_one = params[0:width]
    shift_one = params[width : 2 * width]
    bias_query = params[2 * width : 3 * width]
    bias_value = params[3 * width : 4 * width]
    bias_out = params[4 * width : 5 * width]
    gain_two = params[5 * width : 6 * width]
    shift_two = params[6 * width : 7 * width]
    bias_down = params[7 * width : 8 * width]
    bias_up = params[8 * width :]
    inputs = tokens.astype(jnp.float32)
    hidden_one = layer_norm(inputs, gain_one, shift_one).astype(jnp.bfloat16)
    qkv_bias = jnp.concatenate([bias_query, jnp.zeros((width,), jnp.float32), bias_value])
    qkv_all = (jnp.dot(hidden_one, qkv_full, preferred_element_type=jnp.float32) + qkv_bias).astype(
        jnp.bfloat16
    )
    margin = P_THREE
    blocks = rows // QROWS
    span = QROWS + 2 * margin
    scale = HEAD_DIM ** (-0.5)
    query_blk = qkv_all[:, :width].reshape(blocks, QROWS, HEADS, HEAD_DIM)
    keys_win = windows_of(qkv_all[:, width : 2 * width], margin, blocks, 0).reshape(
        blocks, span, HEADS, HEAD_DIM
    )
    values_win = windows_of(qkv_all[:, 2 * width :], margin, blocks, 0).reshape(
        blocks, span, HEADS, HEAD_DIM
    )
    segment = image_ids(bucket_counts[0], rows)
    seg_rows = segment.reshape(blocks, QROWS)
    seg_cols = windows_of(segment, margin, blocks, -1)
    same = seg_rows[:, None, :, None] == seg_cols[:, None, None, :]
    raw = (
        jnp.einsum("bqhd,bkhd->bhqk", query_blk, keys_win, preferred_element_type=jnp.float32)
        * scale
    )
    masked = jnp.where(same, raw, NEG)
    top = jnp.max(masked, axis=3, keepdims=True)
    expo = jnp.exp(masked - top)
    total = jnp.sum(expo, axis=3, keepdims=True)
    probs_low = (expo / total).astype(jnp.bfloat16)
    log_total = top + jnp.log(total)
    attended = jnp.einsum(
        "bhqk,bkhd->bqhd", probs_low, values_win, preferred_element_type=jnp.float32
    )
    attn_low = attended.reshape(rows, width).astype(jnp.bfloat16)
    mid = inputs + jnp.dot(attn_low, out_full, preferred_element_type=jnp.float32) + bias_out
    hidden_two = layer_norm(mid, gain_two, shift_two).astype(jnp.bfloat16)
    pre_act = jnp.dot(hidden_two, up_full, preferred_element_type=jnp.float32) + bias_up
    activated = gelu_exact(pre_act).astype(jnp.bfloat16)
    output = mid + jnp.dot(activated, down_full, preferred_element_type=jnp.float32) + bias_down
    block_out = output.astype(jnp.bfloat16)
    grad_top = cotangent.astype(jnp.float32)
    d_down = contract_rows(activated, cotangent)
    d_bias_down = jnp.sum(grad_top, axis=0)
    grad_act = contract_cols(cotangent, down_full)
    unused_act, gelu_back = jax.vjp(gelu_exact, pre_act)
    grad_pre = gelu_back(grad_act)[0].astype(jnp.bfloat16)
    d_up = contract_rows(hidden_two, grad_pre)
    d_bias_up = jnp.sum(grad_pre.astype(jnp.float32), axis=0)
    grad_hidden_two = contract_cols(grad_pre, up_full)
    unused_two, norm_back_two = jax.vjp(layer_norm, mid, gain_two, shift_two)
    grad_mid_part, d_gain_two, d_shift_two = norm_back_two(grad_hidden_two)
    grad_mid = grad_top + grad_mid_part
    grad_mid_low = grad_mid.astype(jnp.bfloat16)
    d_out = contract_rows(attn_low, grad_mid_low)
    d_bias_out = jnp.sum(grad_mid_low.astype(jnp.float32), axis=0)
    grad_attn = contract_cols(grad_mid_low, out_full).astype(jnp.bfloat16)
    raw_again = (
        jnp.einsum("bqhd,bkhd->bhqk", query_blk, keys_win, preferred_element_type=jnp.float32)
        * scale
    )
    probs = jnp.exp(jnp.where(same, raw_again, NEG) - log_total)
    grad_blk = grad_attn.reshape(blocks, QROWS, HEADS, HEAD_DIM)
    grad_probs = jnp.einsum(
        "bqhd,bkhd->bhqk", grad_blk, values_win, preferred_element_type=jnp.float32
    )
    grad_scores = (
        probs * (grad_probs - jnp.sum(probs * grad_probs, axis=3, keepdims=True))
    ).astype(jnp.bfloat16)
    grad_query = (
        jnp.einsum("bhqk,bkhd->bqhd", grad_scores, keys_win, preferred_element_type=jnp.float32)
        * scale
    )
    grad_keys_win = (
        jnp.einsum("bhqk,bqhd->bkhd", grad_scores, query_blk, preferred_element_type=jnp.float32)
        * scale
    )
    grad_values_win = jnp.einsum(
        "bhqk,bqhd->bkhd", probs.astype(jnp.bfloat16), grad_blk, preferred_element_type=jnp.float32
    )
    grad_keys = fold_windows(grad_keys_win.reshape(blocks, span, width), margin, QROWS)
    grad_values = fold_windows(grad_values_win.reshape(blocks, span, width), margin, QROWS)
    grad_qkv = jnp.concatenate(
        [grad_query.reshape(rows, width), grad_keys, grad_values], axis=1
    ).astype(jnp.bfloat16)
    d_qkv = contract_rows(hidden_one, grad_qkv)
    column_sums = jnp.sum(grad_qkv.astype(jnp.float32), axis=0)
    grad_hidden_one = contract_cols(grad_qkv, qkv_full)
    unused_one, norm_back_one = jax.vjp(layer_norm, inputs, gain_one, shift_one)
    grad_in_part, d_gain_one, d_shift_one = norm_back_one(grad_hidden_one)
    input_grad = (grad_mid + grad_in_part).astype(jnp.bfloat16)
    d_vector = jnp.concatenate(
        [
            d_gain_one,
            d_shift_one,
            column_sums[:width],
            column_sums[2 * width :],
            d_bias_out,
            d_gain_two,
            d_shift_two,
            d_bias_down,
            d_bias_up,
        ]
    )
    partial_sums = (
        lax.psum_scatter(
            d_qkv.astype(jnp.bfloat16), "wide", scatter_dimension=1, tiled=True
        ).astype(jnp.float32),
        lax.psum_scatter(
            d_out.astype(jnp.bfloat16), "wide", scatter_dimension=0, tiled=True
        ).astype(jnp.float32),
        lax.psum_scatter(d_up.astype(jnp.bfloat16), "wide", scatter_dimension=1, tiled=True).astype(
            jnp.float32
        ),
        lax.psum_scatter(
            d_down.astype(jnp.bfloat16), "wide", scatter_dimension=0, tiled=True
        ).astype(jnp.float32),
        lax.psum_scatter(
            d_vector.astype(jnp.bfloat16), "wide", scatter_dimension=0, tiled=True
        ).astype(jnp.float32),
    )
    final = (
        lax.psum_scatter(
            partial_sums[0].astype(jnp.bfloat16), "narrow", scatter_dimension=0, tiled=True
        ).astype(jnp.float32),
        lax.psum_scatter(
            partial_sums[1].astype(jnp.bfloat16), "narrow", scatter_dimension=1, tiled=True
        ).astype(jnp.float32),
        lax.psum_scatter(
            partial_sums[2].astype(jnp.bfloat16), "narrow", scatter_dimension=0, tiled=True
        ).astype(jnp.float32),
        lax.psum_scatter(
            partial_sums[3].astype(jnp.bfloat16), "narrow", scatter_dimension=1, tiled=True
        ).astype(jnp.float32),
        lax.psum_scatter(
            partial_sums[4].astype(jnp.bfloat16), "narrow", scatter_dimension=0, tiled=True
        ).astype(jnp.float32),
    )
    return (block_out, input_grad, final[0], final[1], final[2], final[3], final[4])


def solution(mesh):
    return jax.shard_map(
        per_device,
        mesh=mesh,
        in_specs=(
            P(("wide", "narrow"), None),
            P("narrow", "wide"),
            P("wide", "narrow"),
            P("narrow", "wide"),
            P("wide", "narrow"),
            P(("wide", "narrow")),
            P(("wide", "narrow"), None),
            P(("wide", "narrow"), None),
        ),
        out_specs=(
            P(("wide", "narrow"), None),
            P(("wide", "narrow"), None),
            P("narrow", "wide"),
            P("wide", "narrow"),
            P("narrow", "wide"),
            P("wide", "narrow"),
            P(("wide", "narrow")),
        ),
        check_vma=False,
    )
```

```python
import math

import jax
import jax.numpy as jnp
from jax import lax
from jax.experimental import pallas as pl
from jax.experimental.pallas import tpu as pltpu
from jax.sharding import PartitionSpec as P

HEADS = 12
HEAD_DIM = 64
QROWS = 512
P_ONE = 25
P_TWO = 49
P_THREE = 64


EPS = 1e-06
NEG = -1e30


def layer_norm(values, gain, shift):
    center = values - jnp.mean(values, axis=-1, keepdims=True)
    spread = jnp.mean(center * center, axis=-1, keepdims=True)
    return center * lax.rsqrt(spread + EPS) * gain + shift


def image_ids(counts, rows):
    place = jnp.arange(rows, dtype=jnp.int32)
    first = counts[0] * P_ONE
    second = first + counts[1] * P_TWO
    bucket = (place >= first).astype(jnp.int32) + (place >= second).astype(jnp.int32)
    start = jnp.where(bucket == 0, 0, jnp.where(bucket == 1, first, second))
    length = jnp.where(bucket == 0, P_ONE, jnp.where(bucket == 1, P_TWO, P_THREE)).astype(jnp.int32)
    return bucket * rows + (place - start) // length


def gelu_exact(values):
    return jax.nn.gelu(values, approximate=False)


def contract_rows(left, right):
    return lax.dot_general(
        left, right, (((0,), (0,)), ((), ())), preferred_element_type=jnp.float32
    )


def contract_cols(left, right):
    return lax.dot_general(
        left, right, (((1,), (1,)), ((), ())), preferred_element_type=jnp.float32
    )


def windows_of(values, margin, blocks, fill):
    rows = values.shape[0]
    block_rows = rows // blocks
    rest = values.shape[1:]
    padded = jnp.pad(
        values, ((margin, margin),) + tuple(((0, 0) for unused in rest)), constant_values=fill
    )
    before = padded[:rows].reshape((blocks, block_rows) + rest)[:, :margin]
    middle = values.reshape((blocks, block_rows) + rest)
    after = padded[2 * margin : 2 * margin + rows].reshape((blocks, block_rows) + rest)[
        :, block_rows - margin :
    ]
    return jnp.concatenate([before, middle, after], axis=1)


def fold_windows(grads, margin, block_rows):
    blocks = grads.shape[0]
    width = grads.shape[2]
    middle = grads[:, margin : margin + block_rows]
    before = jnp.pad(grads[1:, :margin], ((0, 1), (block_rows - margin, 0), (0, 0)))
    after = jnp.pad(grads[:-1, margin + block_rows :], ((1, 0), (0, block_rows - margin), (0, 0)))
    return (middle + before + after).reshape(blocks * block_rows, width)


BF = jnp.bfloat16
F32 = jnp.float32
AXES = ("wide", "narrow")


class Topo:
    def __init__(self, wide, narrow):
        self.wide, self.narrow = wide, narrow
        self.Y = narrow // 2
        self.X = self.Y
        self.Z = wide // self.X
        side, deep = self.X, self.Z
        self.zp = [self.perm(lambda z, x, y, c, k=k: ((z + k) % deep, x, y, c)) for k in range(deep)]
        self.ap = [
            self.perm(
                lambda z, x, y, c, k=k: (z, (x + k) % side, y, c) if c == 0 else (z, x, (y + k) % side, c)
            )
            for k in range(side)
        ]
        self.bp = [
            self.perm(
                lambda z, x, y, c, k=k: (z, x, (y + k) % side, c) if c == 0 else (z, (x + k) % side, y, c)
            )
            for k in range(side)
        ]
        self.cp = self.perm(lambda z, x, y, c: (z, x, y, 1 - c))

    def did(self, z, x, y, c):
        return ((z * self.X + x) * self.Y + y) * 2 + c

    def perm(self, target):
        return [
            (self.did(z, x, y, c), self.did(*target(z, x, y, c)))
            for z in range(self.Z)
            for x in range(self.X)
            for y in range(self.Y)
            for c in range(2)
        ]

    def here(self):
        wide, narrow = lax.axis_index("wide"), lax.axis_index("narrow")
        return wide // self.X, wide % self.X, narrow // 2, narrow % 2

    def origins(self):
        z0, x0, y0, c0 = self.here()
        side, deep = self.X, self.Z
        index = jnp.arange(2 * side * side * deep, dtype=jnp.int32)
        kz, ka, kb = index % deep, index // deep % side, index // (deep * side) % side
        c = (c0 + index // (deep * side * side)) % 2
        x = (x0 + side - jnp.where(c == 0, ka, kb)) % side
        y = (y0 + side - jnp.where(c == 0, kb, ka)) % side
        z = (z0 + deep - kz) % deep
        return jnp.stack([z * side + x, y, c], axis=1).astype(jnp.int32)


def send(values, perm):
    return lax.ppermute(values, AXES, perm)


def pick_half(values, axis, index):
    half = values.shape[axis] // 2
    return lax.dynamic_slice_in_dim(values, index * half, half, axis)


def pair_up(shard, topo, core):
    mine = pick_half(shard, 0, core)
    other = send(pick_half(shard, 0, 1 - core), topo.cp)
    first = jnp.where(core == 0, mine, other)
    second = jnp.where(core == 0, other, mine)
    return jnp.concatenate([first, second], axis=1)


def unpair(piece, topo, core):
    mine = pick_half(piece, 1, core)
    other = send(pick_half(piece, 1, 1 - core), topo.cp)
    first = jnp.where(core == 0, mine, other)
    second = jnp.where(core == 0, other, mine)
    return jnp.concatenate([first, second], axis=0)


def gather(piece, topo):
    stack = jnp.stack([piece] + [send(piece, topo.zp[k]) for k in range(1, topo.Z)])
    line = [stack] + [send(stack, topo.ap[k]) for k in range(1, topo.X)]
    own = [p for k in range(topo.X) for p in (line if k == 0 else [send(q, topo.bp[k]) for q in line])]
    return own + [send(p, topo.cp) for p in own]


def nn(a, b):
    return lax.dot_general(a, b, (((1,), (0,)), ((), ())), preferred_element_type=F32)


def nt(a, b):
    return lax.dot_general(a, b, (((1,), (1,)), ((), ())), preferred_element_type=F32)


def tn(a, b):
    return lax.dot_general(a, b, (((0,), (0,)), ((), ())), preferred_element_type=F32)


def normed(values):
    center = values - jnp.mean(values, axis=-1, keepdims=True)
    spread = jnp.mean(center * center, axis=-1, keepdims=True)
    inverse = lax.rsqrt(spread + EPS)
    return center * inverse, inverse


def norm_back(grad, hat, inverse, gain):
    scaled = grad * gain
    first = jnp.mean(scaled, axis=-1, keepdims=True)
    second = jnp.mean(scaled * hat, axis=-1, keepdims=True)
    return inverse * (scaled - first - hat * second)


ROOT_HALF = 0.7071067811865476
ROOT_TAU = 0.3989422804014327
MIB = 1024 * 1024
WIDTH = HEADS * HEAD_DIM
SCALE = 1.0
BACK = 3


def cdf_pdf(u):
    bell = jnp.exp(-0.5 * (u * u))
    t = 1.0 / (1.0 + (0.3275911 * ROOT_HALF) * jnp.abs(u))
    poly = 1.061405429 * 0.5
    for coef in (-1.453152027, 1.421413741, -0.284496736, 0.254829592):
        poly = poly * t + coef * 0.5
    upper = poly * t * bell
    return jnp.where(u < 0, upper, 1.0 - upper), ROOT_TAU * bell


def call(kernel, grid, in_specs, out_specs, out_shape, scratch, vmem, us, operands, prefetch=0, aliases=None, after=()):
    first, count = len(operands), len(after)

    def body(*refs):
        kernel(*refs[:first], *refs[first + count :])

    return pl.pallas_call(
        body,
        grid_spec=pltpu.PrefetchScalarGridSpec(
            num_scalar_prefetch=prefetch,
            grid=grid,
            in_specs=in_specs + [ANYWHERE] * count,
            out_specs=out_specs,
            scratch_shapes=scratch,
        ),
        out_shape=out_shape,
        input_output_aliases=aliases or {},
        compiler_params=pltpu.CompilerParams(vmem_limit_bytes=vmem * MIB),
        cost_estimate=pl.CostEstimate(flops=int(us * SCALE * 1.0e9), bytes_accessed=int(us * SCALE * 3.0e6), transcendentals=0),
    )(*operands, *after)


ANYWHERE = pl.BlockSpec(memory_space=pltpu.HBM)


def full(shape):
    return pl.BlockSpec(shape, lambda *unused: (0,) * len(shape))


def rows_of(shape):
    return pl.BlockSpec(shape, lambda i, *unused: (i,) + (0,) * (len(shape) - 1))


def lanes_of(shape):
    return pl.BlockSpec(shape, lambda i, *unused: (0, i))


def piece_place(at, j, rows, lanes):
    row = pl.multiple_of((at[j, 0] * 2 + at[j, 2]) * rows, 16)
    lane = pl.multiple_of(at[j, 1] * lanes, 128)
    return pl.ds(row, rows), pl.ds(lane, lanes)


def sites_of(at, pieces, rows, lanes):
    if len(pieces) == 1:
        (piece,) = pieces
        narrow = 2 * (WIDTH // lanes)
        for j in range(piece.shape[0]):
            wide, y, core = j // narrow, j % narrow // 2, j % 2
            yield piece.at[j], (pl.ds((wide * 2 + core) * rows, rows), pl.ds(y * lanes, lanes))
    else:
        side, deep = pieces[0].shape[:2]
        for i, piece in enumerate(pieces):
            for a in range(side):
                for k in range(deep):
                    yield piece.at[a, k], piece_place(at, (i * side + a) * deep + k, rows, lanes)


def count_of(pieces):
    return len(pieces) * math.prod(pieces[0].shape[:-2])


def load_pieces(at, pieces, low, rows, whole, sem):
    copies = []
    for j, (piece, place) in enumerate(sites_of(at, pieces, rows, pieces[0].shape[-1])):
        copy = pltpu.make_async_copy(piece.at[pl.ds(low, rows), :], whole.at[place], sem.at[j])
        copy.start()
        copies.append(copy)
    return copies


def store_pieces(at, whole, rows, outs, low, sem):
    copies = []
    for j, (piece, place) in enumerate(sites_of(at, outs, rows, outs[0].shape[-1])):
        copy = pltpu.make_async_copy(whole.at[place], piece.at[pl.ds(low, rows), :], sem.at[j])
        copy.start()
        copies.append(copy)
    return copies


def wait_all(copies):
    for copy in copies:
        copy.wait()


def unpack_vectors(pieces, places, low, share, width, wide, narrow):
    n, lanes = len(pieces), pieces[0].shape[-1]
    hidden = wide * narrow * share - 8 * width
    group = hidden // (2 * wide)
    unit = group // 2
    lines = 8 + hidden // width

    def kernel(at, *refs):
        parts, (vecs, bias, up_a, up_b, slots, flat, sem) = refs[:n], refs[n:]
        copies = []
        for j, (piece, unused) in enumerate(sites_of(at, parts, 16, lanes)):
            slot = at[j, 0] * narrow + at[j, 1] * 2 + at[j, 2]
            copy = pltpu.make_async_copy(piece.at[pl.ds(low, 16), :], slots.at[slot], sem.at[j])
            copy.start()
            copies.append(copy)
        wait_all(copies)
        for j in range(wide * narrow):
            values = slots[j].astype(F32)[0:1, :]
            done = 0
            while done < share:
                line, lane = divmod(j * share + done, width)
                take = min(share - done, width - lane)
                flat[line : line + 1, lane : lane + take] = values[:, done : done + take]
                done += take
        vecs[...] = flat[0:8, :]
        columns = lambda line: jnp.broadcast_to(flat[line : line + 1, :], (128, width)).T[:, 0:1]
        bias[0:width, :] = columns(2)
        bias[width : 2 * width, :] = jnp.zeros((width, 1), F32)
        bias[2 * width :, :] = columns(3)
        up = jnp.concatenate([columns(line) for line in range(8, lines)], axis=0)
        for k in range(2 * wide):
            up_a[k * unit : (k + 1) * unit, :] = up[k * group : k * group + unit, :]
            up_b[k * unit : (k + 1) * unit, :] = up[k * group + unit : (k + 1) * group, :]

    column = jax.ShapeDtypeStruct((hidden // 2, 1), F32)
    return call(
        kernel,
        (1,),
        [ANYWHERE] * n,
        [full((8, width)), full((3 * width, 1)), full(column.shape), full(column.shape)],
        [jax.ShapeDtypeStruct((8, width), F32), jax.ShapeDtypeStruct((3 * width, 1), F32), column, column],
        [
            pltpu.VMEM((wide * narrow, 16, lanes), BF),
            pltpu.VMEM((16, width), F32),
            pltpu.SemaphoreType.DMA((count_of(pieces),)),
        ],
        16,
        3,
        (places, *pieces),
        prefetch=1,
    )


def project_qkv(tokens, vecs, bias, pieces, places, shape, after=()):
    rows, width = tokens.shape
    half, wide = shape
    n, block, steps = len(pieces), 256, 3 * width // 256

    def kernel(at, tok, vec, bias_ref, *refs):
        parts, (hid_out, out, weight, hid, sem) = refs[:n], refs[n:]
        step = pl.program_id(0)

        @pl.when(step == 0)
        def first():
            copies = load_pieces(at, parts, 0, half, weight, sem)
            hat, unused = normed(tok[...].astype(F32))
            hid[...] = (hat * vec[0:1, :] + vec[1:2, :]).astype(BF)
            hid_out[...] = hid[...]
            wait_all(copies)

        start = pl.multiple_of(step * block, block)
        out[...] = (nt(weight[pl.ds(start, block), :], hid[...]) + bias_ref[...]).astype(BF)

    return call(
        kernel,
        (steps,),
        [full((rows, width)), full(vecs.shape), rows_of((block, 1))] + [ANYWHERE] * n,
        [full((rows, width)), rows_of((block, rows))],
        [jax.ShapeDtypeStruct((rows, width), BF), jax.ShapeDtypeStruct((3 * width, rows), BF)],
        [
            pltpu.VMEM((3 * width, width), BF),
            pltpu.VMEM((rows, width), BF),
            pltpu.SemaphoreType.DMA((count_of(pieces),)),
        ],
        20,
        9,
        (places, tokens, vecs, bias, *pieces),
        prefetch=1,
        after=after,
    )


QB = 128
KB = 256
PARTS = 2


def window_bias(seg_row, seg_col):
    return jnp.where(seg_col == seg_row, 0.0, NEG).astype(F32)


def shift_in(dst, src):
    count, rows = src.shape
    half = KB // 4
    zero = jnp.zeros((count, half), src.dtype)
    dst[...] = jnp.concatenate([zero, src, zero], axis=1)


def head_parts(width, rows, part):
    half = width // PARTS
    return [
        pl.BlockSpec((half, QB), lambda i, *unused: (part, i)),
        pl.BlockSpec((half, rows), lambda i, *unused: (PARTS + part, 0)),
        pl.BlockSpec((half, rows), lambda i, *unused: (2 * PARTS + part, 0)),
    ]


def attend(qkv_t, seg_row, seg_col, width, part, after=()):
    rows = qkv_t.shape[1]
    half = width // PARTS
    heads = half // HEAD_DIM

    def kernel(q_ref, k_ref, v_ref, seg_r, seg_c, o_ref, lse_ref, keys, values):
        step = pl.program_id(0)

        @pl.when(step == 0)
        def first():
            shift_in(keys, k_ref[...])
            shift_in(values, v_ref[...])

        start = pl.multiple_of(step * QB, QB)
        window = pl.ds(start, KB)
        bias = window_bias(seg_r[0:1, :], seg_c[window, :])
        ats = [slice(h * HEAD_DIM, (h + 1) * HEAD_DIM) for h in range(heads)]
        scores = [tn(keys[at, window], q_ref[at, :] * BF(HEAD_DIM**-0.5)) + bias for at in ats]
        tops = [jnp.max(s, axis=0, keepdims=True) for s in scores]
        expos = [jnp.exp(s - t) for s, t in zip(scores, tops)]
        sums = [jnp.sum(e, axis=0, keepdims=True) for e in expos]
        probs = [(e * (1.0 / s)).astype(BF) for e, s in zip(expos, sums)]
        for at, p in zip(ats, probs):
            o_ref[at, :] = nn(values[at, window], p).astype(BF)
        for h, (t, s) in enumerate(zip(tops, sums)):
            lse_ref[h : h + 1, :] = t + jnp.log(s)

    return call(
        kernel,
        (rows // QB,),
        head_parts(width, rows, part) + [lanes_of((8, QB)), full(seg_col.shape)],
        [lanes_of((half, QB)), lanes_of((16, QB))],
        [jax.ShapeDtypeStruct((half, rows), BF), jax.ShapeDtypeStruct((16, rows), F32)],
        [pltpu.VMEM((half, rows + QB), BF), pltpu.VMEM((half, rows + QB), BF)],
        20,
        6,
        (qkv_t, qkv_t, qkv_t, seg_row, seg_col),
        after=after,
    )


def project_out(o_parts, tokens, vecs, pieces, places, low, rows_piece, after=()):
    rows, width = tokens.shape
    n, block = len(pieces), 256

    def kernel(at, o_a, o_b, tok, vec, *refs):
        parts, (mid_out, hid_out, weight, sem) = refs[:n], refs[n:]

        @pl.when(pl.program_id(0) == 0)
        def first():
            wait_all(load_pieces(at, parts, low, rows_piece, weight, sem))

        both = jnp.concatenate([o_a[...], o_b[...]], axis=0)
        mid = tok[...].astype(F32) + tn(both, weight[...]) + vec[4:5, :]
        mid_out[...] = mid
        hat, unused = normed(mid)
        hid_out[...] = (hat * vec[5:6, :] + vec[6:7, :]).astype(BF)

    return call(
        kernel,
        (rows // block,),
        [lanes_of((width // PARTS, block))] * PARTS + [rows_of((block, width)), full(vecs.shape)] + [ANYWHERE] * n,
        [rows_of((block, width)), rows_of((block, width))],
        [jax.ShapeDtypeStruct((rows, width), F32), jax.ShapeDtypeStruct((rows, width), BF)],
        [pltpu.VMEM((width, width), BF), pltpu.SemaphoreType.DMA((count_of(pieces),))],
        16,
        5,
        (places, *o_parts, tokens, vecs, *pieces),
        prefetch=1,
        after=after,
    )


def mlp_half(hidden, cot, bias, pieces, places, low, unit_rows, out_shapes, wide, after=()):
    rows, width = hidden.shape
    n, m, count = len(pieces), len(out_shapes), count_of(pieces)
    units = 2 * wide * unit_rows
    block = min(384, units)

    def kernel(at, hid, cot_ref, bias_ref, *refs):
        parts = refs[:n]
        act_out, grad_out, sum_out = refs[n : n + 3]
        outs = refs[n + 3 : n + 3 + m]
        up, down, d_up, d_down, sem_a, sem_b = refs[n + 3 + m :]
        step = pl.program_id(0)

        @pl.when(step == 0)
        def first():
            one = load_pieces(at, parts, low, unit_rows, up, sem_a)
            two = load_pieces(at, parts, low + unit_rows, unit_rows, down, sem_b)
            wait_all(one)
            wait_all(two)

        here = pl.ds(pl.multiple_of(step * block, block), block)
        pre = nt(up[here, :], hid[...]) + bias_ref[...]
        grad_act = nt(down[here, :], cot_ref[...])
        cdf, pdf = cdf_pdf(pre)
        act = (pre * cdf).astype(BF)
        grad = (grad_act * (cdf + pre * pdf)).astype(BF)
        act_out[...] = act
        grad_out[...] = grad
        sum_out[...] = nt(jnp.ones((8, rows), BF), grad)
        d_down[here, :] = nn(act, cot_ref[...]).astype(BF)
        d_up[here, :] = nn(grad, hid[...]).astype(BF)

        @pl.when(step == pl.num_programs(0) - 1)
        def last():
            one = store_pieces(at, d_up, unit_rows, outs, 0, sem_a)
            two = store_pieces(at, d_down, unit_rows, outs, unit_rows, sem_b)
            wait_all(one)
            wait_all(two)

    return call(
        kernel,
        (units // block,),
        [full((rows, width)), full((rows, width)), rows_of((block, 1))] + [ANYWHERE] * n,
        [rows_of((block, rows)), rows_of((block, rows)), lanes_of((8, block))] + [ANYWHERE] * m,
        [
            jax.ShapeDtypeStruct((units, rows), BF),
            jax.ShapeDtypeStruct((units, rows), BF),
            jax.ShapeDtypeStruct((8, units), F32),
            *[jax.ShapeDtypeStruct(shape, BF) for shape in out_shapes],
        ],
        [pltpu.VMEM((units, width), BF)] * 4
        + [pltpu.SemaphoreType.DMA((count,))] * 2,
        32,
        22,
        (places, hidden, cot, bias, *pieces),
        prefetch=1,
        after=after,
    )


def second_norm_back(grads, mid, cot, vecs, groups, places, unit_rows, wide, after=()):
    rows, width = mid.shape
    block = 256
    n, total_n, count = len(groups[0][0]), len(groups[0][0]) + len(groups[1][0]), count_of(groups[0][0])
    units = 2 * wide * unit_rows

    def kernel(at, ga, gb, mid_ref, cot_ref, vec, *refs):
        parts = refs[:total_n]
        out, low_out, sums, up_a, up_b, sem = refs[total_n:]
        step = pl.program_id(0)

        @pl.when(step == 0)
        def first():
            one = load_pieces(at, parts[:n], groups[0][1], unit_rows, up_a, sem.at[0])
            two = load_pieces(at, parts[n:], groups[1][1], unit_rows, up_b, sem.at[1])
            wait_all(one)
            wait_all(two)
            sums[...] = jnp.zeros_like(sums)

        grad = tn(ga[...], up_a[...]) + tn(gb[...], up_b[...])
        hat, inverse = normed(mid_ref[...])
        top = cot_ref[...].astype(F32)
        total_grad = top + norm_back(grad, hat, inverse, vec[5:6, :])
        out[...] = total_grad
        lower = total_grad.astype(BF)
        low_out[...] = lower
        sums[0:1, :] += jnp.sum(grad * hat, axis=0, keepdims=True)
        sums[1:2, :] += jnp.sum(grad, axis=0, keepdims=True)
        sums[2:3, :] += jnp.sum(lower.astype(F32), axis=0, keepdims=True)
        sums[3:4, :] += jnp.sum(top, axis=0, keepdims=True)

    return call(
        kernel,
        (rows // block,),
        [lanes_of((units, block)), lanes_of((units, block)), rows_of((block, width)), rows_of((block, width)), full(vecs.shape)]
        + [ANYWHERE] * total_n,
        [rows_of((block, width)), rows_of((block, width)), full((8, width))],
        [
            jax.ShapeDtypeStruct((rows, width), F32),
            jax.ShapeDtypeStruct((rows, width), BF),
            jax.ShapeDtypeStruct((8, width), F32),
        ],
        [pltpu.VMEM((units, width), BF)] * 2 + [pltpu.SemaphoreType.DMA((2, count))],
        32,
        14 * BACK,
        (places, *grads, mid, cot, vecs, *groups[0][0], *groups[1][0]),
        prefetch=1,
        after=after,
    )


def out_back(o_parts, grad_low, pieces, places, low_in, rows_piece, own, far, low, after=()):
    rows, width = grad_low.shape
    half = width // PARTS
    n = len(pieces)

    def kernel(at, o_a, o_b, grad, own_in, far_in, *refs):
        parts, (do_ref, own_ref, far_ref, weight, d_weight, sem) = refs[:n], refs[n:]
        copies = load_pieces(at, parts, low_in, rows_piece, weight, sem)
        d_weight[:half, :] = nn(o_a[...], grad[...]).astype(BF)
        d_weight[half:, :] = nn(o_b[...], grad[...]).astype(BF)
        wait_all(copies)
        copies = store_pieces(at, d_weight, rows_piece, (own_ref, far_ref), low, sem)
        do_ref[...] = nt(weight[...], grad[...]).astype(BF)
        wait_all(copies)

    return call(
        kernel,
        (1,),
        [full((half, rows))] * PARTS + [full((rows, width)), ANYWHERE, ANYWHERE] + [ANYWHERE] * n,
        [full((width, rows)), ANYWHERE, ANYWHERE],
        [
            jax.ShapeDtypeStruct((width, rows), BF),
            jax.ShapeDtypeStruct(own.shape, BF),
            jax.ShapeDtypeStruct(far.shape, BF),
        ],
        [pltpu.VMEM((width, width), BF)] * 2 + [pltpu.SemaphoreType.DMA((count_of(pieces),))],
        20,
        5 * BACK,
        (places, *o_parts, grad_low, own, far, *pieces),
        prefetch=1,
        aliases={4: 1, 5: 2},
        after=after,
    )


def attend_back(qkv_t, do_t, lse, seg_row, seg_col, width, part, after=()):
    rows = qkv_t.shape[1]
    half = width // PARTS
    heads = half // HEAD_DIM
    scale = HEAD_DIM**-0.5

    def kernel(q_ref, k_ref, v_ref, do_ref, lse_ref, seg_r, seg_c, out, sums, keys, values, d_keys, d_values):
        step = pl.program_id(0)

        @pl.when(step == 0)
        def first():
            shift_in(keys, k_ref[...])
            shift_in(values, v_ref[...])
            d_keys[...] = jnp.zeros_like(d_keys)
            d_values[...] = jnp.zeros_like(d_values)

        start = pl.multiple_of(step * QB, QB)
        window = pl.ds(start, KB)
        bias = window_bias(seg_r[0:1, :], seg_c[window, :])
        ats = [slice(h * HEAD_DIM, (h + 1) * HEAD_DIM) for h in range(heads)]
        queries = [q_ref[at, :] * BF(scale) for at in ats]
        raw = [tn(keys[at, window], q) for at, q in zip(ats, queries)]
        grad_probs = [tn(values[at, window], do_ref[at, :]) for at in ats]
        probs = [jnp.exp(r + (bias - lse_ref[h : h + 1, :])) for h, r in enumerate(raw)]
        weighted = [p * g for p, g in zip(probs, grad_probs)]
        deltas = [jnp.sum(w, axis=0, keepdims=True) for w in weighted]
        scores = [(w - p * d).astype(BF) for w, p, d in zip(weighted, probs, deltas)]
        for at, s in zip(ats, scores):
            out[at, pl.ds(start, QB)] = (nn(keys[at, window], s) * scale).astype(BF)
        for at, q, s in zip(ats, queries, scores):
            d_keys[at, window] += nt(q, s)
        for at, p in zip(ats, probs):
            d_values[at, window] += nt(do_ref[at, :], p.astype(BF))

        @pl.when(step == pl.num_programs(0) - 1)
        def last():
            edge = KB // 4
            out[half : 2 * half, :] = d_keys[...][:, edge : edge + rows].astype(BF)
            out[2 * half : 3 * half, :] = d_values[...][:, edge : edge + rows].astype(BF)
            sums[...] = nt(jnp.ones((8, rows), BF), out[...])

    return call(
        kernel,
        (rows // QB,),
        head_parts(width, rows, part)
        + [
            pl.BlockSpec((half, QB), lambda i, *unused: (part, i)),
            lanes_of((16, QB)),
            lanes_of((8, QB)),
            full(seg_col.shape),
        ],
        [full((3 * half, rows)), full((8, 3 * half))],
        [jax.ShapeDtypeStruct((3 * half, rows), BF), jax.ShapeDtypeStruct((8, 3 * half), F32)],
        [pltpu.VMEM((half, rows + QB), BF)] * 2 + [pltpu.VMEM((half, rows + QB), F32)] * 2,
        28,
        12 * BACK,
        (qkv_t, qkv_t, qkv_t, do_t, lse, seg_row, seg_col),
        after=after,
    )


def qkv_back(grad_parts, hidden, places, rows_piece, topo, after=()):
    rows, width = hidden.shape
    half = width // PARTS
    count = 3 * width
    sites, lanes = topo.X * topo.X, width // topo.Y

    def kernel(at, grad_a, grad_b, hid, own, far, whole, sem):
        step = pl.program_id(0)
        for part, grad in enumerate((grad_a, grad_b)):
            here = pl.ds(pl.multiple_of(step * width + part * half, half), half)
            whole[here, :] = nn(grad[...], hid[...]).astype(BF)

        @pl.when(step == pl.num_programs(0) - 1)
        def last():
            wait_all(store_pieces(at, whole, rows_piece, (own, far), 0, sem))

    piece_shape = jax.ShapeDtypeStruct((sites, topo.Z, rows_piece, lanes), BF)
    return call(
        kernel,
        (3,),
        [rows_of((half, rows))] * PARTS + [full((rows, width))],
        [ANYWHERE, ANYWHERE],
        [piece_shape, piece_shape],
        [pltpu.VMEM((count, width), BF), pltpu.SemaphoreType.DMA((2 * sites * topo.Z,))],
        24,
        7 * BACK,
        (places, *grad_parts, hidden),
        prefetch=1,
        after=after,
    )


def first_norm_back(grad_parts, tokens, grad_mid, vecs, pieces, places, rows_piece, after=()):
    rows, width = tokens.shape
    count, half = 3 * width, width // PARTS
    block = 256
    n = len(pieces)

    def kernel(at, grad_a, grad_b, tok, mid, vec, *refs):
        parts, (out, sums, weight, sem) = refs[:n], refs[n:]

        @pl.when(pl.program_id(0) == 0)
        def first():
            wait_all(load_pieces(at, parts, 0, rows_piece, weight, sem))
            sums[...] = jnp.zeros_like(sums)

        both = jnp.concatenate([g[k * half : (k + 1) * half, :] for k in range(3) for g in (grad_a, grad_b)], axis=0)
        grad = tn(both, weight[...])
        hat, inverse = normed(tok[...].astype(F32))
        out[...] = (mid[...] + norm_back(grad, hat, inverse, vec[0:1, :])).astype(BF)
        sums[0:1, :] += jnp.sum(grad * hat, axis=0, keepdims=True)
        sums[1:2, :] += jnp.sum(grad, axis=0, keepdims=True)

    return call(
        kernel,
        (rows // block,),
        [lanes_of((count // PARTS, block))] * PARTS
        + [rows_of((block, width)), rows_of((block, width)), full(vecs.shape)]
        + [ANYWHERE] * n,
        [rows_of((block, width)), full((8, width))],
        [jax.ShapeDtypeStruct((rows, width), BF), jax.ShapeDtypeStruct((8, width), F32)],
        [pltpu.VMEM((count, width), BF), pltpu.SemaphoreType.DMA((count_of(pieces),))],
        28,
        11 * BACK,
        (places, *grad_parts, tokens, grad_mid, vecs, *pieces),
        prefetch=1,
        after=after,
    )


def finish_out(acts, mid, vecs, groups, places, unit_rows, wide, after=()):
    rows, width = mid.shape
    block = 256
    n, total_n, count = len(groups[0][0]), len(groups[0][0]) + len(groups[1][0]), count_of(groups[0][0])
    units = 2 * wide * unit_rows

    def kernel(at, act_a, act_b, mid_ref, vec, *refs):
        parts = refs[:total_n]
        out, down_a, down_b, sem = refs[total_n:]

        @pl.when(pl.program_id(0) == 0)
        def first():
            one = load_pieces(at, parts[:n], groups[0][1], unit_rows, down_a, sem.at[0])
            two = load_pieces(at, parts[n:], groups[1][1], unit_rows, down_b, sem.at[1])
            wait_all(one)
            wait_all(two)

        result = tn(act_a[...], down_a[...]) + tn(act_b[...], down_b[...])
        out[...] = (mid_ref[...] + result + vec[7:8, :]).astype(BF)

    return call(
        kernel,
        (rows // block,),
        [lanes_of((units, block)), lanes_of((units, block)), rows_of((block, width)), full(vecs.shape)]
        + [ANYWHERE] * total_n,
        rows_of((block, width)),
        jax.ShapeDtypeStruct((rows, width), BF),
        [pltpu.VMEM((units, width), BF)] * 2 + [pltpu.SemaphoreType.DMA((2, count))],
        32,
        11 * BACK,
        (places, *acts, mid, vecs, *groups[0][0], *groups[1][0]),
        prefetch=1,
        after=after,
    )


def pack_vectors(sums_one, sums_two, sums_qkv, sums_up, places, topo, share, after=()):
    width = sums_one.shape[1]
    half = width // PARTS
    hidden = PARTS * sums_up[0].shape[1]
    group = hidden // (2 * topo.wide)
    unit = group // 2
    sites, deep, lanes = topo.X * topo.X, topo.Z, width // topo.Y
    lines = 8 + hidden // width

    def kernel(at, one, two, qkv_a, qkv_b, up_a, up_b, own, far, flat, ups, slots):
        flat[0:2, :] = one[0:2, :]
        for part, ref in enumerate((qkv_a, qkv_b)):
            lane = slice(part * half, (part + 1) * half)
            flat[2:3, lane] = ref[0:1, 0:half]
            flat[3:4, lane] = ref[0:1, 2 * half : 3 * half]
        flat[4:5, :] = two[2:3, :]
        flat[5:7, :] = two[0:2, :]
        flat[7:8, :] = two[3:4, :]
        for k in range(2 * topo.wide):
            for part, ref in enumerate((up_a, up_b)):
                ups[0:1, k * group + part * unit : k * group + (part + 1) * unit] = ref[0:1, k * unit : (k + 1) * unit]
        for line in range(8, lines):
            flat[line : line + 1, :] = ups[0:1, (line - 8) * width : (line - 7) * width]
        slots[...] = jnp.zeros_like(slots)
        for j in range(topo.wide * topo.narrow):
            done = 0
            while done < share:
                line, lane = divmod(j * share + done, width)
                take = min(share - done, width - lane)
                slots[j, 0:1, done : done + take] = flat[line : line + 1, lane : lane + take]
                done += take
        for j in range(2 * sites * deep):
            i, k = divmod(j, deep)
            slot = at[j, 0] * topo.narrow + at[j, 1] * 2 + at[j, 2]
            target = own.at[i, k] if i < sites else far.at[i - sites, k]
            target[...] = jnp.broadcast_to(slots[slot, 0:1, :], (16, lanes)).astype(BF)

    shape = (sites, deep, 16, lanes)
    return call(
        kernel,
        (1,),
        [full(a.shape) for a in (sums_one, sums_two, *sums_qkv, *sums_up)],
        [full(shape)] * 2,
        [jax.ShapeDtypeStruct(shape, BF)] * 2,
        [
            pltpu.VMEM((16, width), F32),
            pltpu.VMEM((8, hidden), F32),
            pltpu.VMEM((topo.wide * topo.narrow, 8, lanes), F32),
        ],
        16,
        3 * BACK,
        (places, sums_one, sums_two, *sums_qkv, *sums_up),
        prefetch=1,
        after=after,
    )


def total(first, *rest):
    result = first.astype(F32)
    for other in rest:
        result = result + other.astype(F32)
    return result


def tied(values, others):
    return lax.optimization_barrier((values, tuple(others)))[0] if others else values


class Spread:
    def __init__(self, piece, topo):
        self.topo, self.piece = topo, piece
        self.coming = tuple(send(piece, topo.zp[k]) for k in range(1, topo.Z))

    def along(self, others=()):
        stack = tied(jnp.stack((self.piece, *self.coming)), others)
        self.first = stack
        self.coming = tuple(send(stack, self.topo.ap[k]) for k in range(1, self.topo.X))

    def across(self, others=()):
        self.line = tied(jnp.stack((self.first, *self.coming)), others)
        self.coming = tuple(send(self.line, self.topo.bp[k]) for k in range(1, self.topo.X))
        self.near = send(self.line, self.topo.cp)

    def core(self, others=()):
        coming = tied(self.coming, others)
        self.pieces = [self.line, *coming, self.near, *[send(p, self.topo.cp) for p in coming]]


class Chain:
    def __init__(self, own, far, topo):
        self.topo, self.held = topo, own
        self.coming = [send(far, topo.cp)]

    def arrived(self):
        return tuple(self.coming)

    def fold(self, part=None):
        terms = (self.held, *self.coming)
        return total(*(terms if part is None else [t[part] for t in terms]))

    def stage(self, count, perms, others):
        self.held, self.coming = tied((self.held, self.coming), others)
        self.held, *sent = [self.fold(k).astype(BF) for k in range(count)]
        self.sent = tuple(sent)
        self.coming = [send(values, perms[count - 1 - k]) for k, values in enumerate(sent)]

    def across(self, others=()):
        side = self.topo.X
        split = lambda values: values.reshape(side, side, *values.shape[1:])
        self.held, self.coming = split(self.held), [split(c) for c in self.coming]
        self.stage(side, self.topo.bp, others)

    def along(self, others=()):
        self.stage(self.topo.X, self.topo.ap, others)

    def down(self, others=()):
        self.stage(self.topo.Z, self.topo.zp, others)

    def result(self, others=()):
        self.held, self.coming = tied((self.held, self.coming), others)
        return self.fold()


def tail_rows(values, rows, lanes):
    return jnp.pad(values[None], ((0, rows - 1), (0, lanes - values.shape[0])))


def fits(topo, rows, width, hidden):
    lanes = 2 * width // topo.narrow
    return (
        lanes % 128 == 0
        and rows % 256 == 0
        and (width // topo.wide) % 32 == 0
        and (hidden // topo.wide) % 64 == 0
        and 2 * P_THREE == QB
    )


def fast_device(
    tokens, qkv_weight, out_weight, up_weight, down_weight, vectors, bucket_counts, cotangent, topo
):
    rows, width = tokens.shape
    wide = topo.wide
    places = topo.origins()
    core = topo.here()[3]
    shards = [qkv_weight.astype(BF).T, out_weight.astype(BF), up_weight.astype(BF).T, down_weight.astype(BF)]
    r_qkv, r_out, r_unit = shards[0].shape[0] // 2, shards[1].shape[0] // 2, shards[2].shape[0] // 4
    lanes = 2 * out_weight.shape[1]
    halves = [jnp.concatenate([pick_half(s, 0, h) for h in range(2) for s in pair], axis=0) for pair in (shards[:2], shards[2:])]
    first = pair_up(halves[0], topo, core)
    vec_low, out_low = r_qkv, r_qkv + 16
    one = Spread(
        jnp.concatenate([first[:r_qkv], tail_rows(vectors.astype(BF), 16, lanes), first[r_qkv:]], axis=0), topo
    )
    rest = pair_up(tied(halves[1], (first,)), topo, core)
    piece_two = jnp.concatenate([rest[:r_unit], rest[2 * r_unit : 3 * r_unit]], axis=0)
    piece_three = jnp.concatenate([rest[r_unit : 2 * r_unit], rest[3 * r_unit :]], axis=0)
    one.along((rest,))
    two = Spread(tied(piece_two, one.coming), topo)
    one.across()
    two.along(one.coming)
    one.core((two.first,))
    one = one.pieces
    sites = topo.X * topo.X
    shapes_a = [(sites, topo.Z, 2 * r_unit, lanes)] * 2
    shapes_b = [(sites, topo.Z, 2 * r_unit + r_out, lanes)] * 2
    vecs, bias_qkv, *bias_up = unpack_vectors(one, places, vec_low, vectors.shape[0], width, wide, topo.narrow)
    segment = image_ids(bucket_counts[0], rows)
    seg_row = jnp.broadcast_to(segment[None], (8, rows))
    seg_col = jnp.pad(segment, (QB // 2, QB // 2), constant_values=-1)[:, None]

    two_along = two.coming
    two.across()
    hidden_one, qkv_t = project_qkv(tokens, vecs, bias_qkv, one, places, (r_qkv, wide))
    three = Spread(tied(piece_three, (hidden_one,)), topo)
    attn_a, lse_a = attend(qkv_t, seg_row, seg_col, width, 0, after=two_along)
    two.core((lse_a,))
    attn_b, lse_b = attend(qkv_t, seg_row, seg_col, width, 1)
    attn_t, lse = (attn_a, attn_b), (lse_a, lse_b)
    three.along((lse_b,))
    two = two.pieces
    mid, hidden_two = project_out(attn_t, tokens, vecs, one, places, out_low, r_out, after=(three.first,))
    three.across((hidden_two,))
    three_along = (three.line,)
    act_a, grad_a, sum_a, own_a, far_a = mlp_half(
        hidden_two, cotangent, bias_up[0], two, places, 0, r_unit, shapes_a, wide, after=three_along
    )
    three.core((sum_a,))
    three = three.pieces
    chain_a = Chain(own_a, far_a, topo)
    act_b, grad_b, sum_b, own_b, far_b = mlp_half(
        hidden_two, cotangent, bias_up[1], three, places, 0, r_unit, shapes_b, wide
    )
    chain_a.across((sum_b,))
    grad_mid, grad_mid_low, sums_two = second_norm_back(
        (grad_a, grad_b), mid, cotangent, vecs, ((two, 0), (three, 0)), places, r_unit, wide,
        after=chain_a.sent,
    )
    do_t, own_b, far_b = out_back(attn_t, grad_mid_low, one, places, out_low, r_out, own_b, far_b, 2 * r_unit)
    chain_b = Chain(own_b, far_b, topo)
    chain_a.along((do_t,))
    grads_0, sums_0 = attend_back(qkv_t, do_t, lse[0], seg_row, seg_col, width, 0, after=chain_a.sent)
    chain_a.down((sums_0,))
    chain_b.across((sums_0,))
    grads_1, sums_1 = attend_back(
        qkv_t, do_t, lse[1], seg_row, seg_col, width, 1, after=chain_a.sent + chain_b.sent
    )
    grad_t = (grads_0, grads_1)
    own_q, far_q = qkv_back(grad_t, hidden_one, places, r_qkv, topo, after=chain_a.arrived())
    chain_q = Chain(own_q, far_q, topo)
    chain_b.along((far_q,))
    chain_q.across()
    input_grad, sums_one = first_norm_back(
        grad_t, tokens, grad_mid, vecs, one, places, r_qkv, after=chain_q.sent + chain_b.sent
    )
    chain_q.along((sums_one,))
    chain_b.down((sums_one,))
    own_v, far_v = pack_vectors(
        sums_one, sums_two, (sums_0, sums_1), (sum_a, sum_b), places, topo, vectors.shape[0], after=chain_q.sent
    )
    chain_v = Chain(own_v, far_v, topo)
    chain_v.across()
    chain_q.down()
    block_out = finish_out(
        (act_a, act_b), mid, vecs, ((two, r_unit), (three, r_unit)), places, r_unit, wide,
        after=chain_q.sent + chain_v.sent,
    )
    chain_v.along((block_out,))
    chain_v.down()
    part_a, part_b, part_q = chain_a.result((sums_one,)), chain_b.result((block_out,)), chain_q.result((block_out,))
    vector_grad = chain_v.result()[0, : vectors.shape[0]]
    down = jnp.concatenate([part_a[r_unit:], part_b[r_unit : 2 * r_unit]], axis=0)
    up = jnp.concatenate([part_a[:r_unit], part_b[:r_unit]], axis=0)
    out = part_b[2 * r_unit :]
    grads = [unpair(g, topo, core) for g in (part_q, out, up, down)]
    return (block_out, input_grad, grads[0].T, grads[1], grads[2].T, grads[3], vector_grad)


def per_device(
    tokens, qkv_weight, out_weight, up_weight, down_weight, vectors, bucket_counts, cotangent
):
    topo = Topo(lax.axis_size("wide"), lax.axis_size("narrow"))
    operands = (tokens, qkv_weight, out_weight, up_weight, down_weight, vectors, bucket_counts, cotangent)
    if fits(topo, *tokens.shape, up_weight.shape[1] * topo.wide):
        return fast_device(*operands, topo)
    return plain_device(*operands)


def plain_device(
    tokens, qkv_weight, out_weight, up_weight, down_weight, vectors, bucket_counts, cotangent
):
    rows, width = tokens.shape
    halves = (
        lax.all_gather(qkv_weight.astype(jnp.bfloat16), "narrow", axis=0, tiled=True),
        lax.all_gather(out_weight.astype(jnp.bfloat16), "narrow", axis=1, tiled=True),
        lax.all_gather(up_weight.astype(jnp.bfloat16), "narrow", axis=0, tiled=True),
        lax.all_gather(down_weight.astype(jnp.bfloat16), "narrow", axis=1, tiled=True),
        lax.all_gather(vectors.astype(jnp.bfloat16), "narrow", axis=0, tiled=True),
    )
    wholes = (
        lax.all_gather(halves[0], "wide", axis=1, tiled=True),
        lax.all_gather(halves[1], "wide", axis=0, tiled=True),
        lax.all_gather(halves[2], "wide", axis=1, tiled=True),
        lax.all_gather(halves[3], "wide", axis=0, tiled=True),
        lax.all_gather(halves[4], "wide", axis=0, tiled=True),
    )
    qkv_full, out_full, up_full, down_full, packed = wholes
    params = packed.astype(jnp.float32)
    gain_one = params[0:width]
    shift_one = params[width : 2 * width]
    bias_query = params[2 * width : 3 * width]
    bias_value = params[3 * width : 4 * width]
    bias_out = params[4 * width : 5 * width]
    gain_two = params[5 * width : 6 * width]
    shift_two = params[6 * width : 7 * width]
    bias_down = params[7 * width : 8 * width]
    bias_up = params[8 * width :]
    inputs = tokens.astype(jnp.float32)
    hidden_one = layer_norm(inputs, gain_one, shift_one).astype(jnp.bfloat16)
    qkv_bias = jnp.concatenate([bias_query, jnp.zeros((width,), jnp.float32), bias_value])
    qkv_all = (jnp.dot(hidden_one, qkv_full, preferred_element_type=jnp.float32) + qkv_bias).astype(
        jnp.bfloat16
    )
    margin = P_THREE
    blocks = rows // QROWS
    span = QROWS + 2 * margin
    scale = HEAD_DIM ** (-0.5)
    query_blk = qkv_all[:, :width].reshape(blocks, QROWS, HEADS, HEAD_DIM)
    keys_win = windows_of(qkv_all[:, width : 2 * width], margin, blocks, 0).reshape(
        blocks, span, HEADS, HEAD_DIM
    )
    values_win = windows_of(qkv_all[:, 2 * width :], margin, blocks, 0).reshape(
        blocks, span, HEADS, HEAD_DIM
    )
    segment = image_ids(bucket_counts[0], rows)
    seg_rows = segment.reshape(blocks, QROWS)
    seg_cols = windows_of(segment, margin, blocks, -1)
    same = seg_rows[:, None, :, None] == seg_cols[:, None, None, :]
    raw = (
        jnp.einsum("bqhd,bkhd->bhqk", query_blk, keys_win, preferred_element_type=jnp.float32)
        * scale
    )
    masked = jnp.where(same, raw, NEG)
    top = jnp.max(masked, axis=3, keepdims=True)
    expo = jnp.exp(masked - top)
    total = jnp.sum(expo, axis=3, keepdims=True)
    probs_low = (expo / total).astype(jnp.bfloat16)
    log_total = top + jnp.log(total)
    attended = jnp.einsum(
        "bhqk,bkhd->bqhd", probs_low, values_win, preferred_element_type=jnp.float32
    )
    attn_low = attended.reshape(rows, width).astype(jnp.bfloat16)
    mid = inputs + jnp.dot(attn_low, out_full, preferred_element_type=jnp.float32) + bias_out
    hidden_two = layer_norm(mid, gain_two, shift_two).astype(jnp.bfloat16)
    pre_act = jnp.dot(hidden_two, up_full, preferred_element_type=jnp.float32) + bias_up
    activated = gelu_exact(pre_act).astype(jnp.bfloat16)
    output = mid + jnp.dot(activated, down_full, preferred_element_type=jnp.float32) + bias_down
    block_out = output.astype(jnp.bfloat16)
    grad_top = cotangent.astype(jnp.float32)
    d_down = contract_rows(activated, cotangent)
    d_bias_down = jnp.sum(grad_top, axis=0)
    grad_act = contract_cols(cotangent, down_full)
    unused_act, gelu_back = jax.vjp(gelu_exact, pre_act)
    grad_pre = gelu_back(grad_act)[0].astype(jnp.bfloat16)
    d_up = contract_rows(hidden_two, grad_pre)
    d_bias_up = jnp.sum(grad_pre.astype(jnp.float32), axis=0)
    grad_hidden_two = contract_cols(grad_pre, up_full)
    unused_two, norm_back_two = jax.vjp(layer_norm, mid, gain_two, shift_two)
    grad_mid_part, d_gain_two, d_shift_two = norm_back_two(grad_hidden_two)
    grad_mid = grad_top + grad_mid_part
    grad_mid_low = grad_mid.astype(jnp.bfloat16)
    d_out = contract_rows(attn_low, grad_mid_low)
    d_bias_out = jnp.sum(grad_mid_low.astype(jnp.float32), axis=0)
    grad_attn = contract_cols(grad_mid_low, out_full).astype(jnp.bfloat16)
    raw_again = (
        jnp.einsum("bqhd,bkhd->bhqk", query_blk, keys_win, preferred_element_type=jnp.float32)
        * scale
    )
    probs = jnp.exp(jnp.where(same, raw_again, NEG) - log_total)
    grad_blk = grad_attn.reshape(blocks, QROWS, HEADS, HEAD_DIM)
    grad_probs = jnp.einsum(
        "bqhd,bkhd->bhqk", grad_blk, values_win, preferred_element_type=jnp.float32
    )
    grad_scores = (
        probs * (grad_probs - jnp.sum(probs * grad_probs, axis=3, keepdims=True))
    ).astype(jnp.bfloat16)
    grad_query = (
        jnp.einsum("bhqk,bkhd->bqhd", grad_scores, keys_win, preferred_element_type=jnp.float32)
        * scale
    )
    grad_keys_win = (
        jnp.einsum("bhqk,bqhd->bkhd", grad_scores, query_blk, preferred_element_type=jnp.float32)
        * scale
    )
    grad_values_win = jnp.einsum(
        "bhqk,bqhd->bkhd", probs.astype(jnp.bfloat16), grad_blk, preferred_element_type=jnp.float32
    )
    grad_keys = fold_windows(grad_keys_win.reshape(blocks, span, width), margin, QROWS)
    grad_values = fold_windows(grad_values_win.reshape(blocks, span, width), margin, QROWS)
    grad_qkv = jnp.concatenate(
        [grad_query.reshape(rows, width), grad_keys, grad_values], axis=1
    ).astype(jnp.bfloat16)
    d_qkv = contract_rows(hidden_one, grad_qkv)
    column_sums = jnp.sum(grad_qkv.astype(jnp.float32), axis=0)
    grad_hidden_one = contract_cols(grad_qkv, qkv_full)
    unused_one, norm_back_one = jax.vjp(layer_norm, inputs, gain_one, shift_one)
    grad_in_part, d_gain_one, d_shift_one = norm_back_one(grad_hidden_one)
    input_grad = (grad_mid + grad_in_part).astype(jnp.bfloat16)
    d_vector = jnp.concatenate(
        [
            d_gain_one,
            d_shift_one,
            column_sums[:width],
            column_sums[2 * width :],
            d_bias_out,
            d_gain_two,
            d_shift_two,
            d_bias_down,
            d_bias_up,
        ]
    )
    partial_sums = (
        lax.psum_scatter(
            d_qkv.astype(jnp.bfloat16), "wide", scatter_dimension=1, tiled=True
        ).astype(jnp.float32),
        lax.psum_scatter(
            d_out.astype(jnp.bfloat16), "wide", scatter_dimension=0, tiled=True
        ).astype(jnp.float32),
        lax.psum_scatter(d_up.astype(jnp.bfloat16), "wide", scatter_dimension=1, tiled=True).astype(
            jnp.float32
        ),
        lax.psum_scatter(
            d_down.astype(jnp.bfloat16), "wide", scatter_dimension=0, tiled=True
        ).astype(jnp.float32),
        lax.psum_scatter(
            d_vector.astype(jnp.bfloat16), "wide", scatter_dimension=0, tiled=True
        ).astype(jnp.float32),
    )
    final = (
        lax.psum_scatter(
            partial_sums[0].astype(jnp.bfloat16), "narrow", scatter_dimension=0, tiled=True
        ).astype(jnp.float32),
        lax.psum_scatter(
            partial_sums[1].astype(jnp.bfloat16), "narrow", scatter_dimension=1, tiled=True
        ).astype(jnp.float32),
        lax.psum_scatter(
            partial_sums[2].astype(jnp.bfloat16), "narrow", scatter_dimension=0, tiled=True
        ).astype(jnp.float32),
        lax.psum_scatter(
            partial_sums[3].astype(jnp.bfloat16), "narrow", scatter_dimension=1, tiled=True
        ).astype(jnp.float32),
        lax.psum_scatter(
            partial_sums[4].astype(jnp.bfloat16), "narrow", scatter_dimension=0, tiled=True
        ).astype(jnp.float32),
    )
    return (block_out, input_grad, final[0], final[1], final[2], final[3], final[4])


def solution(mesh):
    return jax.shard_map(
        per_device,
        mesh=mesh,
        in_specs=(
            P(("wide", "narrow"), None),
            P("narrow", "wide"),
            P("wide", "narrow"),
            P("narrow", "wide"),
            P("wide", "narrow"),
            P(("wide", "narrow")),
            P(("wide", "narrow"), None),
            P(("wide", "narrow"), None),
        ),
        out_specs=(
            P(("wide", "narrow"), None),
            P(("wide", "narrow"), None),
            P("narrow", "wide"),
            P("wide", "narrow"),
            P("narrow", "wide"),
            P("wide", "narrow"),
            P(("wide", "narrow")),
        ),
        check_vma=False,
    )
```

```python
import math

import jax
import jax.numpy as jnp
from jax import lax
from jax.experimental import pallas as pl
from jax.experimental.pallas import tpu as pltpu
from jax.sharding import PartitionSpec as P

HEADS = 12
HEAD_DIM = 64
QROWS = 512
P_ONE = 25
P_TWO = 49
P_THREE = 64


EPS = 1e-06
NEG = -1e30


def layer_norm(values, gain, shift):
    center = values - jnp.mean(values, axis=-1, keepdims=True)
    spread = jnp.mean(center * center, axis=-1, keepdims=True)
    return center * lax.rsqrt(spread + EPS) * gain + shift


def image_ids(counts, rows):
    place = jnp.arange(rows, dtype=jnp.int32)
    first = counts[0] * P_ONE
    second = first + counts[1] * P_TWO
    bucket = (place >= first).astype(jnp.int32) + (place >= second).astype(jnp.int32)
    start = jnp.where(bucket == 0, 0, jnp.where(bucket == 1, first, second))
    length = jnp.where(bucket == 0, P_ONE, jnp.where(bucket == 1, P_TWO, P_THREE)).astype(jnp.int32)
    return bucket * rows + (place - start) // length


def gelu_exact(values):
    return jax.nn.gelu(values, approximate=False)


def contract_rows(left, right):
    return lax.dot_general(
        left, right, (((0,), (0,)), ((), ())), preferred_element_type=jnp.float32
    )


def contract_cols(left, right):
    return lax.dot_general(
        left, right, (((1,), (1,)), ((), ())), preferred_element_type=jnp.float32
    )


def windows_of(values, margin, blocks, fill):
    rows = values.shape[0]
    block_rows = rows // blocks
    rest = values.shape[1:]
    padded = jnp.pad(
        values, ((margin, margin),) + tuple(((0, 0) for unused in rest)), constant_values=fill
    )
    before = padded[:rows].reshape((blocks, block_rows) + rest)[:, :margin]
    middle = values.reshape((blocks, block_rows) + rest)
    after = padded[2 * margin : 2 * margin + rows].reshape((blocks, block_rows) + rest)[
        :, block_rows - margin :
    ]
    return jnp.concatenate([before, middle, after], axis=1)


def fold_windows(grads, margin, block_rows):
    blocks = grads.shape[0]
    width = grads.shape[2]
    middle = grads[:, margin : margin + block_rows]
    before = jnp.pad(grads[1:, :margin], ((0, 1), (block_rows - margin, 0), (0, 0)))
    after = jnp.pad(grads[:-1, margin + block_rows :], ((1, 0), (0, block_rows - margin), (0, 0)))
    return (middle + before + after).reshape(blocks * block_rows, width)


BF = jnp.bfloat16
F32 = jnp.float32
AXES = ("wide", "narrow")


class Topo:
    def __init__(self, wide, narrow):
        self.wide, self.narrow = wide, narrow
        self.Y = narrow // 2
        self.X = self.Y
        self.Z = wide // self.X
        side, deep = self.X, self.Z
        self.zp = [self.perm(lambda z, x, y, c, k=k: ((z + k) % deep, x, y, c)) for k in range(deep)]
        self.ap = [
            self.perm(
                lambda z, x, y, c, k=k: (z, (x + k) % side, y, c) if c == 0 else (z, x, (y + k) % side, c)
            )
            for k in range(side)
        ]
        self.bp = [
            self.perm(
                lambda z, x, y, c, k=k: (z, x, (y + k) % side, c) if c == 0 else (z, (x + k) % side, y, c)
            )
            for k in range(side)
        ]
        self.cp = self.perm(lambda z, x, y, c: (z, x, y, 1 - c))

    def did(self, z, x, y, c):
        return ((z * self.X + x) * self.Y + y) * 2 + c

    def perm(self, target):
        return [
            (self.did(z, x, y, c), self.did(*target(z, x, y, c)))
            for z in range(self.Z)
            for x in range(self.X)
            for y in range(self.Y)
            for c in range(2)
        ]

    def here(self):
        wide, narrow = lax.axis_index("wide"), lax.axis_index("narrow")
        return wide // self.X, wide % self.X, narrow // 2, narrow % 2

    def origins(self):
        z0, x0, y0, c0 = self.here()
        side, deep = self.X, self.Z
        index = jnp.arange(2 * side * side * deep, dtype=jnp.int32)
        kz, ka, kb = index % deep, index // deep % side, index // (deep * side) % side
        c = (c0 + index // (deep * side * side)) % 2
        x = (x0 + side - jnp.where(c == 0, ka, kb)) % side
        y = (y0 + side - jnp.where(c == 0, kb, ka)) % side
        z = (z0 + deep - kz) % deep
        return jnp.stack([z * side + x, y, c], axis=1).astype(jnp.int32)


def send(values, perm):
    return lax.ppermute(values, AXES, perm)


def pick_half(values, axis, index):
    half = values.shape[axis] // 2
    return lax.dynamic_slice_in_dim(values, index * half, half, axis)


def pair_up(shard, topo, core):
    mine = pick_half(shard, 0, core)
    other = send(pick_half(shard, 0, 1 - core), topo.cp)
    first = jnp.where(core == 0, mine, other)
    second = jnp.where(core == 0, other, mine)
    return jnp.concatenate([first, second], axis=1)


def unpair(piece, topo, core):
    mine = pick_half(piece, 1, core)
    other = send(pick_half(piece, 1, 1 - core), topo.cp)
    first = jnp.where(core == 0, mine, other)
    second = jnp.where(core == 0, other, mine)
    return jnp.concatenate([first, second], axis=0)


def gather(piece, topo):
    stack = jnp.stack([piece] + [send(piece, topo.zp[k]) for k in range(1, topo.Z)])
    line = [stack] + [send(stack, topo.ap[k]) for k in range(1, topo.X)]
    own = [p for k in range(topo.X) for p in (line if k == 0 else [send(q, topo.bp[k]) for q in line])]
    return own + [send(p, topo.cp) for p in own]


def nn(a, b):
    return lax.dot_general(a, b, (((1,), (0,)), ((), ())), preferred_element_type=F32)


def nt(a, b):
    return lax.dot_general(a, b, (((1,), (1,)), ((), ())), preferred_element_type=F32)


def tn(a, b):
    return lax.dot_general(a, b, (((0,), (0,)), ((), ())), preferred_element_type=F32)


def normed(values):
    center = values - jnp.mean(values, axis=-1, keepdims=True)
    spread = jnp.mean(center * center, axis=-1, keepdims=True)
    inverse = lax.rsqrt(spread + EPS)
    return center * inverse, inverse


def norm_back(grad, hat, inverse, gain):
    scaled = grad * gain
    first = jnp.mean(scaled, axis=-1, keepdims=True)
    second = jnp.mean(scaled * hat, axis=-1, keepdims=True)
    return inverse * (scaled - first - hat * second)


ROOT_HALF = 0.7071067811865476
ROOT_TAU = 0.3989422804014327
MIB = 1024 * 1024
WIDTH = HEADS * HEAD_DIM
SCALE = 1.0
BACK = 5


def cdf_pdf(u):
    bell = jnp.exp(-0.5 * (u * u))
    t = 1.0 / (1.0 + (0.3275911 * ROOT_HALF) * jnp.abs(u))
    poly = 1.061405429 * 0.5
    for coef in (-1.453152027, 1.421413741, -0.284496736, 0.254829592):
        poly = poly * t + coef * 0.5
    upper = poly * t * bell
    return jnp.where(u < 0, upper, 1.0 - upper), ROOT_TAU * bell


def call(kernel, grid, in_specs, out_specs, out_shape, scratch, vmem, us, operands, prefetch=0, aliases=None, after=()):
    first, count = len(operands), len(after)

    def body(*refs):
        kernel(*refs[:first], *refs[first + count :])

    return pl.pallas_call(
        body,
        grid_spec=pltpu.PrefetchScalarGridSpec(
            num_scalar_prefetch=prefetch,
            grid=grid,
            in_specs=in_specs + [ANYWHERE] * count,
            out_specs=out_specs,
            scratch_shapes=scratch,
        ),
        out_shape=out_shape,
        input_output_aliases=aliases or {},
        compiler_params=pltpu.CompilerParams(vmem_limit_bytes=vmem * MIB),
        cost_estimate=pl.CostEstimate(flops=int(us * SCALE * 1.0e9), bytes_accessed=int(us * SCALE * 3.0e6), transcendentals=0),
    )(*operands, *after)


ANYWHERE = pl.BlockSpec(memory_space=pltpu.HBM)


def full(shape):
    return pl.BlockSpec(shape, lambda *unused: (0,) * len(shape))


def rows_of(shape):
    return pl.BlockSpec(shape, lambda i, *unused: (i,) + (0,) * (len(shape) - 1))


def lanes_of(shape):
    return pl.BlockSpec(shape, lambda i, *unused: (0, i))


def piece_place(at, j, rows, lanes):
    row = pl.multiple_of((at[j, 0] * 2 + at[j, 2]) * rows, 16)
    lane = pl.multiple_of(at[j, 1] * lanes, 128)
    return pl.ds(row, rows), pl.ds(lane, lanes)


def sites_of(at, pieces, rows, lanes):
    if len(pieces) == 1:
        (piece,) = pieces
        narrow = 2 * (WIDTH // lanes)
        for j in range(piece.shape[0]):
            wide, y, core = j // narrow, j % narrow // 2, j % 2
            yield piece.at[j], (pl.ds((wide * 2 + core) * rows, rows), pl.ds(y * lanes, lanes))
    else:
        side, deep = pieces[0].shape[:2]
        for i, piece in enumerate(pieces):
            for a in range(side):
                for k in range(deep):
                    yield piece.at[a, k], piece_place(at, (i * side + a) * deep + k, rows, lanes)


def count_of(pieces):
    return len(pieces) * math.prod(pieces[0].shape[:-2])


def load_pieces(at, pieces, low, rows, whole, sem):
    copies = []
    for j, (piece, place) in enumerate(sites_of(at, pieces, rows, pieces[0].shape[-1])):
        copy = pltpu.make_async_copy(piece.at[pl.ds(low, rows), :], whole.at[place], sem.at[j])
        copy.start()
        copies.append(copy)
    return copies


def store_pieces(at, whole, rows, outs, low, sem):
    copies = []
    for j, (piece, place) in enumerate(sites_of(at, outs, rows, outs[0].shape[-1])):
        copy = pltpu.make_async_copy(whole.at[place], piece.at[pl.ds(low, rows), :], sem.at[j])
        copy.start()
        copies.append(copy)
    return copies


def wait_all(copies):
    for copy in copies:
        copy.wait()


def unpack_vectors(pieces, places, low, share, width, wide, narrow):
    n, lanes = len(pieces), pieces[0].shape[-1]
    hidden = wide * narrow * share - 8 * width
    group = hidden // (2 * wide)
    unit = group // 2
    lines = 8 + hidden // width

    def kernel(at, *refs):
        parts, (vecs, bias, up_a, up_b, slots, flat, sem) = refs[:n], refs[n:]
        copies = []
        for j, (piece, unused) in enumerate(sites_of(at, parts, 16, lanes)):
            slot = at[j, 0] * narrow + at[j, 1] * 2 + at[j, 2]
            copy = pltpu.make_async_copy(piece.at[pl.ds(low, 16), :], slots.at[slot], sem.at[j])
            copy.start()
            copies.append(copy)
        wait_all(copies)
        for j in range(wide * narrow):
            values = slots[j].astype(F32)[0:1, :]
            done = 0
            while done < share:
                line, lane = divmod(j * share + done, width)
                take = min(share - done, width - lane)
                flat[line : line + 1, lane : lane + take] = values[:, done : done + take]
                done += take
        vecs[...] = flat[0:8, :]
        columns = lambda line: jnp.broadcast_to(flat[line : line + 1, :], (128, width)).T[:, 0:1]
        bias[0:width, :] = columns(2)
        bias[width : 2 * width, :] = jnp.zeros((width, 1), F32)
        bias[2 * width :, :] = columns(3)
        up = jnp.concatenate([columns(line) for line in range(8, lines)], axis=0)
        for k in range(2 * wide):
            up_a[k * unit : (k + 1) * unit, :] = up[k * group : k * group + unit, :]
            up_b[k * unit : (k + 1) * unit, :] = up[k * group + unit : (k + 1) * group, :]

    column = jax.ShapeDtypeStruct((hidden // 2, 1), F32)
    return call(
        kernel,
        (1,),
        [ANYWHERE] * n,
        [full((8, width)), full((3 * width, 1)), full(column.shape), full(column.shape)],
        [jax.ShapeDtypeStruct((8, width), F32), jax.ShapeDtypeStruct((3 * width, 1), F32), column, column],
        [
            pltpu.VMEM((wide * narrow, 16, lanes), BF),
            pltpu.VMEM((16, width), F32),
            pltpu.SemaphoreType.DMA((count_of(pieces),)),
        ],
        16,
        3,
        (places, *pieces),
        prefetch=1,
    )


def project_qkv(tokens, vecs, bias, pieces, places, shape, after=()):
    rows, width = tokens.shape
    half, wide = shape
    n, block, steps = len(pieces), 256, 3 * width // 256

    def kernel(at, tok, vec, bias_ref, *refs):
        parts, (hid_out, out, weight, hid, sem) = refs[:n], refs[n:]
        step = pl.program_id(0)

        @pl.when(step == 0)
        def first():
            copies = load_pieces(at, parts, 0, half, weight, sem)
            hat, unused = normed(tok[...].astype(F32))
            hid[...] = (hat * vec[0:1, :] + vec[1:2, :]).astype(BF)
            hid_out[...] = hid[...]
            wait_all(copies)

        start = pl.multiple_of(step * block, block)
        out[...] = (nt(weight[pl.ds(start, block), :], hid[...]) + bias_ref[...]).astype(BF)

    return call(
        kernel,
        (steps,),
        [full((rows, width)), full(vecs.shape), rows_of((block, 1))] + [ANYWHERE] * n,
        [full((rows, width)), rows_of((block, rows))],
        [jax.ShapeDtypeStruct((rows, width), BF), jax.ShapeDtypeStruct((3 * width, rows), BF)],
        [
            pltpu.VMEM((3 * width, width), BF),
            pltpu.VMEM((rows, width), BF),
            pltpu.SemaphoreType.DMA((count_of(pieces),)),
        ],
        20,
        9,
        (places, tokens, vecs, bias, *pieces),
        prefetch=1,
        after=after,
    )


QB = 128
KB = 256
PARTS = 2


def window_bias(seg_row, seg_col):
    return jnp.where(seg_col == seg_row, 0.0, NEG).astype(F32)


def shift_in(dst, src):
    count, rows = src.shape
    half = KB // 4
    zero = jnp.zeros((count, half), src.dtype)
    dst[...] = jnp.concatenate([zero, src, zero], axis=1)


def head_parts(width, rows, part):
    half = width // PARTS
    return [
        pl.BlockSpec((half, QB), lambda i, *unused: (part, i)),
        pl.BlockSpec((half, rows), lambda i, *unused: (PARTS + part, 0)),
        pl.BlockSpec((half, rows), lambda i, *unused: (2 * PARTS + part, 0)),
    ]


def attend(qkv_t, seg_row, seg_col, width, part, after=()):
    rows = qkv_t.shape[1]
    half = width // PARTS
    heads = half // HEAD_DIM

    def kernel(q_ref, k_ref, v_ref, seg_r, seg_c, o_ref, lse_ref, keys, values):
        step = pl.program_id(0)

        @pl.when(step == 0)
        def first():
            shift_in(keys, k_ref[...])
            shift_in(values, v_ref[...])

        start = pl.multiple_of(step * QB, QB)
        window = pl.ds(start, KB)
        bias = window_bias(seg_r[0:1, :], seg_c[window, :])
        ats = [slice(h * HEAD_DIM, (h + 1) * HEAD_DIM) for h in range(heads)]
        scores = [tn(keys[at, window], q_ref[at, :] * BF(HEAD_DIM**-0.5)) + bias for at in ats]
        tops = [jnp.max(s, axis=0, keepdims=True) for s in scores]
        expos = [jnp.exp(s - t) for s, t in zip(scores, tops)]
        sums = [jnp.sum(e, axis=0, keepdims=True) for e in expos]
        probs = [(e * (1.0 / s)).astype(BF) for e, s in zip(expos, sums)]
        for at, p in zip(ats, probs):
            o_ref[at, :] = nn(values[at, window], p).astype(BF)
        for h, (t, s) in enumerate(zip(tops, sums)):
            lse_ref[h : h + 1, :] = t + jnp.log(s)

    return call(
        kernel,
        (rows // QB,),
        head_parts(width, rows, part) + [lanes_of((8, QB)), full(seg_col.shape)],
        [lanes_of((half, QB)), lanes_of((16, QB))],
        [jax.ShapeDtypeStruct((half, rows), BF), jax.ShapeDtypeStruct((16, rows), F32)],
        [pltpu.VMEM((half, rows + QB), BF), pltpu.VMEM((half, rows + QB), BF)],
        20,
        6,
        (qkv_t, qkv_t, qkv_t, seg_row, seg_col),
        after=after,
    )


def project_out(o_parts, tokens, vecs, pieces, places, low, rows_piece, after=()):
    rows, width = tokens.shape
    n, block = len(pieces), 256

    def kernel(at, o_a, o_b, tok, vec, *refs):
        parts, (mid_out, hid_out, weight, sem) = refs[:n], refs[n:]

        @pl.when(pl.program_id(0) == 0)
        def first():
            wait_all(load_pieces(at, parts, low, rows_piece, weight, sem))

        both = jnp.concatenate([o_a[...], o_b[...]], axis=0)
        mid = tok[...].astype(F32) + tn(both, weight[...]) + vec[4:5, :]
        mid_out[...] = mid
        hat, unused = normed(mid)
        hid_out[...] = (hat * vec[5:6, :] + vec[6:7, :]).astype(BF)

    return call(
        kernel,
        (rows // block,),
        [lanes_of((width // PARTS, block))] * PARTS + [rows_of((block, width)), full(vecs.shape)] + [ANYWHERE] * n,
        [rows_of((block, width)), rows_of((block, width))],
        [jax.ShapeDtypeStruct((rows, width), F32), jax.ShapeDtypeStruct((rows, width), BF)],
        [pltpu.VMEM((width, width), BF), pltpu.SemaphoreType.DMA((count_of(pieces),))],
        16,
        5,
        (places, *o_parts, tokens, vecs, *pieces),
        prefetch=1,
        after=after,
    )


def mlp_half(hidden, cot, bias, pieces, places, low, unit_rows, out_shapes, wide, after=()):
    rows, width = hidden.shape
    n, m, count = len(pieces), len(out_shapes), count_of(pieces)
    units = 2 * wide * unit_rows
    block = min(384, units)

    def kernel(at, hid, cot_ref, bias_ref, *refs):
        parts = refs[:n]
        act_out, grad_out, sum_out = refs[n : n + 3]
        outs = refs[n + 3 : n + 3 + m]
        up, down, d_up, d_down, sem_a, sem_b = refs[n + 3 + m :]
        step = pl.program_id(0)

        @pl.when(step == 0)
        def first():
            one = load_pieces(at, parts, low, unit_rows, up, sem_a)
            two = load_pieces(at, parts, low + unit_rows, unit_rows, down, sem_b)
            wait_all(one)
            wait_all(two)

        here = pl.ds(pl.multiple_of(step * block, block), block)
        pre = nt(up[here, :], hid[...]) + bias_ref[...]
        grad_act = nt(down[here, :], cot_ref[...])
        cdf, pdf = cdf_pdf(pre)
        act = (pre * cdf).astype(BF)
        grad = (grad_act * (cdf + pre * pdf)).astype(BF)
        act_out[...] = act
        grad_out[...] = grad
        sum_out[...] = nt(jnp.ones((8, rows), BF), grad)
        d_down[here, :] = nn(act, cot_ref[...]).astype(BF)
        d_up[here, :] = nn(grad, hid[...]).astype(BF)

        @pl.when(step == pl.num_programs(0) - 1)
        def last():
            one = store_pieces(at, d_up, unit_rows, outs, 0, sem_a)
            two = store_pieces(at, d_down, unit_rows, outs, unit_rows, sem_b)
            wait_all(one)
            wait_all(two)

    return call(
        kernel,
        (units // block,),
        [full((rows, width)), full((rows, width)), rows_of((block, 1))] + [ANYWHERE] * n,
        [rows_of((block, rows)), rows_of((block, rows)), lanes_of((8, block))] + [ANYWHERE] * m,
        [
            jax.ShapeDtypeStruct((units, rows), BF),
            jax.ShapeDtypeStruct((units, rows), BF),
            jax.ShapeDtypeStruct((8, units), F32),
            *[jax.ShapeDtypeStruct(shape, BF) for shape in out_shapes],
        ],
        [pltpu.VMEM((units, width), BF)] * 4
        + [pltpu.SemaphoreType.DMA((count,))] * 2,
        32,
        22,
        (places, hidden, cot, bias, *pieces),
        prefetch=1,
        after=after,
    )


def second_norm_back(grads, mid, cot, vecs, groups, places, unit_rows, wide, after=()):
    rows, width = mid.shape
    block = 256
    n, total_n, count = len(groups[0][0]), len(groups[0][0]) + len(groups[1][0]), count_of(groups[0][0])
    units = 2 * wide * unit_rows

    def kernel(at, ga, gb, mid_ref, cot_ref, vec, *refs):
        parts = refs[:total_n]
        out, low_out, sums, up_a, up_b, sem = refs[total_n:]
        step = pl.program_id(0)

        @pl.when(step == 0)
        def first():
            one = load_pieces(at, parts[:n], groups[0][1], unit_rows, up_a, sem.at[0])
            two = load_pieces(at, parts[n:], groups[1][1], unit_rows, up_b, sem.at[1])
            wait_all(one)
            wait_all(two)
            sums[...] = jnp.zeros_like(sums)

        grad = tn(ga[...], up_a[...]) + tn(gb[...], up_b[...])
        hat, inverse = normed(mid_ref[...])
        top = cot_ref[...].astype(F32)
        total_grad = top + norm_back(grad, hat, inverse, vec[5:6, :])
        out[...] = total_grad
        lower = total_grad.astype(BF)
        low_out[...] = lower
        sums[0:1, :] += jnp.sum(grad * hat, axis=0, keepdims=True)
        sums[1:2, :] += jnp.sum(grad, axis=0, keepdims=True)
        sums[2:3, :] += jnp.sum(lower.astype(F32), axis=0, keepdims=True)
        sums[3:4, :] += jnp.sum(top, axis=0, keepdims=True)

    return call(
        kernel,
        (rows // block,),
        [lanes_of((units, block)), lanes_of((units, block)), rows_of((block, width)), rows_of((block, width)), full(vecs.shape)]
        + [ANYWHERE] * total_n,
        [rows_of((block, width)), rows_of((block, width)), full((8, width))],
        [
            jax.ShapeDtypeStruct((rows, width), F32),
            jax.ShapeDtypeStruct((rows, width), BF),
            jax.ShapeDtypeStruct((8, width), F32),
        ],
        [pltpu.VMEM((units, width), BF)] * 2 + [pltpu.SemaphoreType.DMA((2, count))],
        32,
        14 * BACK,
        (places, *grads, mid, cot, vecs, *groups[0][0], *groups[1][0]),
        prefetch=1,
        after=after,
    )


def out_back(o_parts, grad_low, pieces, places, low_in, rows_piece, own, far, low, after=()):
    rows, width = grad_low.shape
    half = width // PARTS
    n = len(pieces)

    def kernel(at, o_a, o_b, grad, own_in, far_in, *refs):
        parts, (do_ref, own_ref, far_ref, weight, d_weight, sem) = refs[:n], refs[n:]
        copies = load_pieces(at, parts, low_in, rows_piece, weight, sem)
        d_weight[:half, :] = nn(o_a[...], grad[...]).astype(BF)
        d_weight[half:, :] = nn(o_b[...], grad[...]).astype(BF)
        wait_all(copies)
        copies = store_pieces(at, d_weight, rows_piece, (own_ref, far_ref), low, sem)
        do_ref[...] = nt(weight[...], grad[...]).astype(BF)
        wait_all(copies)

    return call(
        kernel,
        (1,),
        [full((half, rows))] * PARTS + [full((rows, width)), ANYWHERE, ANYWHERE] + [ANYWHERE] * n,
        [full((width, rows)), ANYWHERE, ANYWHERE],
        [
            jax.ShapeDtypeStruct((width, rows), BF),
            jax.ShapeDtypeStruct(own.shape, BF),
            jax.ShapeDtypeStruct(far.shape, BF),
        ],
        [pltpu.VMEM((width, width), BF)] * 2 + [pltpu.SemaphoreType.DMA((count_of(pieces),))],
        20,
        5 * BACK,
        (places, *o_parts, grad_low, own, far, *pieces),
        prefetch=1,
        aliases={4: 1, 5: 2},
        after=after,
    )


def attend_back(qkv_t, do_t, lse, seg_row, seg_col, width, part, after=()):
    rows = qkv_t.shape[1]
    half = width // PARTS
    heads = half // HEAD_DIM
    scale = HEAD_DIM**-0.5

    def kernel(q_ref, k_ref, v_ref, do_ref, lse_ref, seg_r, seg_c, out, sums, keys, values, d_keys, d_values):
        step = pl.program_id(0)

        @pl.when(step == 0)
        def first():
            shift_in(keys, k_ref[...])
            shift_in(values, v_ref[...])
            d_keys[...] = jnp.zeros_like(d_keys)
            d_values[...] = jnp.zeros_like(d_values)

        start = pl.multiple_of(step * QB, QB)
        window = pl.ds(start, KB)
        bias = window_bias(seg_r[0:1, :], seg_c[window, :])
        ats = [slice(h * HEAD_DIM, (h + 1) * HEAD_DIM) for h in range(heads)]
        queries = [q_ref[at, :] * BF(scale) for at in ats]
        raw = [tn(keys[at, window], q) for at, q in zip(ats, queries)]
        grad_probs = [tn(values[at, window], do_ref[at, :]) for at in ats]
        probs = [jnp.exp(r + (bias - lse_ref[h : h + 1, :])) for h, r in enumerate(raw)]
        weighted = [p * g for p, g in zip(probs, grad_probs)]
        deltas = [jnp.sum(w, axis=0, keepdims=True) for w in weighted]
        scores = [(w - p * d).astype(BF) for w, p, d in zip(weighted, probs, deltas)]
        for at, s in zip(ats, scores):
            out[at, pl.ds(start, QB)] = (nn(keys[at, window], s) * scale).astype(BF)
        for at, q, s in zip(ats, queries, scores):
            d_keys[at, window] += nt(q, s)
        for at, p in zip(ats, probs):
            d_values[at, window] += nt(do_ref[at, :], p.astype(BF))

        @pl.when(step == pl.num_programs(0) - 1)
        def last():
            edge = KB // 4
            out[half : 2 * half, :] = d_keys[...][:, edge : edge + rows].astype(BF)
            out[2 * half : 3 * half, :] = d_values[...][:, edge : edge + rows].astype(BF)
            sums[...] = nt(jnp.ones((8, rows), BF), out[...])

    return call(
        kernel,
        (rows // QB,),
        head_parts(width, rows, part)
        + [
            pl.BlockSpec((half, QB), lambda i, *unused: (part, i)),
            lanes_of((16, QB)),
            lanes_of((8, QB)),
            full(seg_col.shape),
        ],
        [full((3 * half, rows)), full((8, 3 * half))],
        [jax.ShapeDtypeStruct((3 * half, rows), BF), jax.ShapeDtypeStruct((8, 3 * half), F32)],
        [pltpu.VMEM((half, rows + QB), BF)] * 2 + [pltpu.VMEM((half, rows + QB), F32)] * 2,
        28,
        12 * BACK,
        (qkv_t, qkv_t, qkv_t, do_t, lse, seg_row, seg_col),
        after=after,
    )


def qkv_back(grad_parts, hidden, places, rows_piece, topo, after=()):
    rows, width = hidden.shape
    half = width // PARTS
    count = 3 * width
    sites, lanes = topo.X * topo.X, width // topo.Y

    def kernel(at, grad_a, grad_b, hid, own, far, whole, sem):
        step = pl.program_id(0)
        for part, grad in enumerate((grad_a, grad_b)):
            here = pl.ds(pl.multiple_of(step * width + part * half, half), half)
            whole[here, :] = nn(grad[...], hid[...]).astype(BF)

        @pl.when(step == pl.num_programs(0) - 1)
        def last():
            wait_all(store_pieces(at, whole, rows_piece, (own, far), 0, sem))

    piece_shape = jax.ShapeDtypeStruct((sites, topo.Z, rows_piece, lanes), BF)
    return call(
        kernel,
        (3,),
        [rows_of((half, rows))] * PARTS + [full((rows, width))],
        [ANYWHERE, ANYWHERE],
        [piece_shape, piece_shape],
        [pltpu.VMEM((count, width), BF), pltpu.SemaphoreType.DMA((2 * sites * topo.Z,))],
        24,
        7 * BACK,
        (places, *grad_parts, hidden),
        prefetch=1,
        after=after,
    )


def first_norm_back(grad_parts, tokens, grad_mid, vecs, pieces, places, rows_piece, after=()):
    rows, width = tokens.shape
    count, half = 3 * width, width // PARTS
    block = 256
    n = len(pieces)

    def kernel(at, grad_a, grad_b, tok, mid, vec, *refs):
        parts, (out, sums, weight, sem) = refs[:n], refs[n:]

        @pl.when(pl.program_id(0) == 0)
        def first():
            wait_all(load_pieces(at, parts, 0, rows_piece, weight, sem))
            sums[...] = jnp.zeros_like(sums)

        both = jnp.concatenate([g[k * half : (k + 1) * half, :] for k in range(3) for g in (grad_a, grad_b)], axis=0)
        grad = tn(both, weight[...])
        hat, inverse = normed(tok[...].astype(F32))
        out[...] = (mid[...] + norm_back(grad, hat, inverse, vec[0:1, :])).astype(BF)
        sums[0:1, :] += jnp.sum(grad * hat, axis=0, keepdims=True)
        sums[1:2, :] += jnp.sum(grad, axis=0, keepdims=True)

    return call(
        kernel,
        (rows // block,),
        [lanes_of((count // PARTS, block))] * PARTS
        + [rows_of((block, width)), rows_of((block, width)), full(vecs.shape)]
        + [ANYWHERE] * n,
        [rows_of((block, width)), full((8, width))],
        [jax.ShapeDtypeStruct((rows, width), BF), jax.ShapeDtypeStruct((8, width), F32)],
        [pltpu.VMEM((count, width), BF), pltpu.SemaphoreType.DMA((count_of(pieces),))],
        28,
        11 * BACK,
        (places, *grad_parts, tokens, grad_mid, vecs, *pieces),
        prefetch=1,
        after=after,
    )


def finish_out(acts, mid, vecs, groups, places, unit_rows, wide, after=()):
    rows, width = mid.shape
    block = 256
    n, total_n, count = len(groups[0][0]), len(groups[0][0]) + len(groups[1][0]), count_of(groups[0][0])
    units = 2 * wide * unit_rows

    def kernel(at, act_a, act_b, mid_ref, vec, *refs):
        parts = refs[:total_n]
        out, down_a, down_b, sem = refs[total_n:]

        @pl.when(pl.program_id(0) == 0)
        def first():
            one = load_pieces(at, parts[:n], groups[0][1], unit_rows, down_a, sem.at[0])
            two = load_pieces(at, parts[n:], groups[1][1], unit_rows, down_b, sem.at[1])
            wait_all(one)
            wait_all(two)

        result = tn(act_a[...], down_a[...]) + tn(act_b[...], down_b[...])
        out[...] = (mid_ref[...] + result + vec[7:8, :]).astype(BF)

    return call(
        kernel,
        (rows // block,),
        [lanes_of((units, block)), lanes_of((units, block)), rows_of((block, width)), full(vecs.shape)]
        + [ANYWHERE] * total_n,
        rows_of((block, width)),
        jax.ShapeDtypeStruct((rows, width), BF),
        [pltpu.VMEM((units, width), BF)] * 2 + [pltpu.SemaphoreType.DMA((2, count))],
        32,
        11 * BACK,
        (places, *acts, mid, vecs, *groups[0][0], *groups[1][0]),
        prefetch=1,
        after=after,
    )


def pack_vectors(sums_one, sums_two, sums_qkv, sums_up, places, topo, share, after=()):
    width = sums_one.shape[1]
    half = width // PARTS
    hidden = PARTS * sums_up[0].shape[1]
    group = hidden // (2 * topo.wide)
    unit = group // 2
    sites, deep, lanes = topo.X * topo.X, topo.Z, width // topo.Y
    lines = 8 + hidden // width

    def kernel(at, one, two, qkv_a, qkv_b, up_a, up_b, own, far, flat, ups, slots):
        flat[0:2, :] = one[0:2, :]
        for part, ref in enumerate((qkv_a, qkv_b)):
            lane = slice(part * half, (part + 1) * half)
            flat[2:3, lane] = ref[0:1, 0:half]
            flat[3:4, lane] = ref[0:1, 2 * half : 3 * half]
        flat[4:5, :] = two[2:3, :]
        flat[5:7, :] = two[0:2, :]
        flat[7:8, :] = two[3:4, :]
        for k in range(2 * topo.wide):
            for part, ref in enumerate((up_a, up_b)):
                ups[0:1, k * group + part * unit : k * group + (part + 1) * unit] = ref[0:1, k * unit : (k + 1) * unit]
        for line in range(8, lines):
            flat[line : line + 1, :] = ups[0:1, (line - 8) * width : (line - 7) * width]
        slots[...] = jnp.zeros_like(slots)
        for j in range(topo.wide * topo.narrow):
            done = 0
            while done < share:
                line, lane = divmod(j * share + done, width)
                take = min(share - done, width - lane)
                slots[j, 0:1, done : done + take] = flat[line : line + 1, lane : lane + take]
                done += take
        for j in range(2 * sites * deep):
            i, k = divmod(j, deep)
            slot = at[j, 0] * topo.narrow + at[j, 1] * 2 + at[j, 2]
            target = own.at[i, k] if i < sites else far.at[i - sites, k]
            target[...] = jnp.broadcast_to(slots[slot, 0:1, :], (16, lanes)).astype(BF)

    shape = (sites, deep, 16, lanes)
    return call(
        kernel,
        (1,),
        [full(a.shape) for a in (sums_one, sums_two, *sums_qkv, *sums_up)],
        [full(shape)] * 2,
        [jax.ShapeDtypeStruct(shape, BF)] * 2,
        [
            pltpu.VMEM((16, width), F32),
            pltpu.VMEM((8, hidden), F32),
            pltpu.VMEM((topo.wide * topo.narrow, 8, lanes), F32),
        ],
        16,
        3 * BACK,
        (places, sums_one, sums_two, *sums_qkv, *sums_up),
        prefetch=1,
        after=after,
    )


def total(first, *rest):
    result = first.astype(F32)
    for other in rest:
        result = result + other.astype(F32)
    return result


def tied(values, others):
    return lax.optimization_barrier((values, tuple(others)))[0] if others else values


class Spread:
    def __init__(self, piece, topo):
        self.topo, self.piece = topo, piece
        self.coming = tuple(send(piece, topo.zp[k]) for k in range(1, topo.Z))

    def along(self, others=()):
        stack = tied(jnp.stack((self.piece, *self.coming)), others)
        self.first = stack
        self.coming = tuple(send(stack, self.topo.ap[k]) for k in range(1, self.topo.X))

    def across(self, others=()):
        self.line = tied(jnp.stack((self.first, *self.coming)), others)
        self.coming = tuple(send(self.line, self.topo.bp[k]) for k in range(1, self.topo.X))
        self.near = send(self.line, self.topo.cp)

    def core(self, others=()):
        coming = tied(self.coming, others)
        self.pieces = [self.line, *coming, self.near, *[send(p, self.topo.cp) for p in coming]]


class Chain:
    def __init__(self, own, far, topo):
        self.topo, self.held = topo, own
        self.coming = [send(far, topo.cp)]

    def arrived(self):
        return tuple(self.coming)

    def fold(self, part=None):
        terms = (self.held, *self.coming)
        return total(*(terms if part is None else [t[part] for t in terms]))

    def stage(self, count, perms, others):
        self.held, self.coming = tied((self.held, self.coming), others)
        self.held, *sent = [self.fold(k).astype(BF) for k in range(count)]
        self.sent = tuple(sent)
        self.coming = [send(values, perms[count - 1 - k]) for k, values in enumerate(sent)]

    def across(self, others=()):
        side = self.topo.X
        split = lambda values: values.reshape(side, side, *values.shape[1:])
        self.held, self.coming = split(self.held), [split(c) for c in self.coming]
        self.stage(side, self.topo.bp, others)

    def along(self, others=()):
        self.stage(self.topo.X, self.topo.ap, others)

    def down(self, others=()):
        self.stage(self.topo.Z, self.topo.zp, others)

    def result(self, others=()):
        self.held, self.coming = tied((self.held, self.coming), others)
        return self.fold()


def tail_rows(values, rows, lanes):
    return jnp.pad(values[None], ((0, rows - 1), (0, lanes - values.shape[0])))


def fits(topo, rows, width, hidden):
    lanes = 2 * width // topo.narrow
    return (
        lanes % 128 == 0
        and rows % 256 == 0
        and (width // topo.wide) % 32 == 0
        and (hidden // topo.wide) % 64 == 0
        and 2 * P_THREE == QB
    )


def fast_device(
    tokens, qkv_weight, out_weight, up_weight, down_weight, vectors, bucket_counts, cotangent, topo
):
    rows, width = tokens.shape
    wide = topo.wide
    places = topo.origins()
    core = topo.here()[3]
    shards = [qkv_weight.astype(BF).T, out_weight.astype(BF), up_weight.astype(BF).T, down_weight.astype(BF)]
    r_qkv, r_out, r_unit = shards[0].shape[0] // 2, shards[1].shape[0] // 2, shards[2].shape[0] // 4
    lanes = 2 * out_weight.shape[1]
    halves = [jnp.concatenate([pick_half(s, 0, h) for h in range(2) for s in pair], axis=0) for pair in (shards[:2], shards[2:])]
    first = pair_up(halves[0], topo, core)
    vec_low, out_low = r_qkv, r_qkv + 16
    one = Spread(
        jnp.concatenate([first[:r_qkv], tail_rows(vectors.astype(BF), 16, lanes), first[r_qkv:]], axis=0), topo
    )
    rest = pair_up(tied(halves[1], (first,)), topo, core)
    piece_two = jnp.concatenate([rest[:r_unit], rest[2 * r_unit : 3 * r_unit]], axis=0)
    piece_three = jnp.concatenate([rest[r_unit : 2 * r_unit], rest[3 * r_unit :]], axis=0)
    one.along((rest,))
    two = Spread(tied(piece_two, one.coming), topo)
    one.across()
    two.along(one.coming)
    one.core((two.first,))
    one = one.pieces
    sites = topo.X * topo.X
    shapes_a = [(sites, topo.Z, 2 * r_unit, lanes)] * 2
    shapes_b = [(sites, topo.Z, 2 * r_unit + r_out, lanes)] * 2
    vecs, bias_qkv, *bias_up = unpack_vectors(one, places, vec_low, vectors.shape[0], width, wide, topo.narrow)
    segment = image_ids(bucket_counts[0], rows)
    seg_row = jnp.broadcast_to(segment[None], (8, rows))
    seg_col = jnp.pad(segment, (QB // 2, QB // 2), constant_values=-1)[:, None]

    two_along = two.coming
    two.across()
    hidden_one, qkv_t = project_qkv(tokens, vecs, bias_qkv, one, places, (r_qkv, wide))
    three = Spread(tied(piece_three, (hidden_one,)), topo)
    attn_a, lse_a = attend(qkv_t, seg_row, seg_col, width, 0, after=two_along)
    two.core((lse_a,))
    attn_b, lse_b = attend(qkv_t, seg_row, seg_col, width, 1)
    attn_t, lse = (attn_a, attn_b), (lse_a, lse_b)
    three.along((lse_b,))
    two = two.pieces
    mid, hidden_two = project_out(attn_t, tokens, vecs, one, places, out_low, r_out, after=(three.first,))
    three.across((hidden_two,))
    three_along = (three.line,)
    act_a, grad_a, sum_a, own_a, far_a = mlp_half(
        hidden_two, cotangent, bias_up[0], two, places, 0, r_unit, shapes_a, wide, after=three_along
    )
    three.core((sum_a,))
    three = three.pieces
    chain_a = Chain(own_a, far_a, topo)
    act_b, grad_b, sum_b, own_b, far_b = mlp_half(
        hidden_two, cotangent, bias_up[1], three, places, 0, r_unit, shapes_b, wide
    )
    chain_a.across((sum_b,))
    grad_mid, grad_mid_low, sums_two = second_norm_back(
        (grad_a, grad_b), mid, cotangent, vecs, ((two, 0), (three, 0)), places, r_unit, wide,
        after=chain_a.sent,
    )
    do_t, own_b, far_b = out_back(attn_t, grad_mid_low, one, places, out_low, r_out, own_b, far_b, 2 * r_unit)
    chain_b = Chain(own_b, far_b, topo)
    chain_a.along((do_t,))
    grads_0, sums_0 = attend_back(qkv_t, do_t, lse[0], seg_row, seg_col, width, 0, after=chain_a.sent)
    chain_a.down((sums_0,))
    chain_b.across((sums_0,))
    grads_1, sums_1 = attend_back(
        qkv_t, do_t, lse[1], seg_row, seg_col, width, 1, after=chain_a.sent + chain_b.sent
    )
    grad_t = (grads_0, grads_1)
    chain_b.along((sums_1,))
    own_q, far_q = qkv_back(grad_t, hidden_one, places, r_qkv, topo, after=(*chain_a.arrived(), *chain_b.sent))
    chain_q = Chain(own_q, far_q, topo)
    chain_q.across()
    input_grad, sums_one = first_norm_back(
        grad_t, tokens, grad_mid, vecs, one, places, r_qkv, after=chain_q.sent + chain_b.sent
    )
    chain_q.along((sums_one,))
    chain_b.down((sums_one,))
    own_v, far_v = pack_vectors(
        sums_one, sums_two, (sums_0, sums_1), (sum_a, sum_b), places, topo, vectors.shape[0], after=chain_q.sent
    )
    chain_v = Chain(own_v, far_v, topo)
    chain_v.across()
    chain_q.down()
    block_out = finish_out(
        (act_a, act_b), mid, vecs, ((two, r_unit), (three, r_unit)), places, r_unit, wide,
        after=chain_q.sent + chain_v.sent,
    )
    chain_v.along((block_out,))
    chain_v.down()
    part_a, part_b, part_q = chain_a.result((sums_one,)), chain_b.result((block_out,)), chain_q.result((block_out,))
    vector_grad = chain_v.result()[0, : vectors.shape[0]]
    down = jnp.concatenate([part_a[r_unit:], part_b[r_unit : 2 * r_unit]], axis=0)
    up = jnp.concatenate([part_a[:r_unit], part_b[:r_unit]], axis=0)
    out = part_b[2 * r_unit :]
    grads = [unpair(g, topo, core) for g in (part_q, out, up, down)]
    return (block_out, input_grad, grads[0].T, grads[1], grads[2].T, grads[3], vector_grad)


def per_device(
    tokens, qkv_weight, out_weight, up_weight, down_weight, vectors, bucket_counts, cotangent
):
    topo = Topo(lax.axis_size("wide"), lax.axis_size("narrow"))
    operands = (tokens, qkv_weight, out_weight, up_weight, down_weight, vectors, bucket_counts, cotangent)
    if fits(topo, *tokens.shape, up_weight.shape[1] * topo.wide):
        return fast_device(*operands, topo)
    return plain_device(*operands)


def plain_device(
    tokens, qkv_weight, out_weight, up_weight, down_weight, vectors, bucket_counts, cotangent
):
    rows, width = tokens.shape
    halves = (
        lax.all_gather(qkv_weight.astype(jnp.bfloat16), "narrow", axis=0, tiled=True),
        lax.all_gather(out_weight.astype(jnp.bfloat16), "narrow", axis=1, tiled=True),
        lax.all_gather(up_weight.astype(jnp.bfloat16), "narrow", axis=0, tiled=True),
        lax.all_gather(down_weight.astype(jnp.bfloat16), "narrow", axis=1, tiled=True),
        lax.all_gather(vectors.astype(jnp.bfloat16), "narrow", axis=0, tiled=True),
    )
    wholes = (
        lax.all_gather(halves[0], "wide", axis=1, tiled=True),
        lax.all_gather(halves[1], "wide", axis=0, tiled=True),
        lax.all_gather(halves[2], "wide", axis=1, tiled=True),
        lax.all_gather(halves[3], "wide", axis=0, tiled=True),
        lax.all_gather(halves[4], "wide", axis=0, tiled=True),
    )
    qkv_full, out_full, up_full, down_full, packed = wholes
    params = packed.astype(jnp.float32)
    gain_one = params[0:width]
    shift_one = params[width : 2 * width]
    bias_query = params[2 * width : 3 * width]
    bias_value = params[3 * width : 4 * width]
    bias_out = params[4 * width : 5 * width]
    gain_two = params[5 * width : 6 * width]
    shift_two = params[6 * width : 7 * width]
    bias_down = params[7 * width : 8 * width]
    bias_up = params[8 * width :]
    inputs = tokens.astype(jnp.float32)
    hidden_one = layer_norm(inputs, gain_one, shift_one).astype(jnp.bfloat16)
    qkv_bias = jnp.concatenate([bias_query, jnp.zeros((width,), jnp.float32), bias_value])
    qkv_all = (jnp.dot(hidden_one, qkv_full, preferred_element_type=jnp.float32) + qkv_bias).astype(
        jnp.bfloat16
    )
    margin = P_THREE
    blocks = rows // QROWS
    span = QROWS + 2 * margin
    scale = HEAD_DIM ** (-0.5)
    query_blk = qkv_all[:, :width].reshape(blocks, QROWS, HEADS, HEAD_DIM)
    keys_win = windows_of(qkv_all[:, width : 2 * width], margin, blocks, 0).reshape(
        blocks, span, HEADS, HEAD_DIM
    )
    values_win = windows_of(qkv_all[:, 2 * width :], margin, blocks, 0).reshape(
        blocks, span, HEADS, HEAD_DIM
    )
    segment = image_ids(bucket_counts[0], rows)
    seg_rows = segment.reshape(blocks, QROWS)
    seg_cols = windows_of(segment, margin, blocks, -1)
    same = seg_rows[:, None, :, None] == seg_cols[:, None, None, :]
    raw = (
        jnp.einsum("bqhd,bkhd->bhqk", query_blk, keys_win, preferred_element_type=jnp.float32)
        * scale
    )
    masked = jnp.where(same, raw, NEG)
    top = jnp.max(masked, axis=3, keepdims=True)
    expo = jnp.exp(masked - top)
    total = jnp.sum(expo, axis=3, keepdims=True)
    probs_low = (expo / total).astype(jnp.bfloat16)
    log_total = top + jnp.log(total)
    attended = jnp.einsum(
        "bhqk,bkhd->bqhd", probs_low, values_win, preferred_element_type=jnp.float32
    )
    attn_low = attended.reshape(rows, width).astype(jnp.bfloat16)
    mid = inputs + jnp.dot(attn_low, out_full, preferred_element_type=jnp.float32) + bias_out
    hidden_two = layer_norm(mid, gain_two, shift_two).astype(jnp.bfloat16)
    pre_act = jnp.dot(hidden_two, up_full, preferred_element_type=jnp.float32) + bias_up
    activated = gelu_exact(pre_act).astype(jnp.bfloat16)
    output = mid + jnp.dot(activated, down_full, preferred_element_type=jnp.float32) + bias_down
    block_out = output.astype(jnp.bfloat16)
    grad_top = cotangent.astype(jnp.float32)
    d_down = contract_rows(activated, cotangent)
    d_bias_down = jnp.sum(grad_top, axis=0)
    grad_act = contract_cols(cotangent, down_full)
    unused_act, gelu_back = jax.vjp(gelu_exact, pre_act)
    grad_pre = gelu_back(grad_act)[0].astype(jnp.bfloat16)
    d_up = contract_rows(hidden_two, grad_pre)
    d_bias_up = jnp.sum(grad_pre.astype(jnp.float32), axis=0)
    grad_hidden_two = contract_cols(grad_pre, up_full)
    unused_two, norm_back_two = jax.vjp(layer_norm, mid, gain_two, shift_two)
    grad_mid_part, d_gain_two, d_shift_two = norm_back_two(grad_hidden_two)
    grad_mid = grad_top + grad_mid_part
    grad_mid_low = grad_mid.astype(jnp.bfloat16)
    d_out = contract_rows(attn_low, grad_mid_low)
    d_bias_out = jnp.sum(grad_mid_low.astype(jnp.float32), axis=0)
    grad_attn = contract_cols(grad_mid_low, out_full).astype(jnp.bfloat16)
    raw_again = (
        jnp.einsum("bqhd,bkhd->bhqk", query_blk, keys_win, preferred_element_type=jnp.float32)
        * scale
    )
    probs = jnp.exp(jnp.where(same, raw_again, NEG) - log_total)
    grad_blk = grad_attn.reshape(blocks, QROWS, HEADS, HEAD_DIM)
    grad_probs = jnp.einsum(
        "bqhd,bkhd->bhqk", grad_blk, values_win, preferred_element_type=jnp.float32
    )
    grad_scores = (
        probs * (grad_probs - jnp.sum(probs * grad_probs, axis=3, keepdims=True))
    ).astype(jnp.bfloat16)
    grad_query = (
        jnp.einsum("bhqk,bkhd->bqhd", grad_scores, keys_win, preferred_element_type=jnp.float32)
        * scale
    )
    grad_keys_win = (
        jnp.einsum("bhqk,bqhd->bkhd", grad_scores, query_blk, preferred_element_type=jnp.float32)
        * scale
    )
    grad_values_win = jnp.einsum(
        "bhqk,bqhd->bkhd", probs.astype(jnp.bfloat16), grad_blk, preferred_element_type=jnp.float32
    )
    grad_keys = fold_windows(grad_keys_win.reshape(blocks, span, width), margin, QROWS)
    grad_values = fold_windows(grad_values_win.reshape(blocks, span, width), margin, QROWS)
    grad_qkv = jnp.concatenate(
        [grad_query.reshape(rows, width), grad_keys, grad_values], axis=1
    ).astype(jnp.bfloat16)
    d_qkv = contract_rows(hidden_one, grad_qkv)
    column_sums = jnp.sum(grad_qkv.astype(jnp.float32), axis=0)
    grad_hidden_one = contract_cols(grad_qkv, qkv_full)
    unused_one, norm_back_one = jax.vjp(layer_norm, inputs, gain_one, shift_one)
    grad_in_part, d_gain_one, d_shift_one = norm_back_one(grad_hidden_one)
    input_grad = (grad_mid + grad_in_part).astype(jnp.bfloat16)
    d_vector = jnp.concatenate(
        [
            d_gain_one,
            d_shift_one,
            column_sums[:width],
            column_sums[2 * width :],
            d_bias_out,
            d_gain_two,
            d_shift_two,
            d_bias_down,
            d_bias_up,
        ]
    )
    partial_sums = (
        lax.psum_scatter(
            d_qkv.astype(jnp.bfloat16), "wide", scatter_dimension=1, tiled=True
        ).astype(jnp.float32),
        lax.psum_scatter(
            d_out.astype(jnp.bfloat16), "wide", scatter_dimension=0, tiled=True
        ).astype(jnp.float32),
        lax.psum_scatter(d_up.astype(jnp.bfloat16), "wide", scatter_dimension=1, tiled=True).astype(
            jnp.float32
        ),
        lax.psum_scatter(
            d_down.astype(jnp.bfloat16), "wide", scatter_dimension=0, tiled=True
        ).astype(jnp.float32),
        lax.psum_scatter(
            d_vector.astype(jnp.bfloat16), "wide", scatter_dimension=0, tiled=True
        ).astype(jnp.float32),
    )
    final = (
        lax.psum_scatter(
            partial_sums[0].astype(jnp.bfloat16), "narrow", scatter_dimension=0, tiled=True
        ).astype(jnp.float32),
        lax.psum_scatter(
            partial_sums[1].astype(jnp.bfloat16), "narrow", scatter_dimension=1, tiled=True
        ).astype(jnp.float32),
        lax.psum_scatter(
            partial_sums[2].astype(jnp.bfloat16), "narrow", scatter_dimension=0, tiled=True
        ).astype(jnp.float32),
        lax.psum_scatter(
            partial_sums[3].astype(jnp.bfloat16), "narrow", scatter_dimension=1, tiled=True
        ).astype(jnp.float32),
        lax.psum_scatter(
            partial_sums[4].astype(jnp.bfloat16), "narrow", scatter_dimension=0, tiled=True
        ).astype(jnp.float32),
    )
    return (block_out, input_grad, final[0], final[1], final[2], final[3], final[4])


def solution(mesh):
    return jax.shard_map(
        per_device,
        mesh=mesh,
        in_specs=(
            P(("wide", "narrow"), None),
            P("narrow", "wide"),
            P("wide", "narrow"),
            P("narrow", "wide"),
            P("wide", "narrow"),
            P(("wide", "narrow")),
            P(("wide", "narrow"), None),
            P(("wide", "narrow"), None),
        ),
        out_specs=(
            P(("wide", "narrow"), None),
            P(("wide", "narrow"), None),
            P("narrow", "wide"),
            P("wide", "narrow"),
            P("narrow", "wide"),
            P("wide", "narrow"),
            P(("wide", "narrow")),
        ),
        check_vma=False,
    )
```

```python
import math

import jax
import jax.numpy as jnp
from jax import lax
from jax.experimental import pallas as pl
from jax.experimental.pallas import tpu as pltpu
from jax.sharding import PartitionSpec as P

HEADS = 12
HEAD_DIM = 64
QROWS = 512
P_ONE = 25
P_TWO = 49
P_THREE = 64


EPS = 1e-06
NEG = -1e30


def layer_norm(values, gain, shift):
    center = values - jnp.mean(values, axis=-1, keepdims=True)
    spread = jnp.mean(center * center, axis=-1, keepdims=True)
    return center * lax.rsqrt(spread + EPS) * gain + shift


def image_ids(counts, rows):
    place = jnp.arange(rows, dtype=jnp.int32)
    first = counts[0] * P_ONE
    second = first + counts[1] * P_TWO
    bucket = (place >= first).astype(jnp.int32) + (place >= second).astype(jnp.int32)
    start = jnp.where(bucket == 0, 0, jnp.where(bucket == 1, first, second))
    length = jnp.where(bucket == 0, P_ONE, jnp.where(bucket == 1, P_TWO, P_THREE)).astype(jnp.int32)
    return bucket * rows + (place - start) // length


def gelu_exact(values):
    return jax.nn.gelu(values, approximate=False)


def contract_rows(left, right):
    return lax.dot_general(
        left, right, (((0,), (0,)), ((), ())), preferred_element_type=jnp.float32
    )


def contract_cols(left, right):
    return lax.dot_general(
        left, right, (((1,), (1,)), ((), ())), preferred_element_type=jnp.float32
    )


def windows_of(values, margin, blocks, fill):
    rows = values.shape[0]
    block_rows = rows // blocks
    rest = values.shape[1:]
    padded = jnp.pad(
        values, ((margin, margin),) + tuple(((0, 0) for unused in rest)), constant_values=fill
    )
    before = padded[:rows].reshape((blocks, block_rows) + rest)[:, :margin]
    middle = values.reshape((blocks, block_rows) + rest)
    after = padded[2 * margin : 2 * margin + rows].reshape((blocks, block_rows) + rest)[
        :, block_rows - margin :
    ]
    return jnp.concatenate([before, middle, after], axis=1)


def fold_windows(grads, margin, block_rows):
    blocks = grads.shape[0]
    width = grads.shape[2]
    middle = grads[:, margin : margin + block_rows]
    before = jnp.pad(grads[1:, :margin], ((0, 1), (block_rows - margin, 0), (0, 0)))
    after = jnp.pad(grads[:-1, margin + block_rows :], ((1, 0), (0, block_rows - margin), (0, 0)))
    return (middle + before + after).reshape(blocks * block_rows, width)


BF = jnp.bfloat16
F32 = jnp.float32
AXES = ("wide", "narrow")


class Topo:
    def __init__(self, wide, narrow):
        self.wide, self.narrow = wide, narrow
        self.Y = narrow // 2
        self.X = self.Y
        self.Z = wide // self.X
        side, deep = self.X, self.Z
        self.zp = [self.perm(lambda z, x, y, c, k=k: ((z + k) % deep, x, y, c)) for k in range(deep)]
        self.ap = [
            self.perm(
                lambda z, x, y, c, k=k: (z, (x + k) % side, y, c) if c == 0 else (z, x, (y + k) % side, c)
            )
            for k in range(side)
        ]
        self.bp = [
            self.perm(
                lambda z, x, y, c, k=k: (z, x, (y + k) % side, c) if c == 0 else (z, (x + k) % side, y, c)
            )
            for k in range(side)
        ]
        self.cp = self.perm(lambda z, x, y, c: (z, x, y, 1 - c))

    def did(self, z, x, y, c):
        return ((z * self.X + x) * self.Y + y) * 2 + c

    def perm(self, target):
        return [
            (self.did(z, x, y, c), self.did(*target(z, x, y, c)))
            for z in range(self.Z)
            for x in range(self.X)
            for y in range(self.Y)
            for c in range(2)
        ]

    def here(self):
        wide, narrow = lax.axis_index("wide"), lax.axis_index("narrow")
        return wide // self.X, wide % self.X, narrow // 2, narrow % 2

    def origins(self):
        z0, x0, y0, c0 = self.here()
        side, deep = self.X, self.Z
        index = jnp.arange(2 * side * side * deep, dtype=jnp.int32)
        kz, ka, kb = index % deep, index // deep % side, index // (deep * side) % side
        c = (c0 + index // (deep * side * side)) % 2
        x = (x0 + side - jnp.where(c == 0, ka, kb)) % side
        y = (y0 + side - jnp.where(c == 0, kb, ka)) % side
        z = (z0 + deep - kz) % deep
        return jnp.stack([z * side + x, y, c], axis=1).astype(jnp.int32)


def send(values, perm):
    return lax.ppermute(values, AXES, perm)


def pick_half(values, axis, index):
    half = values.shape[axis] // 2
    return lax.dynamic_slice_in_dim(values, index * half, half, axis)


def pair_up(shard, topo, core):
    mine = pick_half(shard, 0, core)
    other = send(pick_half(shard, 0, 1 - core), topo.cp)
    first = jnp.where(core == 0, mine, other)
    second = jnp.where(core == 0, other, mine)
    return jnp.concatenate([first, second], axis=1)


def unpair(piece, topo, core):
    mine = pick_half(piece, 1, core)
    other = send(pick_half(piece, 1, 1 - core), topo.cp)
    first = jnp.where(core == 0, mine, other)
    second = jnp.where(core == 0, other, mine)
    return jnp.concatenate([first, second], axis=0)


def gather(piece, topo):
    stack = jnp.stack([piece] + [send(piece, topo.zp[k]) for k in range(1, topo.Z)])
    line = [stack] + [send(stack, topo.ap[k]) for k in range(1, topo.X)]
    own = [p for k in range(topo.X) for p in (line if k == 0 else [send(q, topo.bp[k]) for q in line])]
    return own + [send(p, topo.cp) for p in own]


def nn(a, b):
    return lax.dot_general(a, b, (((1,), (0,)), ((), ())), preferred_element_type=F32)


def nt(a, b):
    return lax.dot_general(a, b, (((1,), (1,)), ((), ())), preferred_element_type=F32)


def tn(a, b):
    return lax.dot_general(a, b, (((0,), (0,)), ((), ())), preferred_element_type=F32)


def normed(values):
    center = values - jnp.mean(values, axis=-1, keepdims=True)
    spread = jnp.mean(center * center, axis=-1, keepdims=True)
    inverse = lax.rsqrt(spread + EPS)
    return center * inverse, inverse


def norm_back(grad, hat, inverse, gain):
    scaled = grad * gain
    first = jnp.mean(scaled, axis=-1, keepdims=True)
    second = jnp.mean(scaled * hat, axis=-1, keepdims=True)
    return inverse * (scaled - first - hat * second)


ROOT_HALF = 0.7071067811865476
ROOT_TAU = 0.3989422804014327
MIB = 1024 * 1024
WIDTH = HEADS * HEAD_DIM
SCALE = 1.0
BACK = 5


def cdf_pdf(u):
    bell = jnp.exp(-0.5 * (u * u))
    below = 1.0 + (0.3275911 * ROOT_HALF) * jnp.abs(u)
    t = pltpu.reciprocal(below, approx=True)
    t = t * (2.0 - below * t)
    poly = 1.061405429 * 0.5
    for coef in (-1.453152027, 1.421413741, -0.284496736, 0.254829592):
        poly = poly * t + coef * 0.5
    upper = poly * t * bell
    return jnp.where(u < 0, upper, 1.0 - upper), ROOT_TAU * bell


def call(kernel, grid, in_specs, out_specs, out_shape, scratch, vmem, us, operands, prefetch=0, aliases=None, after=()):
    first, count = len(operands), len(after)

    def body(*refs):
        kernel(*refs[:first], *refs[first + count :])

    return pl.pallas_call(
        body,
        grid_spec=pltpu.PrefetchScalarGridSpec(
            num_scalar_prefetch=prefetch,
            grid=grid,
            in_specs=in_specs + [ANYWHERE] * count,
            out_specs=out_specs,
            scratch_shapes=scratch,
        ),
        out_shape=out_shape,
        input_output_aliases=aliases or {},
        compiler_params=pltpu.CompilerParams(vmem_limit_bytes=vmem * MIB),
        cost_estimate=pl.CostEstimate(flops=int(us * SCALE * 1.0e9), bytes_accessed=int(us * SCALE * 3.0e6), transcendentals=0),
    )(*operands, *after)


ANYWHERE = pl.BlockSpec(memory_space=pltpu.HBM)


def full(shape):
    return pl.BlockSpec(shape, lambda *unused: (0,) * len(shape))


def rows_of(shape):
    return pl.BlockSpec(shape, lambda i, *unused: (i,) + (0,) * (len(shape) - 1))


def lanes_of(shape):
    return pl.BlockSpec(shape, lambda i, *unused: (0, i))


def piece_place(at, j, rows, lanes):
    row = pl.multiple_of((at[j, 0] * 2 + at[j, 2]) * rows, 16)
    lane = pl.multiple_of(at[j, 1] * lanes, 128)
    return pl.ds(row, rows), pl.ds(lane, lanes)


def sites_of(at, pieces, rows, lanes):
    if len(pieces) == 1:
        (piece,) = pieces
        narrow = 2 * (WIDTH // lanes)
        for j in range(piece.shape[0]):
            wide, y, core = j // narrow, j % narrow // 2, j % 2
            yield piece.at[j], (pl.ds((wide * 2 + core) * rows, rows), pl.ds(y * lanes, lanes))
    else:
        side, deep = pieces[0].shape[:2]
        for i, piece in enumerate(pieces):
            for a in range(side):
                for k in range(deep):
                    yield piece.at[a, k], piece_place(at, (i * side + a) * deep + k, rows, lanes)


def count_of(pieces):
    return len(pieces) * math.prod(pieces[0].shape[:-2])


def load_pieces(at, pieces, low, rows, whole, sem):
    copies = []
    for j, (piece, place) in enumerate(sites_of(at, pieces, rows, pieces[0].shape[-1])):
        copy = pltpu.make_async_copy(piece.at[pl.ds(low, rows), :], whole.at[place], sem.at[j])
        copy.start()
        copies.append(copy)
    return copies


def store_pieces(at, whole, rows, outs, low, sem):
    copies = []
    for j, (piece, place) in enumerate(sites_of(at, outs, rows, outs[0].shape[-1])):
        copy = pltpu.make_async_copy(whole.at[place], piece.at[pl.ds(low, rows), :], sem.at[j])
        copy.start()
        copies.append(copy)
    return copies


def wait_all(copies):
    for copy in copies:
        copy.wait()


def unpack_vectors(pieces, places, low, share, width, wide, narrow):
    n, lanes = len(pieces), pieces[0].shape[-1]
    hidden = wide * narrow * share - 8 * width
    group = hidden // (2 * wide)
    unit = group // 2
    lines = 8 + hidden // width

    def kernel(at, *refs):
        parts, (vecs, bias, up_a, up_b, slots, flat, sem) = refs[:n], refs[n:]
        copies = []
        for j, (piece, unused) in enumerate(sites_of(at, parts, 16, lanes)):
            slot = at[j, 0] * narrow + at[j, 1] * 2 + at[j, 2]
            copy = pltpu.make_async_copy(piece.at[pl.ds(low, 16), :], slots.at[slot], sem.at[j])
            copy.start()
            copies.append(copy)
        wait_all(copies)
        for j in range(wide * narrow):
            values = slots[j].astype(F32)[0:1, :]
            done = 0
            while done < share:
                line, lane = divmod(j * share + done, width)
                take = min(share - done, width - lane)
                flat[line : line + 1, lane : lane + take] = values[:, done : done + take]
                done += take
        vecs[...] = flat[0:8, :]
        columns = lambda line: jnp.broadcast_to(flat[line : line + 1, :], (128, width)).T[:, 0:1]
        bias[0:width, :] = columns(2)
        bias[width : 2 * width, :] = jnp.zeros((width, 1), F32)
        bias[2 * width :, :] = columns(3)
        up = jnp.concatenate([columns(line) for line in range(8, lines)], axis=0)
        for k in range(2 * wide):
            up_a[k * unit : (k + 1) * unit, :] = up[k * group : k * group + unit, :]
            up_b[k * unit : (k + 1) * unit, :] = up[k * group + unit : (k + 1) * group, :]

    column = jax.ShapeDtypeStruct((hidden // 2, 1), F32)
    return call(
        kernel,
        (1,),
        [ANYWHERE] * n,
        [full((8, width)), full((3 * width, 1)), full(column.shape), full(column.shape)],
        [jax.ShapeDtypeStruct((8, width), F32), jax.ShapeDtypeStruct((3 * width, 1), F32), column, column],
        [
            pltpu.VMEM((wide * narrow, 16, lanes), BF),
            pltpu.VMEM((16, width), F32),
            pltpu.SemaphoreType.DMA((count_of(pieces),)),
        ],
        16,
        3,
        (places, *pieces),
        prefetch=1,
    )


def project_qkv(tokens, vecs, bias, pieces, places, shape, after=()):
    rows, width = tokens.shape
    half, wide = shape
    n, block, steps = len(pieces), 256, 3 * width // 256

    def kernel(at, tok, vec, bias_ref, *refs):
        parts, (hid_out, out, weight, hid, sem) = refs[:n], refs[n:]
        step = pl.program_id(0)

        @pl.when(step == 0)
        def first():
            copies = load_pieces(at, parts, 0, half, weight, sem)
            hat, unused = normed(tok[...].astype(F32))
            hid[...] = (hat * vec[0:1, :] + vec[1:2, :]).astype(BF)
            hid_out[...] = hid[...]
            wait_all(copies)

        start = pl.multiple_of(step * block, block)
        out[...] = (nt(weight[pl.ds(start, block), :], hid[...]) + bias_ref[...]).astype(BF)

    return call(
        kernel,
        (steps,),
        [full((rows, width)), full(vecs.shape), rows_of((block, 1))] + [ANYWHERE] * n,
        [full((rows, width)), rows_of((block, rows))],
        [jax.ShapeDtypeStruct((rows, width), BF), jax.ShapeDtypeStruct((3 * width, rows), BF)],
        [
            pltpu.VMEM((3 * width, width), BF),
            pltpu.VMEM((rows, width), BF),
            pltpu.SemaphoreType.DMA((count_of(pieces),)),
        ],
        20,
        9,
        (places, tokens, vecs, bias, *pieces),
        prefetch=1,
        after=after,
    )


QB = 128
KB = 256
PARTS = 2


def window_bias(seg_row, seg_col):
    return jnp.where(seg_col == seg_row, 0.0, NEG).astype(F32)


def shift_in(dst, src):
    count, rows = src.shape
    half = KB // 4
    zero = jnp.zeros((count, half), src.dtype)
    dst[...] = jnp.concatenate([zero, src, zero], axis=1)


def head_parts(width, rows, part):
    half = width // PARTS
    return [
        pl.BlockSpec((half, QB), lambda i, *unused: (part, i)),
        pl.BlockSpec((half, rows), lambda i, *unused: (PARTS + part, 0)),
        pl.BlockSpec((half, rows), lambda i, *unused: (2 * PARTS + part, 0)),
    ]


def attend(qkv_t, seg_row, seg_col, width, part, after=()):
    rows = qkv_t.shape[1]
    half = width // PARTS
    heads = half // HEAD_DIM

    def kernel(q_ref, k_ref, v_ref, seg_r, seg_c, o_ref, lse_ref, keys, values):
        step = pl.program_id(0)

        @pl.when(step == 0)
        def first():
            shift_in(keys, k_ref[...])
            shift_in(values, v_ref[...])

        start = pl.multiple_of(step * QB, QB)
        window = pl.ds(start, KB)
        bias = window_bias(seg_r[0:1, :], seg_c[window, :])
        ats = [slice(h * HEAD_DIM, (h + 1) * HEAD_DIM) for h in range(heads)]
        scores = [tn(keys[at, window], q_ref[at, :] * BF(HEAD_DIM**-0.5)) + bias for at in ats]
        tops = [jnp.max(s, axis=0, keepdims=True) for s in scores]
        expos = [jnp.exp(s - t) for s, t in zip(scores, tops)]
        sums = [jnp.sum(e, axis=0, keepdims=True) for e in expos]
        probs = [(e * (1.0 / s)).astype(BF) for e, s in zip(expos, sums)]
        for at, p in zip(ats, probs):
            o_ref[at, :] = nn(values[at, window], p).astype(BF)
        for h, (t, s) in enumerate(zip(tops, sums)):
            lse_ref[h : h + 1, :] = t + jnp.log(s)

    return call(
        kernel,
        (rows // QB,),
        head_parts(width, rows, part) + [lanes_of((8, QB)), full(seg_col.shape)],
        [lanes_of((half, QB)), lanes_of((16, QB))],
        [jax.ShapeDtypeStruct((half, rows), BF), jax.ShapeDtypeStruct((16, rows), F32)],
        [pltpu.VMEM((half, rows + QB), BF), pltpu.VMEM((half, rows + QB), BF)],
        20,
        6,
        (qkv_t, qkv_t, qkv_t, seg_row, seg_col),
        after=after,
    )


def project_out(o_parts, tokens, vecs, pieces, places, low, rows_piece, after=()):
    rows, width = tokens.shape
    n, block = len(pieces), 256

    def kernel(at, o_a, o_b, tok, vec, *refs):
        parts, (mid_out, hid_out, weight, sem) = refs[:n], refs[n:]

        @pl.when(pl.program_id(0) == 0)
        def first():
            wait_all(load_pieces(at, parts, low, rows_piece, weight, sem))

        both = jnp.concatenate([o_a[...], o_b[...]], axis=0)
        mid = tok[...].astype(F32) + tn(both, weight[...]) + vec[4:5, :]
        mid_out[...] = mid
        hat, unused = normed(mid)
        hid_out[...] = (hat * vec[5:6, :] + vec[6:7, :]).astype(BF)

    return call(
        kernel,
        (rows // block,),
        [lanes_of((width // PARTS, block))] * PARTS + [rows_of((block, width)), full(vecs.shape)] + [ANYWHERE] * n,
        [rows_of((block, width)), rows_of((block, width))],
        [jax.ShapeDtypeStruct((rows, width), F32), jax.ShapeDtypeStruct((rows, width), BF)],
        [pltpu.VMEM((width, width), BF), pltpu.SemaphoreType.DMA((count_of(pieces),))],
        16,
        5,
        (places, *o_parts, tokens, vecs, *pieces),
        prefetch=1,
        after=after,
    )


def mlp_half(hidden, cot, bias, pieces, places, low, unit_rows, out_shapes, wide, after=()):
    rows, width = hidden.shape
    n, m, count = len(pieces), len(out_shapes), count_of(pieces)
    units = 2 * wide * unit_rows
    block = min(384, units)

    def kernel(at, hid, cot_ref, bias_ref, *refs):
        parts = refs[:n]
        act_out, grad_out, sum_out = refs[n : n + 3]
        outs = refs[n + 3 : n + 3 + m]
        up, down, d_up, d_down, sem_a, sem_b = refs[n + 3 + m :]
        step = pl.program_id(0)

        @pl.when(step == 0)
        def first():
            one = load_pieces(at, parts, low, unit_rows, up, sem_a)
            two = load_pieces(at, parts, low + unit_rows, unit_rows, down, sem_b)
            wait_all(one)
            wait_all(two)

        here = pl.ds(pl.multiple_of(step * block, block), block)
        pre = nt(up[here, :], hid[...]) + bias_ref[...]
        grad_act = nt(down[here, :], cot_ref[...])
        cdf, pdf = cdf_pdf(pre)
        act = (pre * cdf).astype(BF)
        grad = (grad_act * (cdf + pre * pdf)).astype(BF)
        act_out[...] = act
        grad_out[...] = grad
        sum_out[...] = nt(jnp.ones((8, rows), BF), grad)
        d_down[here, :] = nn(act, cot_ref[...]).astype(BF)
        d_up[here, :] = nn(grad, hid[...]).astype(BF)

        @pl.when(step == pl.num_programs(0) - 1)
        def last():
            one = store_pieces(at, d_up, unit_rows, outs, 0, sem_a)
            two = store_pieces(at, d_down, unit_rows, outs, unit_rows, sem_b)
            wait_all(one)
            wait_all(two)

    return call(
        kernel,
        (units // block,),
        [full((rows, width)), full((rows, width)), rows_of((block, 1))] + [ANYWHERE] * n,
        [rows_of((block, rows)), rows_of((block, rows)), lanes_of((8, block))] + [ANYWHERE] * m,
        [
            jax.ShapeDtypeStruct((units, rows), BF),
            jax.ShapeDtypeStruct((units, rows), BF),
            jax.ShapeDtypeStruct((8, units), F32),
            *[jax.ShapeDtypeStruct(shape, BF) for shape in out_shapes],
        ],
        [pltpu.VMEM((units, width), BF)] * 4
        + [pltpu.SemaphoreType.DMA((count,))] * 2,
        32,
        22,
        (places, hidden, cot, bias, *pieces),
        prefetch=1,
        after=after,
    )


def second_norm_back(grads, mid, cot, vecs, groups, places, unit_rows, wide, after=()):
    rows, width = mid.shape
    block = 256
    n, total_n, count = len(groups[0][0]), len(groups[0][0]) + len(groups[1][0]), count_of(groups[0][0])
    units = 2 * wide * unit_rows

    def kernel(at, ga, gb, mid_ref, cot_ref, vec, *refs):
        parts = refs[:total_n]
        out, low_out, sums, up_a, up_b, sem = refs[total_n:]
        step = pl.program_id(0)

        @pl.when(step == 0)
        def first():
            one = load_pieces(at, parts[:n], groups[0][1], unit_rows, up_a, sem.at[0])
            two = load_pieces(at, parts[n:], groups[1][1], unit_rows, up_b, sem.at[1])
            wait_all(one)
            wait_all(two)
            sums[...] = jnp.zeros_like(sums)

        grad = tn(ga[...], up_a[...]) + tn(gb[...], up_b[...])
        hat, inverse = normed(mid_ref[...])
        top = cot_ref[...].astype(F32)
        total_grad = top + norm_back(grad, hat, inverse, vec[5:6, :])
        out[...] = total_grad
        lower = total_grad.astype(BF)
        low_out[...] = lower
        sums[0:1, :] += jnp.sum(grad * hat, axis=0, keepdims=True)
        sums[1:2, :] += jnp.sum(grad, axis=0, keepdims=True)
        sums[2:3, :] += jnp.sum(lower.astype(F32), axis=0, keepdims=True)
        sums[3:4, :] += jnp.sum(top, axis=0, keepdims=True)

    return call(
        kernel,
        (rows // block,),
        [lanes_of((units, block)), lanes_of((units, block)), rows_of((block, width)), rows_of((block, width)), full(vecs.shape)]
        + [ANYWHERE] * total_n,
        [rows_of((block, width)), rows_of((block, width)), full((8, width))],
        [
            jax.ShapeDtypeStruct((rows, width), F32),
            jax.ShapeDtypeStruct((rows, width), BF),
            jax.ShapeDtypeStruct((8, width), F32),
        ],
        [pltpu.VMEM((units, width), BF)] * 2 + [pltpu.SemaphoreType.DMA((2, count))],
        32,
        14 * BACK,
        (places, *grads, mid, cot, vecs, *groups[0][0], *groups[1][0]),
        prefetch=1,
        after=after,
    )


def out_back(o_parts, grad_low, pieces, places, low_in, rows_piece, own, far, low, after=()):
    rows, width = grad_low.shape
    half = width // PARTS
    n = len(pieces)

    def kernel(at, o_a, o_b, grad, own_in, far_in, *refs):
        parts, (do_ref, own_ref, far_ref, weight, d_weight, sem) = refs[:n], refs[n:]
        copies = load_pieces(at, parts, low_in, rows_piece, weight, sem)
        d_weight[:half, :] = nn(o_a[...], grad[...]).astype(BF)
        d_weight[half:, :] = nn(o_b[...], grad[...]).astype(BF)
        wait_all(copies)
        copies = store_pieces(at, d_weight, rows_piece, (own_ref, far_ref), low, sem)
        do_ref[...] = nt(weight[...], grad[...]).astype(BF)
        wait_all(copies)

    return call(
        kernel,
        (1,),
        [full((half, rows))] * PARTS + [full((rows, width)), ANYWHERE, ANYWHERE] + [ANYWHERE] * n,
        [full((width, rows)), ANYWHERE, ANYWHERE],
        [
            jax.ShapeDtypeStruct((width, rows), BF),
            jax.ShapeDtypeStruct(own.shape, BF),
            jax.ShapeDtypeStruct(far.shape, BF),
        ],
        [pltpu.VMEM((width, width), BF)] * 2 + [pltpu.SemaphoreType.DMA((count_of(pieces),))],
        20,
        5 * BACK,
        (places, *o_parts, grad_low, own, far, *pieces),
        prefetch=1,
        aliases={4: 1, 5: 2},
        after=after,
    )


def attend_back(qkv_t, do_t, lse, seg_row, seg_col, width, part, after=()):
    rows = qkv_t.shape[1]
    half = width // PARTS
    heads = half // HEAD_DIM
    scale = HEAD_DIM**-0.5

    def kernel(q_ref, k_ref, v_ref, do_ref, lse_ref, seg_r, seg_c, out, sums, keys, values, d_keys, d_values):
        step = pl.program_id(0)

        @pl.when(step == 0)
        def first():
            shift_in(keys, k_ref[...])
            shift_in(values, v_ref[...])
            d_keys[...] = jnp.zeros_like(d_keys)
            d_values[...] = jnp.zeros_like(d_values)

        start = pl.multiple_of(step * QB, QB)
        window = pl.ds(start, KB)
        bias = window_bias(seg_r[0:1, :], seg_c[window, :])
        ats = [slice(h * HEAD_DIM, (h + 1) * HEAD_DIM) for h in range(heads)]
        queries = [q_ref[at, :] * BF(scale) for at in ats]
        raw = [tn(keys[at, window], q) for at, q in zip(ats, queries)]
        grad_probs = [tn(values[at, window], do_ref[at, :]) for at in ats]
        probs = [jnp.exp(r + (bias - lse_ref[h : h + 1, :])) for h, r in enumerate(raw)]
        weighted = [p * g for p, g in zip(probs, grad_probs)]
        deltas = [jnp.sum(w, axis=0, keepdims=True) for w in weighted]
        scores = [(w - p * d).astype(BF) for w, p, d in zip(weighted, probs, deltas)]
        for at, s in zip(ats, scores):
            out[at, pl.ds(start, QB)] = (nn(keys[at, window], s) * scale).astype(BF)
        for at, q, s in zip(ats, queries, scores):
            d_keys[at, window] += nt(q, s)
        for at, p in zip(ats, probs):
            d_values[at, window] += nt(do_ref[at, :], p.astype(BF))

        @pl.when(step == pl.num_programs(0) - 1)
        def last():
            edge = KB // 4
            out[half : 2 * half, :] = d_keys[...][:, edge : edge + rows].astype(BF)
            out[2 * half : 3 * half, :] = d_values[...][:, edge : edge + rows].astype(BF)
            sums[...] = nt(jnp.ones((8, rows), BF), out[...])

    return call(
        kernel,
        (rows // QB,),
        head_parts(width, rows, part)
        + [
            pl.BlockSpec((half, QB), lambda i, *unused: (part, i)),
            lanes_of((16, QB)),
            lanes_of((8, QB)),
            full(seg_col.shape),
        ],
        [full((3 * half, rows)), full((8, 3 * half))],
        [jax.ShapeDtypeStruct((3 * half, rows), BF), jax.ShapeDtypeStruct((8, 3 * half), F32)],
        [pltpu.VMEM((half, rows + QB), BF)] * 2 + [pltpu.VMEM((half, rows + QB), F32)] * 2,
        28,
        12 * BACK,
        (qkv_t, qkv_t, qkv_t, do_t, lse, seg_row, seg_col),
        after=after,
    )


def qkv_back(grad_parts, hidden, places, rows_piece, topo, after=()):
    rows, width = hidden.shape
    half = width // PARTS
    count = 3 * width
    sites, lanes = topo.X * topo.X, width // topo.Y

    def kernel(at, grad_a, grad_b, hid, own, far, whole, sem):
        step = pl.program_id(0)
        for part, grad in enumerate((grad_a, grad_b)):
            here = pl.ds(pl.multiple_of(step * width + part * half, half), half)
            whole[here, :] = nn(grad[...], hid[...]).astype(BF)

        @pl.when(step == pl.num_programs(0) - 1)
        def last():
            wait_all(store_pieces(at, whole, rows_piece, (own, far), 0, sem))

    piece_shape = jax.ShapeDtypeStruct((sites, topo.Z, rows_piece, lanes), BF)
    return call(
        kernel,
        (3,),
        [rows_of((half, rows))] * PARTS + [full((rows, width))],
        [ANYWHERE, ANYWHERE],
        [piece_shape, piece_shape],
        [pltpu.VMEM((count, width), BF), pltpu.SemaphoreType.DMA((2 * sites * topo.Z,))],
        24,
        7 * BACK,
        (places, *grad_parts, hidden),
        prefetch=1,
        after=after,
    )


def first_norm_back(grad_parts, tokens, grad_mid, vecs, pieces, places, rows_piece, after=()):
    rows, width = tokens.shape
    count, half = 3 * width, width // PARTS
    block = 256
    n = len(pieces)

    def kernel(at, grad_a, grad_b, tok, mid, vec, *refs):
        parts, (out, sums, weight, sem) = refs[:n], refs[n:]

        @pl.when(pl.program_id(0) == 0)
        def first():
            wait_all(load_pieces(at, parts, 0, rows_piece, weight, sem))
            sums[...] = jnp.zeros_like(sums)

        both = jnp.concatenate([g[k * half : (k + 1) * half, :] for k in range(3) for g in (grad_a, grad_b)], axis=0)
        grad = tn(both, weight[...])
        hat, inverse = normed(tok[...].astype(F32))
        out[...] = (mid[...] + norm_back(grad, hat, inverse, vec[0:1, :])).astype(BF)
        sums[0:1, :] += jnp.sum(grad * hat, axis=0, keepdims=True)
        sums[1:2, :] += jnp.sum(grad, axis=0, keepdims=True)

    return call(
        kernel,
        (rows // block,),
        [lanes_of((count // PARTS, block))] * PARTS
        + [rows_of((block, width)), rows_of((block, width)), full(vecs.shape)]
        + [ANYWHERE] * n,
        [rows_of((block, width)), full((8, width))],
        [jax.ShapeDtypeStruct((rows, width), BF), jax.ShapeDtypeStruct((8, width), F32)],
        [pltpu.VMEM((count, width), BF), pltpu.SemaphoreType.DMA((count_of(pieces),))],
        28,
        11 * BACK,
        (places, *grad_parts, tokens, grad_mid, vecs, *pieces),
        prefetch=1,
        after=after,
    )


def finish_out(acts, mid, vecs, groups, places, unit_rows, wide, after=()):
    rows, width = mid.shape
    block = 256
    n, total_n, count = len(groups[0][0]), len(groups[0][0]) + len(groups[1][0]), count_of(groups[0][0])
    units = 2 * wide * unit_rows

    def kernel(at, act_a, act_b, mid_ref, vec, *refs):
        parts = refs[:total_n]
        out, down_a, down_b, sem = refs[total_n:]

        @pl.when(pl.program_id(0) == 0)
        def first():
            one = load_pieces(at, parts[:n], groups[0][1], unit_rows, down_a, sem.at[0])
            two = load_pieces(at, parts[n:], groups[1][1], unit_rows, down_b, sem.at[1])
            wait_all(one)
            wait_all(two)

        result = tn(act_a[...], down_a[...]) + tn(act_b[...], down_b[...])
        out[...] = (mid_ref[...] + result + vec[7:8, :]).astype(BF)

    return call(
        kernel,
        (rows // block,),
        [lanes_of((units, block)), lanes_of((units, block)), rows_of((block, width)), full(vecs.shape)]
        + [ANYWHERE] * total_n,
        rows_of((block, width)),
        jax.ShapeDtypeStruct((rows, width), BF),
        [pltpu.VMEM((units, width), BF)] * 2 + [pltpu.SemaphoreType.DMA((2, count))],
        32,
        11 * BACK,
        (places, *acts, mid, vecs, *groups[0][0], *groups[1][0]),
        prefetch=1,
        after=after,
    )


def pack_vectors(sums_one, sums_two, sums_qkv, sums_up, places, topo, share, after=()):
    width = sums_one.shape[1]
    half = width // PARTS
    hidden = PARTS * sums_up[0].shape[1]
    group = hidden // (2 * topo.wide)
    unit = group // 2
    sites, deep, lanes = topo.X * topo.X, topo.Z, width // topo.Y
    lines = 8 + hidden // width

    def kernel(at, one, two, qkv_a, qkv_b, up_a, up_b, own, far, flat, ups, slots):
        flat[0:2, :] = one[0:2, :]
        for part, ref in enumerate((qkv_a, qkv_b)):
            lane = slice(part * half, (part + 1) * half)
            flat[2:3, lane] = ref[0:1, 0:half]
            flat[3:4, lane] = ref[0:1, 2 * half : 3 * half]
        flat[4:5, :] = two[2:3, :]
        flat[5:7, :] = two[0:2, :]
        flat[7:8, :] = two[3:4, :]
        for k in range(2 * topo.wide):
            for part, ref in enumerate((up_a, up_b)):
                ups[0:1, k * group + part * unit : k * group + (part + 1) * unit] = ref[0:1, k * unit : (k + 1) * unit]
        for line in range(8, lines):
            flat[line : line + 1, :] = ups[0:1, (line - 8) * width : (line - 7) * width]
        slots[...] = jnp.zeros_like(slots)
        for j in range(topo.wide * topo.narrow):
            done = 0
            while done < share:
                line, lane = divmod(j * share + done, width)
                take = min(share - done, width - lane)
                slots[j, 0:1, done : done + take] = flat[line : line + 1, lane : lane + take]
                done += take
        for j in range(2 * sites * deep):
            i, k = divmod(j, deep)
            slot = at[j, 0] * topo.narrow + at[j, 1] * 2 + at[j, 2]
            target = own.at[i, k] if i < sites else far.at[i - sites, k]
            target[...] = jnp.broadcast_to(slots[slot, 0:1, :], (16, lanes)).astype(BF)

    shape = (sites, deep, 16, lanes)
    return call(
        kernel,
        (1,),
        [full(a.shape) for a in (sums_one, sums_two, *sums_qkv, *sums_up)],
        [full(shape)] * 2,
        [jax.ShapeDtypeStruct(shape, BF)] * 2,
        [
            pltpu.VMEM((16, width), F32),
            pltpu.VMEM((8, hidden), F32),
            pltpu.VMEM((topo.wide * topo.narrow, 8, lanes), F32),
        ],
        16,
        3 * BACK,
        (places, sums_one, sums_two, *sums_qkv, *sums_up),
        prefetch=1,
        after=after,
    )


def total(first, *rest):
    result = first.astype(F32)
    for other in rest:
        result = result + other.astype(F32)
    return result


def tied(values, others):
    return lax.optimization_barrier((values, tuple(others)))[0] if others else values


class Spread:
    def __init__(self, piece, topo):
        self.topo, self.piece = topo, piece
        self.coming = tuple(send(piece, topo.zp[k]) for k in range(1, topo.Z))

    def along(self, others=()):
        stack = tied(jnp.stack((self.piece, *self.coming)), others)
        self.first = stack
        self.coming = tuple(send(stack, self.topo.ap[k]) for k in range(1, self.topo.X))

    def across(self, others=()):
        self.line = tied(jnp.stack((self.first, *self.coming)), others)
        self.coming = tuple(send(self.line, self.topo.bp[k]) for k in range(1, self.topo.X))
        self.near = send(self.line, self.topo.cp)

    def core(self, others=()):
        coming = tied(self.coming, others)
        self.pieces = [self.line, *coming, self.near, *[send(p, self.topo.cp) for p in coming]]


class Chain:
    def __init__(self, own, far, topo):
        self.topo, self.held = topo, own
        self.coming = [send(far, topo.cp)]

    def arrived(self):
        return tuple(self.coming)

    def fold(self, part=None):
        terms = (self.held, *self.coming)
        return total(*(terms if part is None else [t[part] for t in terms]))

    def stage(self, count, perms, others):
        self.held, self.coming = tied((self.held, self.coming), others)
        self.held, *sent = [self.fold(k).astype(BF) for k in range(count)]
        self.sent = tuple(sent)
        self.coming = [send(values, perms[count - 1 - k]) for k, values in enumerate(sent)]

    def across(self, others=()):
        side = self.topo.X
        split = lambda values: values.reshape(side, side, *values.shape[1:])
        self.held, self.coming = split(self.held), [split(c) for c in self.coming]
        self.stage(side, self.topo.bp, others)

    def along(self, others=()):
        self.stage(self.topo.X, self.topo.ap, others)

    def down(self, others=()):
        self.stage(self.topo.Z, self.topo.zp, others)

    def result(self, others=()):
        self.held, self.coming = tied((self.held, self.coming), others)
        return self.fold()


def tail_rows(values, rows, lanes):
    return jnp.pad(values[None], ((0, rows - 1), (0, lanes - values.shape[0])))


def fits(topo, rows, width, hidden):
    lanes = 2 * width // topo.narrow
    return (
        lanes % 128 == 0
        and rows % 256 == 0
        and (width // topo.wide) % 32 == 0
        and (hidden // topo.wide) % 64 == 0
        and 2 * P_THREE == QB
    )


def fast_device(
    tokens, qkv_weight, out_weight, up_weight, down_weight, vectors, bucket_counts, cotangent, topo
):
    rows, width = tokens.shape
    wide = topo.wide
    places = topo.origins()
    core = topo.here()[3]
    shards = [qkv_weight.astype(BF).T, out_weight.astype(BF), up_weight.astype(BF).T, down_weight.astype(BF)]
    r_qkv, r_out, r_unit = shards[0].shape[0] // 2, shards[1].shape[0] // 2, shards[2].shape[0] // 4
    lanes = 2 * out_weight.shape[1]
    halves = [jnp.concatenate([pick_half(s, 0, h) for h in range(2) for s in pair], axis=0) for pair in (shards[:2], shards[2:])]
    first = pair_up(halves[0], topo, core)
    vec_low, out_low = r_qkv, r_qkv + 16
    one = Spread(
        jnp.concatenate([first[:r_qkv], tail_rows(vectors.astype(BF), 16, lanes), first[r_qkv:]], axis=0), topo
    )
    rest = pair_up(tied(halves[1], (first,)), topo, core)
    piece_two = jnp.concatenate([rest[:r_unit], rest[2 * r_unit : 3 * r_unit]], axis=0)
    piece_three = jnp.concatenate([rest[r_unit : 2 * r_unit], rest[3 * r_unit :]], axis=0)
    one.along((rest,))
    two = Spread(tied(piece_two, one.coming), topo)
    one.across()
    two.along(one.coming)
    one.core((two.first,))
    one = one.pieces
    sites = topo.X * topo.X
    shapes_a = [(sites, topo.Z, 2 * r_unit, lanes)] * 2
    shapes_b = [(sites, topo.Z, 2 * r_unit + r_out, lanes)] * 2
    vecs, bias_qkv, *bias_up = unpack_vectors(one, places, vec_low, vectors.shape[0], width, wide, topo.narrow)
    segment = image_ids(bucket_counts[0], rows)
    seg_row = jnp.broadcast_to(segment[None], (8, rows))
    seg_col = jnp.pad(segment, (QB // 2, QB // 2), constant_values=-1)[:, None]

    two_along = two.coming
    two.across()
    hidden_one, qkv_t = project_qkv(tokens, vecs, bias_qkv, one, places, (r_qkv, wide))
    three = Spread(tied(piece_three, (hidden_one,)), topo)
    attn_a, lse_a = attend(qkv_t, seg_row, seg_col, width, 0, after=two_along)
    two.core((lse_a,))
    attn_b, lse_b = attend(qkv_t, seg_row, seg_col, width, 1)
    attn_t, lse = (attn_a, attn_b), (lse_a, lse_b)
    three.along((lse_b,))
    two = two.pieces
    mid, hidden_two = project_out(attn_t, tokens, vecs, one, places, out_low, r_out, after=(three.first,))
    three.across((hidden_two,))
    three_along = (three.line,)
    act_a, grad_a, sum_a, own_a, far_a = mlp_half(
        hidden_two, cotangent, bias_up[0], two, places, 0, r_unit, shapes_a, wide, after=three_along
    )
    three.core((sum_a,))
    three = three.pieces
    chain_a = Chain(own_a, far_a, topo)
    act_b, grad_b, sum_b, own_b, far_b = mlp_half(
        hidden_two, cotangent, bias_up[1], three, places, 0, r_unit, shapes_b, wide
    )
    chain_a.across((sum_b,))
    grad_mid, grad_mid_low, sums_two = second_norm_back(
        (grad_a, grad_b), mid, cotangent, vecs, ((two, 0), (three, 0)), places, r_unit, wide,
        after=chain_a.sent,
    )
    do_t, own_b, far_b = out_back(attn_t, grad_mid_low, one, places, out_low, r_out, own_b, far_b, 2 * r_unit)
    chain_b = Chain(own_b, far_b, topo)
    chain_a.along((do_t,))
    grads_0, sums_0 = attend_back(qkv_t, do_t, lse[0], seg_row, seg_col, width, 0, after=chain_a.sent)
    chain_a.down((sums_0,))
    chain_b.across((sums_0,))
    grads_1, sums_1 = attend_back(
        qkv_t, do_t, lse[1], seg_row, seg_col, width, 1, after=chain_a.sent + chain_b.sent
    )
    grad_t = (grads_0, grads_1)
    chain_b.along((sums_1,))
    own_q, far_q = qkv_back(grad_t, hidden_one, places, r_qkv, topo, after=(*chain_a.arrived(), *chain_b.sent))
    chain_q = Chain(own_q, far_q, topo)
    chain_q.across()
    input_grad, sums_one = first_norm_back(
        grad_t, tokens, grad_mid, vecs, one, places, r_qkv, after=chain_q.sent + chain_b.sent
    )
    chain_q.along((sums_one,))
    chain_b.down((sums_one,))
    own_v, far_v = pack_vectors(
        sums_one, sums_two, (sums_0, sums_1), (sum_a, sum_b), places, topo, vectors.shape[0], after=chain_q.sent
    )
    chain_v = Chain(own_v, far_v, topo)
    chain_v.across()
    chain_q.down()
    block_out = finish_out(
        (act_a, act_b), mid, vecs, ((two, r_unit), (three, r_unit)), places, r_unit, wide,
        after=chain_q.sent + chain_v.sent,
    )
    chain_v.along((block_out,))
    chain_v.down()
    part_a, part_b, part_q = chain_a.result((sums_one,)), chain_b.result((block_out,)), chain_q.result((block_out,))
    vector_grad = chain_v.result()[0, : vectors.shape[0]]
    down = jnp.concatenate([part_a[r_unit:], part_b[r_unit : 2 * r_unit]], axis=0)
    up = jnp.concatenate([part_a[:r_unit], part_b[:r_unit]], axis=0)
    out = part_b[2 * r_unit :]
    grads = [unpair(g, topo, core) for g in (part_q, out, up, down)]
    return (block_out, input_grad, grads[0].T, grads[1], grads[2].T, grads[3], vector_grad)


def per_device(
    tokens, qkv_weight, out_weight, up_weight, down_weight, vectors, bucket_counts, cotangent
):
    topo = Topo(lax.axis_size("wide"), lax.axis_size("narrow"))
    operands = (tokens, qkv_weight, out_weight, up_weight, down_weight, vectors, bucket_counts, cotangent)
    if fits(topo, *tokens.shape, up_weight.shape[1] * topo.wide):
        return fast_device(*operands, topo)
    return plain_device(*operands)


def plain_device(
    tokens, qkv_weight, out_weight, up_weight, down_weight, vectors, bucket_counts, cotangent
):
    rows, width = tokens.shape
    halves = (
        lax.all_gather(qkv_weight.astype(jnp.bfloat16), "narrow", axis=0, tiled=True),
        lax.all_gather(out_weight.astype(jnp.bfloat16), "narrow", axis=1, tiled=True),
        lax.all_gather(up_weight.astype(jnp.bfloat16), "narrow", axis=0, tiled=True),
        lax.all_gather(down_weight.astype(jnp.bfloat16), "narrow", axis=1, tiled=True),
        lax.all_gather(vectors.astype(jnp.bfloat16), "narrow", axis=0, tiled=True),
    )
    wholes = (
        lax.all_gather(halves[0], "wide", axis=1, tiled=True),
        lax.all_gather(halves[1], "wide", axis=0, tiled=True),
        lax.all_gather(halves[2], "wide", axis=1, tiled=True),
        lax.all_gather(halves[3], "wide", axis=0, tiled=True),
        lax.all_gather(halves[4], "wide", axis=0, tiled=True),
    )
    qkv_full, out_full, up_full, down_full, packed = wholes
    params = packed.astype(jnp.float32)
    gain_one = params[0:width]
    shift_one = params[width : 2 * width]
    bias_query = params[2 * width : 3 * width]
    bias_value = params[3 * width : 4 * width]
    bias_out = params[4 * width : 5 * width]
    gain_two = params[5 * width : 6 * width]
    shift_two = params[6 * width : 7 * width]
    bias_down = params[7 * width : 8 * width]
    bias_up = params[8 * width :]
    inputs = tokens.astype(jnp.float32)
    hidden_one = layer_norm(inputs, gain_one, shift_one).astype(jnp.bfloat16)
    qkv_bias = jnp.concatenate([bias_query, jnp.zeros((width,), jnp.float32), bias_value])
    qkv_all = (jnp.dot(hidden_one, qkv_full, preferred_element_type=jnp.float32) + qkv_bias).astype(
        jnp.bfloat16
    )
    margin = P_THREE
    blocks = rows // QROWS
    span = QROWS + 2 * margin
    scale = HEAD_DIM ** (-0.5)
    query_blk = qkv_all[:, :width].reshape(blocks, QROWS, HEADS, HEAD_DIM)
    keys_win = windows_of(qkv_all[:, width : 2 * width], margin, blocks, 0).reshape(
        blocks, span, HEADS, HEAD_DIM
    )
    values_win = windows_of(qkv_all[:, 2 * width :], margin, blocks, 0).reshape(
        blocks, span, HEADS, HEAD_DIM
    )
    segment = image_ids(bucket_counts[0], rows)
    seg_rows = segment.reshape(blocks, QROWS)
    seg_cols = windows_of(segment, margin, blocks, -1)
    same = seg_rows[:, None, :, None] == seg_cols[:, None, None, :]
    raw = (
        jnp.einsum("bqhd,bkhd->bhqk", query_blk, keys_win, preferred_element_type=jnp.float32)
        * scale
    )
    masked = jnp.where(same, raw, NEG)
    top = jnp.max(masked, axis=3, keepdims=True)
    expo = jnp.exp(masked - top)
    total = jnp.sum(expo, axis=3, keepdims=True)
    probs_low = (expo / total).astype(jnp.bfloat16)
    log_total = top + jnp.log(total)
    attended = jnp.einsum(
        "bhqk,bkhd->bqhd", probs_low, values_win, preferred_element_type=jnp.float32
    )
    attn_low = attended.reshape(rows, width).astype(jnp.bfloat16)
    mid = inputs + jnp.dot(attn_low, out_full, preferred_element_type=jnp.float32) + bias_out
    hidden_two = layer_norm(mid, gain_two, shift_two).astype(jnp.bfloat16)
    pre_act = jnp.dot(hidden_two, up_full, preferred_element_type=jnp.float32) + bias_up
    activated = gelu_exact(pre_act).astype(jnp.bfloat16)
    output = mid + jnp.dot(activated, down_full, preferred_element_type=jnp.float32) + bias_down
    block_out = output.astype(jnp.bfloat16)
    grad_top = cotangent.astype(jnp.float32)
    d_down = contract_rows(activated, cotangent)
    d_bias_down = jnp.sum(grad_top, axis=0)
    grad_act = contract_cols(cotangent, down_full)
    unused_act, gelu_back = jax.vjp(gelu_exact, pre_act)
    grad_pre = gelu_back(grad_act)[0].astype(jnp.bfloat16)
    d_up = contract_rows(hidden_two, grad_pre)
    d_bias_up = jnp.sum(grad_pre.astype(jnp.float32), axis=0)
    grad_hidden_two = contract_cols(grad_pre, up_full)
    unused_two, norm_back_two = jax.vjp(layer_norm, mid, gain_two, shift_two)
    grad_mid_part, d_gain_two, d_shift_two = norm_back_two(grad_hidden_two)
    grad_mid = grad_top + grad_mid_part
    grad_mid_low = grad_mid.astype(jnp.bfloat16)
    d_out = contract_rows(attn_low, grad_mid_low)
    d_bias_out = jnp.sum(grad_mid_low.astype(jnp.float32), axis=0)
    grad_attn = contract_cols(grad_mid_low, out_full).astype(jnp.bfloat16)
    raw_again = (
        jnp.einsum("bqhd,bkhd->bhqk", query_blk, keys_win, preferred_element_type=jnp.float32)
        * scale
    )
    probs = jnp.exp(jnp.where(same, raw_again, NEG) - log_total)
    grad_blk = grad_attn.reshape(blocks, QROWS, HEADS, HEAD_DIM)
    grad_probs = jnp.einsum(
        "bqhd,bkhd->bhqk", grad_blk, values_win, preferred_element_type=jnp.float32
    )
    grad_scores = (
        probs * (grad_probs - jnp.sum(probs * grad_probs, axis=3, keepdims=True))
    ).astype(jnp.bfloat16)
    grad_query = (
        jnp.einsum("bhqk,bkhd->bqhd", grad_scores, keys_win, preferred_element_type=jnp.float32)
        * scale
    )
    grad_keys_win = (
        jnp.einsum("bhqk,bqhd->bkhd", grad_scores, query_blk, preferred_element_type=jnp.float32)
        * scale
    )
    grad_values_win = jnp.einsum(
        "bhqk,bqhd->bkhd", probs.astype(jnp.bfloat16), grad_blk, preferred_element_type=jnp.float32
    )
    grad_keys = fold_windows(grad_keys_win.reshape(blocks, span, width), margin, QROWS)
    grad_values = fold_windows(grad_values_win.reshape(blocks, span, width), margin, QROWS)
    grad_qkv = jnp.concatenate(
        [grad_query.reshape(rows, width), grad_keys, grad_values], axis=1
    ).astype(jnp.bfloat16)
    d_qkv = contract_rows(hidden_one, grad_qkv)
    column_sums = jnp.sum(grad_qkv.astype(jnp.float32), axis=0)
    grad_hidden_one = contract_cols(grad_qkv, qkv_full)
    unused_one, norm_back_one = jax.vjp(layer_norm, inputs, gain_one, shift_one)
    grad_in_part, d_gain_one, d_shift_one = norm_back_one(grad_hidden_one)
    input_grad = (grad_mid + grad_in_part).astype(jnp.bfloat16)
    d_vector = jnp.concatenate(
        [
            d_gain_one,
            d_shift_one,
            column_sums[:width],
            column_sums[2 * width :],
            d_bias_out,
            d_gain_two,
            d_shift_two,
            d_bias_down,
            d_bias_up,
        ]
    )
    partial_sums = (
        lax.psum_scatter(
            d_qkv.astype(jnp.bfloat16), "wide", scatter_dimension=1, tiled=True
        ).astype(jnp.float32),
        lax.psum_scatter(
            d_out.astype(jnp.bfloat16), "wide", scatter_dimension=0, tiled=True
        ).astype(jnp.float32),
        lax.psum_scatter(d_up.astype(jnp.bfloat16), "wide", scatter_dimension=1, tiled=True).astype(
            jnp.float32
        ),
        lax.psum_scatter(
            d_down.astype(jnp.bfloat16), "wide", scatter_dimension=0, tiled=True
        ).astype(jnp.float32),
        lax.psum_scatter(
            d_vector.astype(jnp.bfloat16), "wide", scatter_dimension=0, tiled=True
        ).astype(jnp.float32),
    )
    final = (
        lax.psum_scatter(
            partial_sums[0].astype(jnp.bfloat16), "narrow", scatter_dimension=0, tiled=True
        ).astype(jnp.float32),
        lax.psum_scatter(
            partial_sums[1].astype(jnp.bfloat16), "narrow", scatter_dimension=1, tiled=True
        ).astype(jnp.float32),
        lax.psum_scatter(
            partial_sums[2].astype(jnp.bfloat16), "narrow", scatter_dimension=0, tiled=True
        ).astype(jnp.float32),
        lax.psum_scatter(
            partial_sums[3].astype(jnp.bfloat16), "narrow", scatter_dimension=1, tiled=True
        ).astype(jnp.float32),
        lax.psum_scatter(
            partial_sums[4].astype(jnp.bfloat16), "narrow", scatter_dimension=0, tiled=True
        ).astype(jnp.float32),
    )
    return (block_out, input_grad, final[0], final[1], final[2], final[3], final[4])


def solution(mesh):
    return jax.shard_map(
        per_device,
        mesh=mesh,
        in_specs=(
            P(("wide", "narrow"), None),
            P("narrow", "wide"),
            P("wide", "narrow"),
            P("narrow", "wide"),
            P("wide", "narrow"),
            P(("wide", "narrow")),
            P(("wide", "narrow"), None),
            P(("wide", "narrow"), None),
        ),
        out_specs=(
            P(("wide", "narrow"), None),
            P(("wide", "narrow"), None),
            P("narrow", "wide"),
            P("wide", "narrow"),
            P("narrow", "wide"),
            P("wide", "narrow"),
            P(("wide", "narrow")),
        ),
        check_vma=False,
    )
```
